32 devices in a mesh: tm: 8 (over y, x, core), tile: 4 (over z).
Axes of the slice: x: 2, y: 2, z: 4, core: 2. Of those that a mesh axis runs over, the one named last changes fastest.
Arguments:
- velocity_u: float32 [384, 2, 16, 1024], P('tm', None, None, 'tile'), may hold values from -12 to 12
- velocity_v: float32 [384, 2, 16, 1024], P('tm', None, None, 'tile'), may hold values from -12 to 12
- land_sea: int32 [16, 1024], P(None, 'tile'), may hold values 0 or 1
- bottom_level: int32 [16, 1024], P(None, 'tile'), may hold values from 0 to 2
- spacing_x: float32 [16, 1024], P(None, 'tile'), may hold values from 0.5 to 2
- spacing_y: float32 [16, 1024], P(None, 'tile'), may hold values from 0.5 to 2
Outputs:
- conversion_maps: bfloat16 [384, 2, 16, 1024], P('tm', None, None, 'tile')
- mean_map: float32 [2, 16, 1024], P(None, None, 'tile')
The draws below stay inside these ranges and needn't reach their ends.
All inputs are finite; a program needn't handle non-finite values. No bound on the sum of `land_sea` on one device may be relied on, other than what follows from the above.
Results may differ from the reference program's by a relative error of at most 0.001.
Values sent between devices are 32-bit elements; how exact they have to be, the bound alone decides.
A program may use at most 64 MiB of HBM per device.

```python
import math
import jax
import jax.numpy as jnp
from jax import lax

HALF = 24
SNAPS = 48
LEVELS = 2
ROWS = 16
TOTAL = 384
NX = 1024


def noisy_series(key, series_tag):
    series_key = jax.random.fold_in(key, series_tag)
    full_shape = (TOTAL + 1, LEVELS, ROWS, NX)
    noise_field = jnp.clip(jax.random.normal(series_key, full_shape, jnp.float32), -4.0, 4.0)
    return 1.5 * (noise_field[1:] - noise_field[:-1])


def draw_velocity_u(key, part):
    return noisy_series(key, 101)


def draw_velocity_v(key, part):
    return noisy_series(key, 202)


def place_ends(array, stream_key, smallest, top_value):
    shape = array.shape
    place = [jax.random.randint(jax.random.fold_in(stream_key, axis), (), 0, shape[axis]) for axis in range(len(shape))]
    array = array.at[tuple(place)].set(smallest)
    longest = shape.index(max(shape))
    place[longest] = (place[longest] + 1) % shape[longest]
    return array.at[tuple(place)].set(top_value)


def level_of(stream_key, dims, shards, low, high):
    gain = 1.0
    for dim, shards_of in shards:
        draws = jax.random.uniform(jax.random.fold_in(jax.random.fold_in(stream_key, 6), dim), (shards_of,), jnp.float32, low / len(shards), high / len(shards))
        gain = gain * jnp.repeat(jnp.exp(draws), dims[dim] // shards_of).reshape((-1,) + (1,) * (len(dims) - 1 - dim))
    return gain


def setup_inputs(seed: int = 0) -> dict:
    keys = jax.random.split(jax.random.key(seed), 7)
    velocity_u = draw_velocity_u(jax.random.fold_in(keys[6], 71), 0)
    velocity_v = draw_velocity_v(jax.random.fold_in(keys[6], 71), 0)
    land_sea = place_ends((jax.random.randint(keys[2], (ROWS, NX), 0, 10) < 9).astype(jnp.int32), jax.random.fold_in(keys[2], 1), 0, 1)
    bottom_level = place_ends(jax.random.randint(keys[3], (ROWS, NX), 0, LEVELS + 1), jax.random.fold_in(keys[3], 1), 0, LEVELS).astype(jnp.int32)
    spacing_x = jnp.clip(jnp.exp(math.log(2.0) - 1.3862944 * jax.random.uniform(keys[4], (ROWS, NX), jnp.float32) ** level_of(keys[4], (ROWS, NX), ((1, 4),), -0.2, 0.2)), 0.5, 2.0)
    spacing_y = jnp.clip(jnp.exp(math.log(2.0) - 1.3862944 * jax.random.uniform(keys[5], (ROWS, NX), jnp.float32) ** level_of(keys[5], (ROWS, NX), ((1, 4),), -0.2, 0.2)), 0.5, 2.0)
    return dict(velocity_u=velocity_u, velocity_v=velocity_v, land_sea=land_sea, bottom_level=bottom_level, spacing_x=spacing_x, spacing_y=spacing_y)


cutoff_freq = 1.0 / 40.0


def band_matrix(count):
    out_rows = jnp.arange(count, dtype=jnp.int32)[:, None]
    in_cols = jnp.arange(count + 2 * HALF, dtype=jnp.int32)[None, :]
    offset = (in_cols - out_rows - HALF).astype(jnp.float32)
    weights = 2.0 * cutoff_freq * jnp.sinc(2.0 * cutoff_freq * offset) * jnp.sinc(offset / HALF)
    return jnp.where(jnp.abs(offset) <= HALF, weights, jnp.zeros_like(weights))


def lowpass(padded, validity, blocks, block):
    matrix = band_matrix(block)

    def one_block(block_id):
        start = (block_id * block).astype(jnp.int32)
        window = lax.dynamic_slice_in_dim(padded, start, block + 2 * HALF, 0)
        valid_part = lax.dynamic_slice_in_dim(validity, start, block + 2 * HALF, 0)
        weighted = jnp.dot(matrix, window, precision=lax.Precision.HIGHEST, preferred_element_type=jnp.float32)
        weight_sum = jnp.dot(matrix, valid_part, precision=lax.Precision.HIGHEST, preferred_element_type=jnp.float32)
        return weighted / weight_sum[:, None]

    result = lax.map(one_block, jnp.arange(blocks, dtype=jnp.int32))
    return result.reshape(blocks * block, padded.shape[1])


def wet_cells(land_sea, bottom_level, levels):
    level_ids = jnp.arange(levels, dtype=jnp.int32)[:, None, None]
    return ((land_sea[None] == 1) & (level_ids < bottom_level[None])).astype(jnp.float32)


def conversion_terms(extended, eddies, wet_mask, spacing_x, spacing_y):
    grad_x = (extended[..., 2:] - extended[..., :-2]) * (0.5 / spacing_x)
    centre = extended[..., 1:-1]
    row_padded = jnp.pad(centre, ((0, 0), (0, 0), (0, 0), (1, 1), (0, 0)))
    grad_y = (row_padded[..., 2:, :] - row_padded[..., :-2, :]) * (0.5 / spacing_y)
    eddy_u = eddies[:, 0]
    eddy_v = eddies[:, 1]
    total = eddy_u * eddy_u * grad_x[:, 0] + eddy_u * eddy_v * (grad_y[:, 0] + grad_x[:, 1]) + eddy_v * eddy_v * grad_y[:, 1]
    return -wet_mask[None] * total


def reference(velocity_u, velocity_v, land_sea, bottom_level, spacing_x, spacing_y):
    length = velocity_u.shape[0]
    stacked = jnp.stack([velocity_u, velocity_v], axis=1)
    flattened = stacked.reshape(length, -1)
    padded = jnp.pad(flattened, ((HALF, HALF), (0, 0)))
    validity = jnp.pad(jnp.ones((length,), jnp.float32), (HALF, HALF))
    mean_flow = lowpass(padded, validity, length // SNAPS, SNAPS).reshape(stacked.shape)
    eddies = stacked - mean_flow
    wet_mask = wet_cells(land_sea, bottom_level, stacked.shape[2])
    masked = mean_flow * wet_mask[None, None]
    extended = jnp.pad(masked, ((0, 0), (0, 0), (0, 0), (0, 0), (1, 1)))
    conversion = conversion_terms(extended, eddies, wet_mask, spacing_x, spacing_y)
    return conversion.astype(jnp.bfloat16), jnp.sum(conversion, axis=0) / length
```

```python
import functools

import jax
import jax.numpy as jnp
import numpy as np
from jax import lax
from jax.experimental import pallas as pl
from jax.experimental.pallas import tpu as pltpu
from jax.sharding import PartitionSpec as P

HALF = 24
CUTOFF = 1.0 / 40.0
LANES = 128
CHUNK = 8
DEPTH = 2
MESH = pl.DeviceIdType.MESH


def band_parts(count):
    offset = (np.arange(count + 2 * HALF)[None, :] - np.arange(count)[:, None] - HALF).astype(np.float64)
    weights = 2.0 * CUTOFF * np.sinc(2.0 * CUTOFF * offset) * np.sinc(offset / HALF)
    weights = np.where(np.abs(offset) <= HALF, weights, 0.0).astype(np.float32)
    own = weights[:, HALF : HALF + count]
    halo = np.concatenate([weights[:, :HALF], weights[:, HALF + count :]], axis=1)
    return own, halo


def dot(a, b):
    return jnp.dot(a, b, precision=lax.Precision.HIGHEST, preferred_element_type=jnp.float32)


def halves(a):
    high = a.astype(jnp.bfloat16).astype(jnp.float32)
    return high, a - high


def stacked_weights(w):
    high, low = halves(w)
    return jnp.concatenate(
        [jnp.concatenate([high, high], axis=1), jnp.concatenate([low, low], axis=1)], axis=0
    ).astype(jnp.bfloat16)


def split_dot(weights, pieces):
    split = [halves(p) for p in pieces]
    block = jnp.concatenate([s[0] for s in split] + [s[1] for s in split], axis=0).astype(jnp.bfloat16)
    both = jnp.dot(weights, block, preferred_element_type=jnp.float32)
    half = both.shape[0] // 2
    return both[:half] + both[half:]


def kernel(
    n_tm, n_tile, levels,
    u_ref, v_ref, land_in, bottom_in, sx_in, sy_in, own_in, halo_in,
    conv_ref, mean_ref,
    land_ref, bottom_ref, sx_ref, sy_ref, own_ref, halo_w_ref, small_sem,
    x, halo, mm, cf, wet, cx, cy, part, edge, edge_halo, edge_mean, edge_in,
    near_w, far_w, relayed, relay_send, relay_recv,
    x_sem, bulk_send, bulk_recv, edge_send, edge_recv, em_send, em_recv, part_send, part_recv,
):
    snaps, cells, width = u_ref.shape
    rows = cells // levels
    t = lax.axis_index("tm")
    z = lax.axis_index("tile")
    chunks = cells // CHUNK
    per_level = rows // CHUNK
    fields = (u_ref, v_ref)
    even = lax.rem(t, 2) == 0
    odd = jnp.logical_not(even)

    barrier = pltpu.get_barrier_semaphore()
    for k in range(1, n_tm):
        pl.semaphore_signal(barrier, inc=1, device_id={"tm": lax.rem(t + k, n_tm)}, device_id_type=MESH)

    @pl.when(z > 0)
    def _():
        pl.semaphore_signal(barrier, inc=1, device_id={"tile": z - 1}, device_id_type=MESH)

    @pl.when(z < n_tile - 1)
    def _():
        pl.semaphore_signal(barrier, inc=1, device_id={"tile": z + 1}, device_id_type=MESH)

    def local(c, f, h):
        return pltpu.make_async_copy(
            fields[f].at[:, pl.ds(c * CHUNK, CHUNK), pl.ds(h * LANES, LANES)], x.at[c, f, h], x_sem.at[c, f, h]
        )

    small = (
        (land_in, land_ref), (bottom_in, bottom_ref), (sx_in, sx_ref),
        (sy_in, sy_ref), (own_in, own_ref), (halo_in, halo_w_ref),
    )
    for i, (src, dst) in enumerate(small):
        pltpu.make_async_copy(src, dst, small_sem.at[i]).start()
    for c in range(chunks):
        for f in range(2):
            for h in range(2):
                local(c, f, h).start()

    def bulk(side, c, f, h):
        first = snaps - HALF if side == 0 else 0
        to = t + 1 if side == 0 else t - 1
        return pltpu.make_async_remote_copy(
            src_ref=fields[f].at[pl.ds(first, HALF), pl.ds(c * CHUNK, CHUNK), pl.ds(h * LANES, LANES)],
            dst_ref=halo.at[side, c, f, h],
            send_sem=bulk_send.at[side, c, f, h],
            recv_sem=bulk_recv.at[side, c, f, h],
            device_id={"tm": to},
            device_id_type=MESH,
        )

    middle = (n_tm // 2 - 1, n_tm // 2)
    via = (n_tm - 1, 0)

    def to_relay(side, c, h):
        first = snaps - HALF if side == 0 else 0
        return pltpu.make_async_remote_copy(
            src_ref=fields[1].at[pl.ds(first, HALF), pl.ds(c * CHUNK, CHUNK), pl.ds(h * LANES, LANES)],
            dst_ref=relayed.at[c, h],
            send_sem=bulk_send.at[side, c, 1, h],
            recv_sem=relay_recv.at[c, h],
            device_id={"tm": via[side]},
            device_id_type=MESH,
        )

    def from_relay(side, c, h):
        return pltpu.make_async_remote_copy(
            src_ref=relayed.at[c, h],
            dst_ref=halo.at[side, c, 1, h],
            send_sem=relay_send.at[c, h],
            recv_sem=bulk_recv.at[side, c, 1, h],
            device_id={"tm": middle[1 - side]},
            device_id_type=MESH,
        )

    def pass_on(c):
        if n_tm < 4:
            return
        for side in range(2):

            @pl.when(t == via[side])
            def _():
                for h in range(2):
                    to_relay(side, c, h).wait_recv()
                    from_relay(side, c, h).start()

    def edge_copy(side):
        first = snaps - HALF if side == 0 else 0
        to = t + 1 if side == 0 else t - 1
        return pltpu.make_async_remote_copy(
            src_ref=edge.at[pl.ds(first, HALF), :],
            dst_ref=edge_halo.at[side],
            send_sem=edge_send.at[side],
            recv_sem=edge_recv.at[side],
            device_id={"tm": to},
            device_id_type=MESH,
        )

    def mean_copy(side):
        to = z + 1 if side == 0 else z - 1
        return pltpu.make_async_remote_copy(
            src_ref=edge_mean,
            dst_ref=edge_in.at[side],
            send_sem=em_send.at[side],
            recv_sem=em_recv.at[side],
            device_id={"tile": to},
            device_id_type=MESH,
        )

    def converted(c):
        piece = c % per_level
        low = piece * CHUNK - (1 if piece else 0)
        high = rows if piece == per_level - 1 else (piece + 1) * CHUNK - 1
        return c // per_level, low, high

    def part_copy(c, k, slot):
        l, low, high = converted(c)
        return pltpu.make_async_remote_copy(
            src_ref=part.at[slot, pl.ds(l * rows + low, high - low)],
            dst_ref=part.at[slot, pl.ds(l * rows + low, high - low)],
            send_sem=part_send.at[c, k],
            recv_sem=part_recv.at[c, k],
            device_id={"tm": lax.rem(t + k, n_tm)},
            device_id_type=MESH,
        )

    sends = (t < n_tm - 1, t > 0)
    receives = (t > 0, t < n_tm - 1)
    send_near, send_far = (even, odd), (odd, even)
    near, far = (odd, even), (even, odd)
    z_sends = (z < n_tile - 1, z > 0)
    z_receives = (z > 0, z < n_tile - 1)

    def start_far(c):
        for side in range(2):
            if n_tm >= 4:

                @pl.when(t == middle[side])
                def _():
                    for h in range(2):
                        to_relay(side, c, h).start()
                        bulk(side, c, 0, h).start()

                whole = sends[side] & send_far[side] & (t != middle[side])
            else:
                whole = sends[side] & send_far[side]

            @pl.when(whole)
            def _():
                for f in range(2):
                    for h in range(2):
                        bulk(side, c, f, h).start()

    def finish_send(c, which):
        for side in range(2):

            @pl.when(sends[side] & which[side])
            def _():
                for f in range(2):
                    for h in range(2):
                        bulk(side, c, f, h).wait_send()

    pl.semaphore_wait(barrier, n_tm - 1 + (z > 0).astype(jnp.int32) + (z < n_tile - 1).astype(jnp.int32))

    for c in range(DEPTH):
        start_far(c)
    for side in range(2):

        @pl.when(sends[side] & send_near[side])
        def _():
            for c in range(chunks):
                for f in range(2):
                    for h in range(2):
                        bulk(side, c, f, h).start()

    for side in range(2):

        @pl.when(jnp.logical_not(receives[side]))
        def _():
            halo[side] = jnp.zeros(halo.shape[1:], jnp.float32)
            edge_halo[side] = jnp.zeros(edge_halo.shape[1:], jnp.float32)

        @pl.when(jnp.logical_not(z_receives[side]))
        def _():
            edge_in[side] = jnp.zeros(edge_in.shape[1:], jnp.float32)

    for i, (src, dst) in enumerate(small):
        pltpu.make_async_copy(src, dst, small_sem.at[i]).wait()

    for l in range(levels):
        is_wet = (land_ref[...] == 1) & (l < bottom_ref[...])
        level_wet = jnp.where(is_wet, 1.0, 0.0).astype(jnp.float32)
        for j in range(rows):
            wet[l * rows + j] = level_wet[j : j + 1, :]
    all_x, all_y = 0.5 / sx_ref[...], 0.5 / sy_ref[...]
    for j in range(rows):
        cx[j] = all_x[j : j + 1, :]
        cy[j] = all_y[j : j + 1, :]
    for f in range(2):
        for l in range(levels):
            for j in (0, rows + 1):
                mm[f, l, j] = jnp.zeros((snaps, width), jnp.float32)
    column = lax.broadcasted_iota(jnp.int32, (snaps, 2 * HALF), 1)
    valid = ((column >= HALF) | (t > 0)) & ((column < HALF) | (t < n_tm - 1))
    own_w = own_ref[...]
    halo_w = jnp.where(valid, halo_w_ref[...], 0.0)
    weight_sum = jnp.sum(own_w, axis=1, keepdims=True) + jnp.sum(halo_w, axis=1, keepdims=True)
    own_w = own_w / weight_sum
    halo_w = halo_w / weight_sum
    near_side = 1 - lax.rem(t, 2)
    far_side = lax.rem(t, 2)
    near_half = jnp.where(even, halo_w[:, HALF:], halo_w[:, :HALF])
    far_half = jnp.where(even, halo_w[:, :HALF], halo_w[:, HALF:])
    near_w[...] = stacked_weights(jnp.concatenate([own_w, near_half], axis=1))
    far_w[...] = stacked_weights(far_half)

    for c in range(chunks):
        for f in range(2):
            for h in range(2):
                local(c, f, h).wait()

    def series(ref, count, j):
        return ref.reshape(count * CHUNK, LANES)[pl.ds(j, count, stride=CHUNK), :]

    def both(ref, count, j):
        return jnp.concatenate([series(ref.at[h], count, j) for h in range(2)], axis=1)

    lane = lax.broadcasted_iota(jnp.int32, (snaps, LANES), 1)

    def pack(r, acc):
        c, j = r // CHUNK, lax.rem(r, CHUNK)
        for f in range(2):
            q = f * cells + r
            first = series(x.at[c, f, 0], snaps, j) * wet[r][:, :LANES]
            acc = jnp.where(lane == q, pltpu.roll(first, q, 1), acc)
            q = (2 + f) * cells + r
            last = series(x.at[c, f, 1], snaps, j) * wet[r][:, width - LANES :]
            acc = jnp.where(lane == q, pltpu.roll(last, lax.rem(q + 1, LANES), 1), acc)
        return acc

    edge[...] = lax.fori_loop(0, cells, pack, jnp.zeros((snaps, LANES), jnp.float32), unroll=4)
    for side in range(2):

        @pl.when(sends[side])
        def _():
            edge_copy(side).start()

    pass_on(0)

    for side in range(2):

        @pl.when(receives[side] & near[side])
        def _():
            for c in range(chunks):
                for f in range(2):
                    for h in range(2):
                        bulk(side, c, f, h).wait_recv()

    def near_part(r, carry):
        l, j = r // rows, lax.rem(r, rows)
        c, i = r // CHUNK, lax.rem(r, CHUNK)
        for f in range(2):
            pieces = [both(x.at[c, f], snaps, i), both(halo.at[near_side, c, f], HALF, i)]
            mm[f, l, j + 1] = split_dot(near_w[...], pieces)
        return carry

    lax.fori_loop(0, cells, near_part, 0, unroll=8)
    for c in range(1, DEPTH):
        pass_on(c)

    for side in range(2):

        @pl.when(receives[side])
        def _():
            edge_copy(side).wait_recv()

    edge_mean[...] = dot(own_w, edge[...]) + dot(
        halo_w, jnp.concatenate([edge_halo[0], edge_halo[1]], axis=0)
    )
    for side in range(2):

        @pl.when(z_sends[side])
        def _():
            mean_copy(side).start()

    wide = lax.broadcasted_iota(jnp.int32, (snaps, width), 1)

    def far_part(r, carry):
        l, j = r // rows, lax.rem(r, rows)
        c, i = r // CHUNK, lax.rem(r, CHUNK)
        mask = wet[r]
        for f in range(2):
            pieces = [both(halo.at[far_side, c, f], HALF, i)]
            mm[f, l, j + 1] = (mm[f, l, j + 1] + split_dot(far_w[...], pieces)) * mask
        return carry

    def grad_x(f, r, masked, scale):
        q = (2 + f) * cells + r
        before = pltpu.roll(edge_in[0], lax.rem(2 * LANES - q, LANES), 1)
        q = f * cells + r
        after = pltpu.roll(edge_in[1], lax.rem(2 * LANES - 1 - q, LANES), 1)
        before = jnp.concatenate([before, before], axis=1)
        after = jnp.concatenate([after, after], axis=1)
        behind = jnp.where(wide == 0, before, pltpu.roll(masked, 1, 1))
        ahead = jnp.where(wide == width - 1, after, pltpu.roll(masked, width - 1, 1))
        return (ahead - behind) * scale

    def convert(l):
        def body(j, carry):
            r = l * rows + j
            c, i = r // CHUNK, lax.rem(r, CHUNK)
            mask = wet[r]
            scale_x = cx[j]
            scale_y = cy[j]
            eddy, gx, gy = [], [], []
            for f in range(2):
                masked = mm[f, l, j + 1]
                eddy.append(both(x.at[c, f], snaps, i) - masked)
                gx.append(grad_x(f, r, masked, scale_x))
                gy.append((mm[f, l, j + 2] - mm[f, l, j]) * scale_y)
            eu, ev = eddy
            total = eu * eu * gx[0] + eu * ev * (gy[0] + gx[1]) + ev * ev * gy[1]
            conversion = -mask * total
            for h in range(2):
                cf.at[c, h].reshape(snaps * CHUNK, LANES)[pl.ds(i, snaps, stride=CHUNK), :] = conversion[
                    :, h * LANES : (h + 1) * LANES
                ]
            part[t, r] = jnp.sum(conversion, axis=0, keepdims=True)
            return carry

        return body

    for c in range(chunks):
        finish_send(c, send_far)
        if c + DEPTH < chunks:
            start_far(c + DEPTH)
        for side in range(2):

            @pl.when(receives[side] & far[side])
            def _():
                for f in range(2):
                    for h in range(2):
                        bulk(side, c, f, h).wait_recv()

        lax.fori_loop(c * CHUNK, (c + 1) * CHUNK, far_part, 0, unroll=8)
        if c + DEPTH < chunks:
            pass_on(c + DEPTH)
        if c == 0:
            for side in range(2):

                @pl.when(z_receives[side])
                def _():
                    mean_copy(side).wait_recv()

        l, low, high = converted(c)
        lax.fori_loop(low, high, convert(l), 0, unroll=2)
        for k in range(1, n_tm):
            part_copy(c, k, t).start()
        if c % per_level == per_level - 1:

            def narrow(s, carry):
                for h in range(2):
                    block = jnp.concatenate([cf[l * per_level + p, h, s] for p in range(per_level)], axis=0)
                    conv_ref[s, pl.ds(l * rows, rows), pl.ds(h * LANES, LANES)] = block.astype(jnp.bfloat16)
                return carry

            lax.fori_loop(0, snaps, narrow, 0, unroll=4)

    for c in range(chunks):
        for k in range(1, n_tm):
            part_copy(c, k, lax.rem(t + n_tm - k, n_tm)).wait_recv()
        l, low, high = converted(c)
        for j in range(low, high):
            total = part[0, l * rows + j]
            for s in range(1, n_tm):
                total = total + part[s, l * rows + j]
            mean_ref[l, j : j + 1, :] = total / (snaps * n_tm)

    for c in range(chunks):
        finish_send(c, send_near)
    for side in range(2):

        @pl.when(sends[side])
        def _():
            edge_copy(side).wait_send()

        @pl.when(z_sends[side])
        def _():
            mean_copy(side).wait_send()

        if n_tm >= 4:

            @pl.when(t == via[side])
            def _():
                for c in range(chunks):
                    for h in range(2):
                        from_relay(side, c, h).wait_send()

    for c in range(chunks):
        for k in range(1, n_tm):
            part_copy(c, k, t).wait_send()


def shards(velocity_u, velocity_v, land_sea, bottom_level, spacing_x, spacing_y):
    snaps, levels, rows, width = velocity_u.shape
    cells = levels * rows
    n_tm, n_tile = lax.axis_size("tm"), lax.axis_size("tile")
    assert width == 2 * LANES and 4 * cells == LANES and snaps >= HALF and rows % CHUNK == 0 and n_tm % 4 == 0
    own, halo = band_parts(snaps)
    chunks = cells // CHUNK
    vmem = pl.BlockSpec(memory_space=pltpu.VMEM)
    hbm = pl.BlockSpec(memory_space=pltpu.HBM)
    f32, bf16 = jnp.float32, jnp.bfloat16
    dma = pltpu.SemaphoreType.DMA
    conversion, mean_map = pl.pallas_call(
        functools.partial(kernel, n_tm, n_tile, levels),
        out_shape=(
            jax.ShapeDtypeStruct((snaps, cells, width), bf16),
            jax.ShapeDtypeStruct((levels, rows, width), f32),
        ),
        in_specs=[hbm] * 8,
        out_specs=(vmem, vmem),
        scratch_shapes=[
            pltpu.VMEM((rows, width), jnp.int32),
            pltpu.VMEM((rows, width), jnp.int32),
            pltpu.VMEM((rows, width), f32),
            pltpu.VMEM((rows, width), f32),
            pltpu.VMEM(own.shape, f32),
            pltpu.VMEM(halo.shape, f32),
            dma((6,)),
            pltpu.VMEM((chunks, 2, 2, snaps, CHUNK, LANES), f32),
            pltpu.VMEM((2, chunks, 2, 2, HALF, CHUNK, LANES), f32),
            pltpu.VMEM((2, levels, rows + 2, snaps, width), f32),
            pltpu.VMEM((chunks, 2, snaps, CHUNK, LANES), f32),
            pltpu.VMEM((cells, 1, width), f32),
            pltpu.VMEM((rows, 1, width), f32),
            pltpu.VMEM((rows, 1, width), f32),
            pltpu.VMEM((n_tm, cells, 1, width), f32),
            pltpu.VMEM((snaps, LANES), f32),
            pltpu.VMEM((2, HALF, LANES), f32),
            pltpu.VMEM((snaps, LANES), f32),
            pltpu.VMEM((2, snaps, LANES), f32),
            pltpu.VMEM((2 * snaps, 2 * (snaps + HALF)), bf16),
            pltpu.VMEM((2 * snaps, 2 * HALF), bf16),
            pltpu.VMEM((chunks, 2, HALF, CHUNK, LANES), f32),
            dma((chunks, 2)),
            dma((chunks, 2)),
            dma((chunks, 2, 2)),
            dma((2, chunks, 2, 2)),
            dma((2, chunks, 2, 2)),
            dma((2,)),
            dma((2,)),
            dma((2,)),
            dma((2,)),
            dma((chunks, n_tm)),
            dma((chunks, n_tm)),
        ],
        compiler_params=pltpu.CompilerParams(
            collective_id=0, has_side_effects=True, vmem_limit_bytes=60 * 1024 * 1024
        ),
        cost_estimate=pl.CostEstimate(flops=10**9, bytes_accessed=4 * 10**6, transcendentals=0),
    )(
        velocity_u.reshape(snaps, cells, width),
        velocity_v.reshape(snaps, cells, width),
        land_sea, bottom_level, spacing_x, spacing_y,
        jnp.asarray(own), jnp.asarray(halo),
    )
    return conversion.reshape(velocity_u.shape), mean_map


def solution(mesh):
    in_specs = (
        P("tm", None, None, "tile"),
        P("tm", None, None, "tile"),
        P(None, "tile"),
        P(None, "tile"),
        P(None, "tile"),
        P(None, "tile"),
    )
    out_specs = (P("tm", None, None, "tile"), P(None, None, "tile"))
    return jax.shard_map(shards, mesh=mesh, in_specs=in_specs, out_specs=out_specs, check_vma=False)
```

```python
import functools

import jax
import jax.numpy as jnp
import numpy as np
from jax import lax
from jax.experimental import pallas as pl
from jax.experimental.pallas import tpu as pltpu
from jax.sharding import PartitionSpec as P

HALF = 24
CUTOFF = 1.0 / 40.0
LANES = 128
CHUNK = 8
DEPTH = 2
MESH = pl.DeviceIdType.MESH


def band_parts(count):
    offset = (np.arange(count + 2 * HALF)[None, :] - np.arange(count)[:, None] - HALF).astype(np.float64)
    weights = 2.0 * CUTOFF * np.sinc(2.0 * CUTOFF * offset) * np.sinc(offset / HALF)
    weights = np.where(np.abs(offset) <= HALF, weights, 0.0).astype(np.float32)
    own = weights[:, HALF : HALF + count]
    halo = np.concatenate([weights[:, :HALF], weights[:, HALF + count :]], axis=1)
    return own, halo


def dot(a, b):
    return jnp.dot(a, b, precision=lax.Precision.HIGHEST, preferred_element_type=jnp.float32)


def halves(a):
    high = a.astype(jnp.bfloat16).astype(jnp.float32)
    return high, a - high


def stacked_weights(w):
    high, low = halves(w)
    return jnp.concatenate(
        [jnp.concatenate([high, high], axis=1), jnp.concatenate([low, low], axis=1)], axis=0
    ).astype(jnp.bfloat16)


def split_dot(weights, pieces):
    split = [halves(p) for p in pieces]
    block = jnp.concatenate([s[0] for s in split] + [s[1] for s in split], axis=0).astype(jnp.bfloat16)
    both = jnp.dot(weights, block, preferred_element_type=jnp.float32)
    half = both.shape[0] // 2
    return both[:half] + both[half:]


def kernel(
    n_tm, n_tile, levels,
    u_ref, v_ref, land_in, bottom_in, sx_in, sy_in, own_in, halo_in,
    conv_ref, mean_ref,
    land_ref, bottom_ref, sx_ref, sy_ref, own_ref, halo_w_ref, small_sem,
    x, halo, mm, cf, wet, cx, cy, part, edge, edge_halo, edge_mean, edge_in,
    near_w, far_w, relayed, relay_send, relay_recv,
    x_sem, bulk_send, bulk_recv, edge_send, edge_recv, em_send, em_recv, part_send, part_recv,
):
    snaps, cells, width = u_ref.shape
    rows = cells // levels
    t = lax.axis_index("tm")
    z = lax.axis_index("tile")
    chunks = cells // CHUNK
    per_level = rows // CHUNK
    fields = (u_ref, v_ref)
    even = lax.rem(t, 2) == 0
    odd = jnp.logical_not(even)

    barrier = pltpu.get_barrier_semaphore()
    for k in range(1, n_tm):
        pl.semaphore_signal(barrier, inc=1, device_id={"tm": lax.rem(t + k, n_tm)}, device_id_type=MESH)

    @pl.when(z > 0)
    def _():
        pl.semaphore_signal(barrier, inc=1, device_id={"tile": z - 1}, device_id_type=MESH)

    @pl.when(z < n_tile - 1)
    def _():
        pl.semaphore_signal(barrier, inc=1, device_id={"tile": z + 1}, device_id_type=MESH)

    def local(c, f, h):
        return pltpu.make_async_copy(
            fields[f].at[:, pl.ds(c * CHUNK, CHUNK), pl.ds(h * LANES, LANES)], x.at[c, f, h], x_sem.at[c, f, h]
        )

    small = (
        (land_in, land_ref), (bottom_in, bottom_ref), (sx_in, sx_ref),
        (sy_in, sy_ref), (own_in, own_ref), (halo_in, halo_w_ref),
    )
    for i, (src, dst) in enumerate(small):
        pltpu.make_async_copy(src, dst, small_sem.at[i]).start()
    for c in range(chunks):
        for f in range(2):
            for h in range(2):
                local(c, f, h).start()

    def bulk(side, c, f, h):
        first = snaps - HALF if side == 0 else 0
        to = t + 1 if side == 0 else t - 1
        return pltpu.make_async_remote_copy(
            src_ref=fields[f].at[pl.ds(first, HALF), pl.ds(c * CHUNK, CHUNK), pl.ds(h * LANES, LANES)],
            dst_ref=halo.at[side, c, f, h],
            send_sem=bulk_send.at[side, c, f, h],
            recv_sem=bulk_recv.at[side, c, f, h],
            device_id={"tm": to},
            device_id_type=MESH,
        )

    middle = (n_tm // 2 - 1, n_tm // 2)
    via = (n_tm - 1, 0)

    def to_relay(side, c, h):
        first = snaps - HALF if side == 0 else 0
        return pltpu.make_async_remote_copy(
            src_ref=fields[1].at[pl.ds(first, HALF), pl.ds(c * CHUNK, CHUNK), pl.ds(h * LANES, LANES)],
            dst_ref=relayed.at[c, h],
            send_sem=bulk_send.at[side, c, 1, h],
            recv_sem=relay_recv.at[c, h],
            device_id={"tm": via[side]},
            device_id_type=MESH,
        )

    def from_relay(side, c, h):
        return pltpu.make_async_remote_copy(
            src_ref=relayed.at[c, h],
            dst_ref=halo.at[side, c, 1, h],
            send_sem=relay_send.at[c, h],
            recv_sem=bulk_recv.at[side, c, 1, h],
            device_id={"tm": middle[1 - side]},
            device_id_type=MESH,
        )

    def pass_on(c):
        if n_tm < 4:
            return
        for side in range(2):

            @pl.when(t == via[side])
            def _():
                for h in range(2):
                    to_relay(side, c, h).wait_recv()
                    from_relay(side, c, h).start()

    def edge_copy(side):
        first = snaps - HALF if side == 0 else 0
        to = t + 1 if side == 0 else t - 1
        return pltpu.make_async_remote_copy(
            src_ref=edge.at[pl.ds(first, HALF), :],
            dst_ref=edge_halo.at[side],
            send_sem=edge_send.at[side],
            recv_sem=edge_recv.at[side],
            device_id={"tm": to},
            device_id_type=MESH,
        )

    def mean_copy(side):
        to = z + 1 if side == 0 else z - 1
        return pltpu.make_async_remote_copy(
            src_ref=edge_mean,
            dst_ref=edge_in.at[side],
            send_sem=em_send.at[side],
            recv_sem=em_recv.at[side],
            device_id={"tile": to},
            device_id_type=MESH,
        )

    def converted(c):
        piece = c % per_level
        low = piece * CHUNK - (1 if piece else 0)
        high = rows if piece == per_level - 1 else (piece + 1) * CHUNK - 1
        return c // per_level, low, high

    def part_copy(c, k, slot):
        l, low, high = converted(c)
        return pltpu.make_async_remote_copy(
            src_ref=part.at[slot, pl.ds(l * rows + low, high - low)],
            dst_ref=part.at[slot, pl.ds(l * rows + low, high - low)],
            send_sem=part_send.at[c, k],
            recv_sem=part_recv.at[c, k],
            device_id={"tm": lax.rem(t + k, n_tm)},
            device_id_type=MESH,
        )

    sends = (t < n_tm - 1, t > 0)
    receives = (t > 0, t < n_tm - 1)
    send_near, send_far = (even, odd), (odd, even)
    near, far = (odd, even), (even, odd)
    z_sends = (z < n_tile - 1, z > 0)
    z_receives = (z > 0, z < n_tile - 1)

    def start_far(c):
        for side in range(2):
            if n_tm >= 4:

                @pl.when(t == middle[side])
                def _():
                    for h in range(2):
                        to_relay(side, c, h).start()
                        bulk(side, c, 0, h).start()

                whole = sends[side] & send_far[side] & (t != middle[side])
            else:
                whole = sends[side] & send_far[side]

            @pl.when(whole)
            def _():
                for f in range(2):
                    for h in range(2):
                        bulk(side, c, f, h).start()

    def finish_send(c, which):
        for side in range(2):

            @pl.when(sends[side] & which[side])
            def _():
                for f in range(2):
                    for h in range(2):
                        bulk(side, c, f, h).wait_send()

    pl.semaphore_wait(barrier, n_tm - 1 + (z > 0).astype(jnp.int32) + (z < n_tile - 1).astype(jnp.int32))

    for c in range(DEPTH):
        start_far(c)
    for side in range(2):

        @pl.when(sends[side] & send_near[side])
        def _():
            for c in range(chunks):
                for f in range(2):
                    for h in range(2):
                        bulk(side, c, f, h).start()

    for side in range(2):

        @pl.when(jnp.logical_not(receives[side]))
        def _():
            halo[side] = jnp.zeros(halo.shape[1:], jnp.float32)
            edge_halo[side] = jnp.zeros(edge_halo.shape[1:], jnp.float32)

        @pl.when(jnp.logical_not(z_receives[side]))
        def _():
            edge_in[side] = jnp.zeros(edge_in.shape[1:], jnp.float32)

    for i, (src, dst) in enumerate(small):
        pltpu.make_async_copy(src, dst, small_sem.at[i]).wait()

    for l in range(levels):
        is_wet = (land_ref[...] == 1) & (l < bottom_ref[...])
        level_wet = jnp.where(is_wet, 1.0, 0.0).astype(jnp.float32)
        for j in range(rows):
            wet[l * rows + j] = level_wet[j : j + 1, :]
    all_x, all_y = 0.5 / sx_ref[...], 0.5 / sy_ref[...]
    for j in range(rows):
        cx[j] = all_x[j : j + 1, :]
        cy[j] = all_y[j : j + 1, :]
    for f in range(2):
        for l in range(levels):
            for j in (0, rows + 1):
                mm[f, l, j] = jnp.zeros((snaps, width), jnp.float32)
    column = lax.broadcasted_iota(jnp.int32, (snaps, 2 * HALF), 1)
    valid = ((column >= HALF) | (t > 0)) & ((column < HALF) | (t < n_tm - 1))
    own_w = own_ref[...]
    halo_w = jnp.where(valid, halo_w_ref[...], 0.0)
    weight_sum = jnp.sum(own_w, axis=1, keepdims=True) + jnp.sum(halo_w, axis=1, keepdims=True)
    own_w = own_w / weight_sum
    halo_w = halo_w / weight_sum
    near_side = 1 - lax.rem(t, 2)
    far_side = lax.rem(t, 2)
    near_half = jnp.where(even, halo_w[:, HALF:], halo_w[:, :HALF])
    far_half = jnp.where(even, halo_w[:, :HALF], halo_w[:, HALF:])
    near_w[...] = stacked_weights(jnp.concatenate([own_w, near_half], axis=1))
    far_w[...] = stacked_weights(far_half)

    for c in range(chunks):
        for f in range(2):
            for h in range(2):
                local(c, f, h).wait()

    def series(ref, count, j):
        return ref.reshape(count * CHUNK, LANES)[pl.ds(j, count, stride=CHUNK), :]

    def both(ref, count, j):
        return jnp.concatenate([series(ref.at[h], count, j) for h in range(2)], axis=1)

    lane = lax.broadcasted_iota(jnp.int32, (snaps, LANES), 1)

    def pack(r, acc):
        c, j = r // CHUNK, lax.rem(r, CHUNK)
        for f in range(2):
            q = f * cells + r
            first = series(x.at[c, f, 0], snaps, j) * wet[r][:, :LANES]
            acc = jnp.where(lane == q, pltpu.roll(first, q, 1), acc)
            q = (2 + f) * cells + r
            last = series(x.at[c, f, 1], snaps, j) * wet[r][:, width - LANES :]
            acc = jnp.where(lane == q, pltpu.roll(last, lax.rem(q + 1, LANES), 1), acc)
        return acc

    edge[...] = lax.fori_loop(0, cells, pack, jnp.zeros((snaps, LANES), jnp.float32), unroll=4)
    for side in range(2):

        @pl.when(sends[side])
        def _():
            edge_copy(side).start()

    pass_on(0)

    for side in range(2):

        @pl.when(receives[side] & near[side])
        def _():
            for c in range(chunks):
                for f in range(2):
                    for h in range(2):
                        bulk(side, c, f, h).wait_recv()

    def near_part(r, carry):
        l, j = r // rows, lax.rem(r, rows)
        c, i = r // CHUNK, lax.rem(r, CHUNK)
        for f in range(2):
            pieces = [both(x.at[c, f], snaps, i), both(halo.at[near_side, c, f], HALF, i)]
            mm[f, l, j + 1] = split_dot(near_w[...], pieces)
        return carry

    lax.fori_loop(0, cells, near_part, 0, unroll=8)
    for c in range(1, DEPTH):
        pass_on(c)

    for side in range(2):

        @pl.when(receives[side])
        def _():
            edge_copy(side).wait_recv()

    edge_mean[...] = dot(own_w, edge[...]) + dot(
        halo_w, jnp.concatenate([edge_halo[0], edge_halo[1]], axis=0)
    )
    for side in range(2):

        @pl.when(z_sends[side])
        def _():
            mean_copy(side).start()

    wide = lax.broadcasted_iota(jnp.int32, (snaps, width), 1)

    def far_part(r, carry):
        l, j = r // rows, lax.rem(r, rows)
        c, i = r // CHUNK, lax.rem(r, CHUNK)
        mask = wet[r]
        for f in range(2):
            pieces = [both(halo.at[far_side, c, f], HALF, i)]
            mm[f, l, j + 1] = (mm[f, l, j + 1] + split_dot(far_w[...], pieces)) * mask
        return carry

    def grad_x(f, r, masked, scale):
        q = (2 + f) * cells + r
        before = pltpu.roll(edge_in[0], lax.rem(2 * LANES - q, LANES), 1)
        q = f * cells + r
        after = pltpu.roll(edge_in[1], lax.rem(2 * LANES - 1 - q, LANES), 1)
        before = jnp.concatenate([before, before], axis=1)
        after = jnp.concatenate([after, after], axis=1)
        behind = jnp.where(wide == 0, before, pltpu.roll(masked, 1, 1))
        ahead = jnp.where(wide == width - 1, after, pltpu.roll(masked, width - 1, 1))
        return (ahead - behind) * scale

    def convert(l):
        def body(j, carry):
            r = l * rows + j
            c, i = r // CHUNK, lax.rem(r, CHUNK)
            mask = wet[r]
            scale_x = cx[j]
            scale_y = cy[j]
            eddy, gx, gy = [], [], []
            for f in range(2):
                masked = mm[f, l, j + 1]
                eddy.append(both(x.at[c, f], snaps, i) - masked)
                gx.append(grad_x(f, r, masked, scale_x))
                gy.append((mm[f, l, j + 2] - mm[f, l, j]) * scale_y)
            eu, ev = eddy
            total = eu * eu * gx[0] + eu * ev * (gy[0] + gx[1]) + ev * ev * gy[1]
            conversion = -mask * total
            for h in range(2):
                cf.at[c, h].reshape(snaps * CHUNK, LANES)[pl.ds(i, snaps, stride=CHUNK), :] = conversion[
                    :, h * LANES : (h + 1) * LANES
                ]
            part[t, r] = jnp.sum(conversion, axis=0, keepdims=True)
            return carry

        return body

    for c in range(chunks):
        finish_send(c, send_far)
        if c + DEPTH < chunks:
            start_far(c + DEPTH)
        for side in range(2):

            @pl.when(receives[side] & far[side])
            def _():
                for f in range(2):
                    for h in range(2):
                        bulk(side, c, f, h).wait_recv()

        lax.fori_loop(c * CHUNK, (c + 1) * CHUNK, far_part, 0, unroll=8)
        if c + DEPTH < chunks:
            pass_on(c + DEPTH)
        if c == 0:
            for side in range(2):

                @pl.when(z_receives[side])
                def _():
                    mean_copy(side).wait_recv()

        l, low, high = converted(c)
        lax.fori_loop(low, high, convert(l), 0, unroll=2)
        for k in range(1, n_tm):
            part_copy(c, k, t).start()
        if c % per_level == per_level - 1:

            def narrow(s, carry):
                for h in range(2):
                    block = jnp.concatenate([cf[l * per_level + p, h, s] for p in range(per_level)], axis=0)
                    conv_ref[s, pl.ds(l * rows, rows), pl.ds(h * LANES, LANES)] = block.astype(jnp.bfloat16)
                return carry

            lax.fori_loop(0, snaps, narrow, 0, unroll=4)

    for c in range(chunks):
        for k in range(1, n_tm):
            part_copy(c, k, lax.rem(t + n_tm - k, n_tm)).wait_recv()
        l, low, high = converted(c)
        for j in range(low, high):
            total = part[0, l * rows + j]
            for s in range(1, n_tm):
                total = total + part[s, l * rows + j]
            mean_ref[l, j : j + 1, :] = total / (snaps * n_tm)

    for c in range(chunks):
        finish_send(c, send_near)
    for side in range(2):

        @pl.when(sends[side])
        def _():
            edge_copy(side).wait_send()

        @pl.when(z_sends[side])
        def _():
            mean_copy(side).wait_send()

        if n_tm >= 4:

            @pl.when(t == via[side])
            def _():
                for c in range(chunks):
                    for h in range(2):
                        from_relay(side, c, h).wait_send()

    for c in range(chunks):
        for k in range(1, n_tm):
            part_copy(c, k, t).wait_send()


def fast_kernel(
    n_tm, n_tile, levels,
    u_ref, v_ref, land_in, bottom_in, sx_in, sy_in, own_in, halo_in,
    conv_ref, mean_ref, flag_ref,
    land_ref, bottom_ref, sx_ref, sy_ref, own_ref, halo_w_ref, small_sem,
    x, near, mm, cf, wet, key, cx, cy, part, edge, edge_halo, edge_mean, edge_in,
    near_w, far_w, place, packed, far, relayed, flags,
    relay_send, relay_recv, x_sem, near_sem, far_send, far_recv, edge_send, edge_recv, em_send, em_recv,
    part_send, part_recv, flag_send, flag_recv,
):
    snaps, cells, width = u_ref.shape
    rows = cells // levels
    t = lax.axis_index("tm")
    z = lax.axis_index("tile")
    chunks = cells // CHUNK
    per_level = rows // CHUNK
    fields = (u_ref, v_ref)
    even = lax.rem(t, 2) == 0
    odd = jnp.logical_not(even)

    barrier = pltpu.get_barrier_semaphore()
    for k in range(1, n_tm):
        pl.semaphore_signal(barrier, inc=1, device_id={"tm": lax.rem(t + k, n_tm)}, device_id_type=MESH)
    for k in range(1, n_tile):
        pl.semaphore_signal(barrier, inc=1, device_id={"tile": lax.rem(z + k, n_tile)}, device_id_type=MESH)

    def local(c, f, h):
        return pltpu.make_async_copy(
            fields[f].at[:, pl.ds(c * CHUNK, CHUNK), pl.ds(h * LANES, LANES)], x.at[c, f, h], x_sem.at[c, f, h]
        )

    small = (
        (land_in, land_ref), (bottom_in, bottom_ref), (sx_in, sx_ref),
        (sy_in, sy_ref), (own_in, own_ref), (halo_in, halo_w_ref),
    )
    for i, (src, dst) in enumerate(small):
        pltpu.make_async_copy(src, dst, small_sem.at[i]).start()
    for c in range(chunks):
        for f in range(2):
            for h in range(2):
                local(c, f, h).start()

    first_far = jnp.where(even, 0, snaps - HALF)
    first_near = jnp.where(even, snaps - HALF, 0)
    has_far = (t > 0) & (t < n_tm - 1)
    at_end = jnp.logical_not(has_far)
    is_middle = (t == n_tm // 2 - 1) | (t == n_tm // 2)
    far_to = jnp.where(even, t - 1, t + 1)
    via_to = jnp.where(t < n_tm // 2, n_tm - 1, 0)
    forward_to = jnp.where(t == 0, n_tm // 2 - 1, n_tm // 2)

    def tiles(c):
        wide = CHUNK * 3 // 2
        l = c // per_level
        start = c * wide if l == 0 else per_level * wide + (c - per_level) * CHUNK
        return start, wide if l == 0 else CHUNK

    def near_copy():
        return pltpu.make_async_remote_copy(
            src_ref=x.at[:, :, :, pl.ds(first_near, HALF)],
            dst_ref=near,
            send_sem=near_sem.at[0],
            recv_sem=near_sem.at[1],
            device_id={"tm": t + 1 - 2 * lax.rem(t, 2)},
            device_id_type=MESH,
        )

    def far_copy(c, f):
        start, count = tiles(c)
        return pltpu.make_async_remote_copy(
            src_ref=packed.at[f, pl.ds(start, count)],
            dst_ref=far.at[f, pl.ds(start, count)],
            send_sem=far_send.at[c, f],
            recv_sem=far_recv.at[c, f],
            device_id={"tm": far_to},
            device_id_type=MESH,
        )

    def to_relay(c):
        start, count = tiles(c)
        return pltpu.make_async_remote_copy(
            src_ref=packed.at[1, pl.ds(start, count)],
            dst_ref=relayed.at[pl.ds(start, count)],
            send_sem=far_send.at[c, 1],
            recv_sem=relay_recv.at[c],
            device_id={"tm": via_to},
            device_id_type=MESH,
        )

    def from_relay(c):
        start, count = tiles(c)
        return pltpu.make_async_remote_copy(
            src_ref=relayed.at[pl.ds(start, count)],
            dst_ref=far.at[1, pl.ds(start, count)],
            send_sem=relay_send.at[c],
            recv_sem=far_recv.at[c, 1],
            device_id={"tm": forward_to},
            device_id_type=MESH,
        )

    def pass_on(c):
        @pl.when(at_end)
        def _():
            to_relay(c).wait_recv()
            from_relay(c).start()

    def start_far(c):
        @pl.when(has_far)
        def _():
            far_copy(c, 0).start()

        @pl.when(is_middle)
        def _():
            to_relay(c).start()

        @pl.when(has_far & jnp.logical_not(is_middle))
        def _():
            far_copy(c, 1).start()

    def edge_copy(side):
        first = snaps - HALF if side == 0 else 0
        to = t + 1 if side == 0 else t - 1
        return pltpu.make_async_remote_copy(
            src_ref=edge.at[pl.ds(first, HALF), :],
            dst_ref=edge_halo.at[side],
            send_sem=edge_send.at[side],
            recv_sem=edge_recv.at[side],
            device_id={"tm": to},
            device_id_type=MESH,
        )

    def mean_copy(side):
        to = z + 1 if side == 0 else z - 1
        return pltpu.make_async_remote_copy(
            src_ref=edge_mean,
            dst_ref=edge_in.at[side],
            send_sem=em_send.at[side],
            recv_sem=em_recv.at[side],
            device_id={"tile": to},
            device_id_type=MESH,
        )

    def flag_copy(k, slot):
        return pltpu.make_async_remote_copy(
            src_ref=flags.at[slot],
            dst_ref=flags.at[slot],
            send_sem=flag_send.at[k],
            recv_sem=flag_recv.at[k],
            device_id={"tile": lax.rem(z + k, n_tile)},
            device_id_type=MESH,
        )

    def converted(c):
        piece = c % per_level
        low = piece * CHUNK - (1 if piece else 0)
        high = rows if piece == per_level - 1 else (piece + 1) * CHUNK - 1
        return c // per_level, low, high

    def part_copy(c, k, slot):
        l, low, high = converted(c)
        return pltpu.make_async_remote_copy(
            src_ref=part.at[slot, pl.ds(l * rows + low, high - low)],
            dst_ref=part.at[slot, pl.ds(l * rows + low, high - low)],
            send_sem=part_send.at[c, k],
            recv_sem=part_recv.at[c, k],
            device_id={"tm": lax.rem(t + k, n_tm)},
            device_id_type=MESH,
        )

    sends = (t < n_tm - 1, t > 0)
    receives = (t > 0, t < n_tm - 1)
    z_sends = (z < n_tile - 1, z > 0)
    z_receives = (z > 0, z < n_tile - 1)

    for i, (src, dst) in enumerate(small):
        pltpu.make_async_copy(src, dst, small_sem.at[i]).wait()

    levels_wet = []
    for l in range(levels):
        is_wet = (land_ref[...] == 1) & (l < bottom_ref[...])
        levels_wet.append(jnp.where(is_wet, 1.0, 0.0).astype(jnp.float32))
    all_wet = jnp.concatenate(levels_wet, axis=0)
    lower = lax.broadcasted_iota(jnp.int32, (width, width), 0)
    upper = lax.broadcasted_iota(jnp.int32, (width, width), 1)
    before = jnp.where(lower < upper, 1.0, 0.0).astype(jnp.bfloat16)
    order = jnp.dot(all_wet.astype(jnp.bfloat16), before, preferred_element_type=jnp.float32)
    row = lax.broadcasted_iota(jnp.int32, (cells, width), 0)
    room = jnp.where(row < rows, float(width * 3 // 4), float(width // 2))
    shift = jnp.where((row < rows) & (lax.rem(row, 2) == 1), float(width // 4), 0.0)
    all_key = jnp.where((all_wet > 0.0) & (order < room), order + shift, -1.0)
    over = jnp.max(order + all_wet - room, axis=0, keepdims=True)
    flags[z] = jnp.broadcast_to(jnp.maximum(over[:, :LANES], over[:, LANES:]), (8, LANES))
    for r in range(cells):
        wet[r] = all_wet[r : r + 1, :]
        key[r] = all_key[r : r + 1, :]

    def series(ref, count, j):
        return ref.reshape(count * CHUNK, LANES)[pl.ds(j, count, stride=CHUNK), :]

    def both(ref, count, j):
        return jnp.concatenate([series(ref.at[h], count, j) for h in range(2)], axis=1)

    def put(size):
        index = lax.broadcasted_iota(jnp.int32, (size, width), 0).astype(jnp.float32)

        def body(r, carry):
            place[r, :size] = jnp.where(index == key[r], 1.0, 0.0).astype(jnp.bfloat16)
            return carry

        return body

    def gather(c, i, size):
        split = []
        for f in range(2):
            block = [x.at[c, f, h].reshape(snaps * CHUNK, LANES) for h in range(2)]
            at = pl.ds(first_far * CHUNK + i, HALF, stride=CHUNK)
            split.extend(halves(jnp.concatenate([b[at, :] for b in block], axis=1)))
        split = jnp.concatenate(split, axis=0).astype(jnp.bfloat16)
        out = lax.dot_general(
            split, place[c * CHUNK + i, :size], (((1,), (1,)), ((), ())), preferred_element_type=jnp.float32
        )
        return [out[2 * f * HALF : (2 * f + 1) * HALF] + out[(2 * f + 1) * HALF : (2 * f + 2) * HALF] for f in range(2)]

    def compact(c):
        start, _ = tiles(c)
        if c < per_level:
            lax.fori_loop(c * CHUNK, (c + 1) * CHUNK, put(width), 0, unroll=2)

            def body(m, carry):
                one, two = gather(c, 2 * m, width), gather(c, 2 * m + 1, width)
                for f in range(2):
                    packed[f, start + 3 * m] = one[f][:, :LANES]
                    packed[f, start + 3 * m + 1] = one[f][:, LANES:] + two[f][:, :LANES]
                    packed[f, start + 3 * m + 2] = two[f][:, LANES:]
                return carry

            lax.fori_loop(0, CHUNK // 2, body, 0, unroll=2)
        else:
            lax.fori_loop(c * CHUNK, (c + 1) * CHUNK, put(LANES), 0, unroll=4)

            def body(i, carry):
                one = gather(c, i, LANES)
                for f in range(2):
                    packed[f, start + i] = one[f]
                return carry

            lax.fori_loop(0, CHUNK, body, 0, unroll=4)

    def wait_local(c):
        for f in range(2):
            for h in range(2):
                local(c, f, h).wait()

    wait_local(0)
    compact(0)
    pl.semaphore_wait(barrier, n_tm - 1 + n_tile - 1)
    start_far(0)
    for k in range(1, n_tile):
        flag_copy(k, z).start()
    for c in range(1, chunks):
        wait_local(c)
    near_copy().start()
    compact(1)
    if DEPTH > 1:
        start_far(1)

    @pl.when(at_end)
    def _():
        far[...] = jnp.zeros(far.shape, jnp.float32)

    for side in range(2):

        @pl.when(jnp.logical_not(receives[side]))
        def _():
            edge_halo[side] = jnp.zeros(edge_halo.shape[1:], jnp.float32)

        @pl.when(jnp.logical_not(z_receives[side]))
        def _():
            edge_in[side] = jnp.zeros(edge_in.shape[1:], jnp.float32)

    all_x, all_y = 0.5 / sx_ref[...], 0.5 / sy_ref[...]
    for j in range(rows):
        cx[j] = all_x[j : j + 1, :]
        cy[j] = all_y[j : j + 1, :]
    for f in range(2):
        for l in range(levels):
            for j in (0, rows + 1):
                mm[f, l, j] = jnp.zeros((snaps, width), jnp.float32)
    column = lax.broadcasted_iota(jnp.int32, (snaps, 2 * HALF), 1)
    valid = ((column >= HALF) | (t > 0)) & ((column < HALF) | (t < n_tm - 1))
    own_w = own_ref[...]
    halo_w = jnp.where(valid, halo_w_ref[...], 0.0)
    weight_sum = jnp.sum(own_w, axis=1, keepdims=True) + jnp.sum(halo_w, axis=1, keepdims=True)
    own_w = own_w / weight_sum
    halo_w = halo_w / weight_sum
    near_half = jnp.where(even, halo_w[:, HALF:], halo_w[:, :HALF])
    far_half = jnp.where(even, halo_w[:, :HALF], halo_w[:, HALF:])
    near_w[...] = stacked_weights(jnp.concatenate([own_w, near_half], axis=1))
    far_w[...] = stacked_weights(far_half)

    lane = lax.broadcasted_iota(jnp.int32, (snaps, LANES), 1)

    def pack(r, acc):
        c, j = r // CHUNK, lax.rem(r, CHUNK)
        for f in range(2):
            q = f * cells + r
            first = series(x.at[c, f, 0], snaps, j) * wet[r][:, :LANES]
            acc = jnp.where(lane == q, pltpu.roll(first, q, 1), acc)
            q = (2 + f) * cells + r
            last = series(x.at[c, f, 1], snaps, j) * wet[r][:, width - LANES :]
            acc = jnp.where(lane == q, pltpu.roll(last, lax.rem(q + 1, LANES), 1), acc)
        return acc

    edge[...] = lax.fori_loop(0, cells, pack, jnp.zeros((snaps, LANES), jnp.float32), unroll=4)
    for side in range(2):

        @pl.when(sends[side])
        def _():
            edge_copy(side).start()

    pass_on(0)
    near_copy().wait_recv()

    def near_part(r, carry):
        l, j = r // rows, lax.rem(r, rows)
        c, i = r // CHUNK, lax.rem(r, CHUNK)
        for f in range(2):
            pieces = [both(x.at[c, f], snaps, i), both(near.at[c, f], HALF, i)]
            mm[f, l, j + 1] = split_dot(near_w[...], pieces)
        return carry

    lax.fori_loop(0, cells, near_part, 0, unroll=8)
    for c in range(2, chunks):
        compact(c)
        if c < DEPTH:
            start_far(c)
    for c in range(1, DEPTH):
        pass_on(c)

    for side in range(2):

        @pl.when(receives[side])
        def _():
            edge_copy(side).wait_recv()

    edge_mean[...] = dot(own_w, edge[...]) + dot(
        halo_w, jnp.concatenate([edge_halo[0], edge_halo[1]], axis=0)
    )
    for side in range(2):

        @pl.when(z_sends[side])
        def _():
            mean_copy(side).start()

    wide = lax.broadcasted_iota(jnp.int32, (snaps, width), 1)

    def spread(r, blocks):
        l, j = r // rows, lax.rem(r, rows)
        size = blocks[0].shape[1]
        split = []
        for block in blocks:
            split.extend(halves(block))
        out = jnp.dot(
            jnp.concatenate(split, axis=0).astype(jnp.bfloat16), place[r, :size], preferred_element_type=jnp.float32
        ).astype(jnp.bfloat16)
        mask = wet[r]
        for f in range(2):
            both_halves = jnp.dot(
                far_w[...], out[2 * f * HALF : 2 * (f + 1) * HALF], preferred_element_type=jnp.float32
            )
            mm[f, l, j + 1] = (mm[f, l, j + 1] + both_halves[:snaps] + both_halves[snaps:]) * mask

    def far_part(c):
        start, _ = tiles(c)
        if c < per_level:

            def body(m, carry):
                base = start + 3 * m
                for k in range(2):
                    spread(
                        c * CHUNK + 2 * m + k,
                        [jnp.concatenate([far[f, base + k], far[f, base + k + 1]], axis=1) for f in range(2)],
                    )
                return carry

            lax.fori_loop(0, CHUNK // 2, body, 0, unroll=2)
        else:

            def body(i, carry):
                spread(c * CHUNK + i, [far[f, start + i] for f in range(2)])
                return carry

            lax.fori_loop(0, CHUNK, body, 0, unroll=4)

    def grad_x(f, r, masked, scale):
        q = (2 + f) * cells + r
        before = pltpu.roll(edge_in[0], lax.rem(2 * LANES - q, LANES), 1)
        q = f * cells + r
        after = pltpu.roll(edge_in[1], lax.rem(2 * LANES - 1 - q, LANES), 1)
        before = jnp.concatenate([before, before], axis=1)
        after = jnp.concatenate([after, after], axis=1)
        behind = jnp.where(wide == 0, before, pltpu.roll(masked, 1, 1))
        ahead = jnp.where(wide == width - 1, after, pltpu.roll(masked, width - 1, 1))
        return (ahead - behind) * scale

    def convert(l):
        def body(j, carry):
            r = l * rows + j
            c, i = r // CHUNK, lax.rem(r, CHUNK)
            mask = wet[r]
            scale_x = cx[j]
            scale_y = cy[j]
            eddy, gx, gy = [], [], []
            for f in range(2):
                masked = mm[f, l, j + 1]
                eddy.append(both(x.at[c, f], snaps, i) - masked)
                gx.append(grad_x(f, r, masked, scale_x))
                gy.append((mm[f, l, j + 2] - mm[f, l, j]) * scale_y)
            eu, ev = eddy
            total = eu * eu * gx[0] + eu * ev * (gy[0] + gx[1]) + ev * ev * gy[1]
            conversion = -mask * total
            for h in range(2):
                cf.at[c, h].reshape(snaps * CHUNK, LANES)[pl.ds(i, snaps, stride=CHUNK), :] = conversion[
                    :, h * LANES : (h + 1) * LANES
                ]
            part[t, r] = jnp.sum(conversion, axis=0, keepdims=True)
            return carry

        return body

    def finish(c):
        for k in range(1, n_tm):
            part_copy(c, k, lax.rem(t + n_tm - k, n_tm)).wait_recv()
        l, low, high = converted(c)
        for j in range(low, high):
            total = part[0, l * rows + j]
            for s in range(1, n_tm):
                total = total + part[s, l * rows + j]
            mean_ref[l, j : j + 1, :] = total / (snaps * n_tm)

    for c in range(chunks):
        @pl.when(has_far)
        def _():
            for f in range(2):
                far_copy(c, f).wait_send()

        if c + DEPTH < chunks:
            start_far(c + DEPTH)

        @pl.when(has_far)
        def _():
            for f in range(2):
                far_copy(c, f).wait_recv()

        far_part(c)
        if c + DEPTH < chunks:
            pass_on(c + DEPTH)
        if c == 0:
            for side in range(2):

                @pl.when(z_receives[side])
                def _():
                    mean_copy(side).wait_recv()

        l, low, high = converted(c)
        lax.fori_loop(low, high, convert(l), 0, unroll=2)
        for k in range(1, n_tm):
            part_copy(c, k, t).start()
        if c % per_level == per_level - 1:

            def narrow(s, carry):
                for h in range(2):
                    block = jnp.concatenate([cf[l * per_level + p, h, s] for p in range(per_level)], axis=0)
                    conv_ref[s, pl.ds(l * rows, rows), pl.ds(h * LANES, LANES)] = block.astype(jnp.bfloat16)
                return carry

            lax.fori_loop(0, snaps, narrow, 0, unroll=4)

    for k in range(1, n_tile):
        flag_copy(k, lax.rem(z + n_tile - k, n_tile)).wait_recv()
    worst = flags[0]
    for s in range(1, n_tile):
        worst = jnp.maximum(worst, flags[s])
    flag_ref[...] = worst
    for c in range(chunks):
        finish(c)

    near_copy().wait_send()
    for side in range(2):

        @pl.when(sends[side])
        def _():
            edge_copy(side).wait_send()

        @pl.when(z_sends[side])
        def _():
            mean_copy(side).wait_send()

    @pl.when(at_end)
    def _():
        for c in range(chunks):
            from_relay(c).wait_send()

    for k in range(1, n_tile):
        flag_copy(k, z).wait_send()
    for c in range(chunks):
        for k in range(1, n_tm):
            part_copy(c, k, t).wait_send()


def full(own, halo, velocity_u, velocity_v, land_sea, bottom_level, spacing_x, spacing_y):
    snaps, cells, width = velocity_u.shape
    rows = land_sea.shape[0]
    levels = cells // rows
    n_tm, n_tile = lax.axis_size("tm"), lax.axis_size("tile")
    chunks = cells // CHUNK
    vmem = pl.BlockSpec(memory_space=pltpu.VMEM)
    hbm = pl.BlockSpec(memory_space=pltpu.HBM)
    f32, bf16 = jnp.float32, jnp.bfloat16
    dma = pltpu.SemaphoreType.DMA
    return pl.pallas_call(
        functools.partial(kernel, n_tm, n_tile, levels),
        out_shape=(
            jax.ShapeDtypeStruct((snaps, cells, width), bf16),
            jax.ShapeDtypeStruct((levels, rows, width), f32),
        ),
        in_specs=[hbm] * 8,
        out_specs=(vmem, vmem),
        scratch_shapes=[
            pltpu.VMEM((rows, width), jnp.int32),
            pltpu.VMEM((rows, width), jnp.int32),
            pltpu.VMEM((rows, width), f32),
            pltpu.VMEM((rows, width), f32),
            pltpu.VMEM(own.shape, f32),
            pltpu.VMEM(halo.shape, f32),
            dma((6,)),
            pltpu.VMEM((chunks, 2, 2, snaps, CHUNK, LANES), f32),
            pltpu.VMEM((2, chunks, 2, 2, HALF, CHUNK, LANES), f32),
            pltpu.VMEM((2, levels, rows + 2, snaps, width), f32),
            pltpu.VMEM((chunks, 2, snaps, CHUNK, LANES), f32),
            pltpu.VMEM((cells, 1, width), f32),
            pltpu.VMEM((rows, 1, width), f32),
            pltpu.VMEM((rows, 1, width), f32),
            pltpu.VMEM((n_tm, cells, 1, width), f32),
            pltpu.VMEM((snaps, LANES), f32),
            pltpu.VMEM((2, HALF, LANES), f32),
            pltpu.VMEM((snaps, LANES), f32),
            pltpu.VMEM((2, snaps, LANES), f32),
            pltpu.VMEM((2 * snaps, 2 * (snaps + HALF)), bf16),
            pltpu.VMEM((2 * snaps, 2 * HALF), bf16),
            pltpu.VMEM((chunks, 2, HALF, CHUNK, LANES), f32),
            dma((chunks, 2)),
            dma((chunks, 2)),
            dma((chunks, 2, 2)),
            dma((2, chunks, 2, 2)),
            dma((2, chunks, 2, 2)),
            dma((2,)),
            dma((2,)),
            dma((2,)),
            dma((2,)),
            dma((chunks, n_tm)),
            dma((chunks, n_tm)),
        ],
        compiler_params=pltpu.CompilerParams(
            collective_id=1, has_side_effects=True, vmem_limit_bytes=60 * 1024 * 1024
        ),
        cost_estimate=pl.CostEstimate(flops=10**9, bytes_accessed=4 * 10**6, transcendentals=0),
    )(
        velocity_u, velocity_v, land_sea, bottom_level, spacing_x, spacing_y, own, halo,
    )


def quick(own, halo, velocity_u, velocity_v, land_sea, bottom_level, spacing_x, spacing_y):
    snaps, cells, width = velocity_u.shape
    rows = land_sea.shape[0]
    levels = cells // rows
    n_tm, n_tile = lax.axis_size("tm"), lax.axis_size("tile")
    chunks = cells // CHUNK
    packs = rows * 3 // 2 + (levels - 1) * rows
    vmem = pl.BlockSpec(memory_space=pltpu.VMEM)
    hbm = pl.BlockSpec(memory_space=pltpu.HBM)
    f32, bf16 = jnp.float32, jnp.bfloat16
    dma = pltpu.SemaphoreType.DMA
    return pl.pallas_call(
        functools.partial(fast_kernel, n_tm, n_tile, levels),
        out_shape=(
            jax.ShapeDtypeStruct((snaps, cells, width), bf16),
            jax.ShapeDtypeStruct((levels, rows, width), f32),
            jax.ShapeDtypeStruct((8, LANES), f32),
        ),
        in_specs=[hbm] * 8,
        out_specs=(vmem, vmem, vmem),
        scratch_shapes=[
            pltpu.VMEM((rows, width), jnp.int32),
            pltpu.VMEM((rows, width), jnp.int32),
            pltpu.VMEM((rows, width), f32),
            pltpu.VMEM((rows, width), f32),
            pltpu.VMEM(own.shape, f32),
            pltpu.VMEM(halo.shape, f32),
            dma((6,)),
            pltpu.VMEM((chunks, 2, 2, snaps, CHUNK, LANES), f32),
            pltpu.VMEM((chunks, 2, 2, HALF, CHUNK, LANES), f32),
            pltpu.VMEM((2, levels, rows + 2, snaps, width), f32),
            pltpu.VMEM((chunks, 2, snaps, CHUNK, LANES), f32),
            pltpu.VMEM((cells, 1, width), f32),
            pltpu.VMEM((cells, 1, width), f32),
            pltpu.VMEM((rows, 1, width), f32),
            pltpu.VMEM((rows, 1, width), f32),
            pltpu.VMEM((n_tm, cells, 1, width), f32),
            pltpu.VMEM((snaps, LANES), f32),
            pltpu.VMEM((2, HALF, LANES), f32),
            pltpu.VMEM((snaps, LANES), f32),
            pltpu.VMEM((2, snaps, LANES), f32),
            pltpu.VMEM((2 * snaps, 2 * (snaps + HALF)), bf16),
            pltpu.VMEM((2 * snaps, 2 * HALF), bf16),
            pltpu.VMEM((cells, width, width), bf16),
            pltpu.VMEM((2, packs, HALF, LANES), f32),
            pltpu.VMEM((2, packs, HALF, LANES), f32),
            pltpu.VMEM((packs, HALF, LANES), f32),
            pltpu.VMEM((n_tile, 8, LANES), f32),
            dma((chunks,)),
            dma((chunks,)),
            dma((chunks, 2, 2)),
            dma((2,)),
            dma((chunks, 2)),
            dma((chunks, 2)),
            dma((2,)),
            dma((2,)),
            dma((2,)),
            dma((2,)),
            dma((chunks, n_tm)),
            dma((chunks, n_tm)),
            dma((n_tile,)),
            dma((n_tile,)),
        ],
        compiler_params=pltpu.CompilerParams(
            collective_id=0, has_side_effects=True, vmem_limit_bytes=60 * 1024 * 1024
        ),
        cost_estimate=pl.CostEstimate(flops=10**9, bytes_accessed=4 * 10**6, transcendentals=0),
    )(
        velocity_u, velocity_v, land_sea, bottom_level, spacing_x, spacing_y, own, halo,
    )


def shards(velocity_u, velocity_v, land_sea, bottom_level, spacing_x, spacing_y):
    snaps, levels, rows, width = velocity_u.shape
    cells = levels * rows
    n_tm = lax.axis_size("tm")
    assert width == 2 * LANES and 4 * cells == LANES and snaps == 2 * HALF
    assert rows % (2 * CHUNK) == 0 and n_tm % 4 == 0 and n_tm >= 8
    own, halo = band_parts(snaps)
    args = (
        jnp.asarray(own), jnp.asarray(halo),
        velocity_u.reshape(snaps, cells, width), velocity_v.reshape(snaps, cells, width),
        land_sea, bottom_level, spacing_x, spacing_y,
    )
    conversion, mean_map, excess = quick(*args)
    conversion, mean_map = lax.cond(
        excess[0, LANES - 1] > 0.0, lambda args, done: full(*args), lambda args, done: done, args, (conversion, mean_map)
    )
    return conversion.reshape(velocity_u.shape), mean_map


def solution(mesh):
    in_specs = (
        P("tm", None, None, "tile"),
        P("tm", None, None, "tile"),
        P(None, "tile"),
        P(None, "tile"),
        P(None, "tile"),
        P(None, "tile"),
    )
    out_specs = (P("tm", None, None, "tile"), P(None, None, "tile"))
    return jax.shard_map(shards, mesh=mesh, in_specs=in_specs, out_specs=out_specs, check_vma=False)
```

```python
import functools

import jax
import jax.numpy as jnp
import numpy as np
from jax import lax
from jax.experimental import pallas as pl
from jax.experimental.pallas import tpu as pltpu
from jax.sharding import PartitionSpec as P

HALF = 24
CUTOFF = 1.0 / 40.0
LANES = 128
CHUNK = 8
DEPTH = 2
MESH = pl.DeviceIdType.MESH


def band_parts(count):
    offset = (np.arange(count + 2 * HALF)[None, :] - np.arange(count)[:, None] - HALF).astype(np.float64)
    weights = 2.0 * CUTOFF * np.sinc(2.0 * CUTOFF * offset) * np.sinc(offset / HALF)
    weights = np.where(np.abs(offset) <= HALF, weights, 0.0).astype(np.float32)
    own = weights[:, HALF : HALF + count]
    halo = np.concatenate([weights[:, :HALF], weights[:, HALF + count :]], axis=1)
    return own, halo


def dot(a, b):
    return jnp.dot(a, b, precision=lax.Precision.HIGHEST, preferred_element_type=jnp.float32)


def halves(a):
    high = a.astype(jnp.bfloat16).astype(jnp.float32)
    return high, a - high


def stacked_weights(w):
    high, low = halves(w)
    return jnp.concatenate(
        [jnp.concatenate([high, high], axis=1), jnp.concatenate([low, low], axis=1)], axis=0
    ).astype(jnp.bfloat16)


def split_dot(weights, pieces):
    split = [halves(p) for p in pieces]
    block = jnp.concatenate([s[0] for s in split] + [s[1] for s in split], axis=0).astype(jnp.bfloat16)
    both = jnp.dot(weights, block, preferred_element_type=jnp.float32)
    half = both.shape[0] // 2
    return both[:half] + both[half:]


def kernel(
    n_tm, n_tile, levels,
    u_ref, v_ref, land_in, bottom_in, sx_in, sy_in, own_in, halo_in,
    conv_ref, mean_ref,
    land_ref, bottom_ref, sx_ref, sy_ref, own_ref, halo_w_ref, small_sem,
    x, halo, mm, cf, wet, cx, cy, part, edge, edge_halo, edge_mean, edge_in,
    near_w, far_w, relayed, relay_send, relay_recv,
    x_sem, bulk_send, bulk_recv, edge_send, edge_recv, em_send, em_recv, part_send, part_recv,
):
    snaps, cells, width = u_ref.shape
    rows = cells // levels
    t = lax.axis_index("tm")
    z = lax.axis_index("tile")
    chunks = cells // CHUNK
    per_level = rows // CHUNK
    fields = (u_ref, v_ref)
    even = lax.rem(t, 2) == 0
    odd = jnp.logical_not(even)

    barrier = pltpu.get_barrier_semaphore()
    for k in range(1, n_tm):
        pl.semaphore_signal(barrier, inc=1, device_id={"tm": lax.rem(t + k, n_tm)}, device_id_type=MESH)

    @pl.when(z > 0)
    def _():
        pl.semaphore_signal(barrier, inc=1, device_id={"tile": z - 1}, device_id_type=MESH)

    @pl.when(z < n_tile - 1)
    def _():
        pl.semaphore_signal(barrier, inc=1, device_id={"tile": z + 1}, device_id_type=MESH)

    def local(c, f, h):
        return pltpu.make_async_copy(
            fields[f].at[:, pl.ds(c * CHUNK, CHUNK), pl.ds(h * LANES, LANES)], x.at[c, f, h], x_sem.at[c, f, h]
        )

    small = (
        (land_in, land_ref), (bottom_in, bottom_ref), (sx_in, sx_ref),
        (sy_in, sy_ref), (own_in, own_ref), (halo_in, halo_w_ref),
    )
    for i, (src, dst) in enumerate(small):
        pltpu.make_async_copy(src, dst, small_sem.at[i]).start()
    for c in range(chunks):
        for f in range(2):
            for h in range(2):
                local(c, f, h).start()

    def bulk(side, c, f, h):
        first = snaps - HALF if side == 0 else 0
        to = t + 1 if side == 0 else t - 1
        return pltpu.make_async_remote_copy(
            src_ref=fields[f].at[pl.ds(first, HALF), pl.ds(c * CHUNK, CHUNK), pl.ds(h * LANES, LANES)],
            dst_ref=halo.at[side, c, f, h],
            send_sem=bulk_send.at[side, c, f, h],
            recv_sem=bulk_recv.at[side, c, f, h],
            device_id={"tm": to},
            device_id_type=MESH,
        )

    middle = (n_tm // 2 - 1, n_tm // 2)
    via = (n_tm - 1, 0)

    def to_relay(side, c, h):
        first = snaps - HALF if side == 0 else 0
        return pltpu.make_async_remote_copy(
            src_ref=fields[1].at[pl.ds(first, HALF), pl.ds(c * CHUNK, CHUNK), pl.ds(h * LANES, LANES)],
            dst_ref=relayed.at[c, h],
            send_sem=bulk_send.at[side, c, 1, h],
            recv_sem=relay_recv.at[c, h],
            device_id={"tm": via[side]},
            device_id_type=MESH,
        )

    def from_relay(side, c, h):
        return pltpu.make_async_remote_copy(
            src_ref=relayed.at[c, h],
            dst_ref=halo.at[side, c, 1, h],
            send_sem=relay_send.at[c, h],
            recv_sem=bulk_recv.at[side, c, 1, h],
            device_id={"tm": middle[1 - side]},
            device_id_type=MESH,
        )

    def pass_on(c):
        if n_tm < 4:
            return
        for side in range(2):

            @pl.when(t == via[side])
            def _():
                for h in range(2):
                    to_relay(side, c, h).wait_recv()
                    from_relay(side, c, h).start()

    def edge_copy(side):
        first = snaps - HALF if side == 0 else 0
        to = t + 1 if side == 0 else t - 1
        return pltpu.make_async_remote_copy(
            src_ref=edge.at[pl.ds(first, HALF), :],
            dst_ref=edge_halo.at[side],
            send_sem=edge_send.at[side],
            recv_sem=edge_recv.at[side],
            device_id={"tm": to},
            device_id_type=MESH,
        )

    def mean_copy(side):
        to = z + 1 if side == 0 else z - 1
        return pltpu.make_async_remote_copy(
            src_ref=edge_mean,
            dst_ref=edge_in.at[side],
            send_sem=em_send.at[side],
            recv_sem=em_recv.at[side],
            device_id={"tile": to},
            device_id_type=MESH,
        )

    def converted(c):
        piece = c % per_level
        low = piece * CHUNK - (1 if piece else 0)
        high = rows if piece == per_level - 1 else (piece + 1) * CHUNK - 1
        return c // per_level, low, high

    def part_copy(c, k, slot):
        l, low, high = converted(c)
        return pltpu.make_async_remote_copy(
            src_ref=part.at[slot, pl.ds(l * rows + low, high - low)],
            dst_ref=part.at[slot, pl.ds(l * rows + low, high - low)],
            send_sem=part_send.at[c, k],
            recv_sem=part_recv.at[c, k],
            device_id={"tm": lax.rem(t + k, n_tm)},
            device_id_type=MESH,
        )

    sends = (t < n_tm - 1, t > 0)
    receives = (t > 0, t < n_tm - 1)
    send_near, send_far = (even, odd), (odd, even)
    near, far = (odd, even), (even, odd)
    z_sends = (z < n_tile - 1, z > 0)
    z_receives = (z > 0, z < n_tile - 1)

    def start_far(c):
        for side in range(2):
            if n_tm >= 4:

                @pl.when(t == middle[side])
                def _():
                    for h in range(2):
                        to_relay(side, c, h).start()
                        bulk(side, c, 0, h).start()

                whole = sends[side] & send_far[side] & (t != middle[side])
            else:
                whole = sends[side] & send_far[side]

            @pl.when(whole)
            def _():
                for f in range(2):
                    for h in range(2):
                        bulk(side, c, f, h).start()

    def finish_send(c, which):
        for side in range(2):

            @pl.when(sends[side] & which[side])
            def _():
                for f in range(2):
                    for h in range(2):
                        bulk(side, c, f, h).wait_send()

    pl.semaphore_wait(barrier, n_tm - 1 + (z > 0).astype(jnp.int32) + (z < n_tile - 1).astype(jnp.int32))

    for c in range(DEPTH):
        start_far(c)
    for side in range(2):

        @pl.when(sends[side] & send_near[side])
        def _():
            for c in range(chunks):
                for f in range(2):
                    for h in range(2):
                        bulk(side, c, f, h).start()

    for side in range(2):

        @pl.when(jnp.logical_not(receives[side]))
        def _():
            halo[side] = jnp.zeros(halo.shape[1:], jnp.float32)
            edge_halo[side] = jnp.zeros(edge_halo.shape[1:], jnp.float32)

        @pl.when(jnp.logical_not(z_receives[side]))
        def _():
            edge_in[side] = jnp.zeros(edge_in.shape[1:], jnp.float32)

    for i, (src, dst) in enumerate(small):
        pltpu.make_async_copy(src, dst, small_sem.at[i]).wait()

    for l in range(levels):
        is_wet = (land_ref[...] == 1) & (l < bottom_ref[...])
        level_wet = jnp.where(is_wet, 1.0, 0.0).astype(jnp.float32)
        for j in range(rows):
            wet[l * rows + j] = level_wet[j : j + 1, :]
    all_x, all_y = 0.5 / sx_ref[...], 0.5 / sy_ref[...]
    for j in range(rows):
        cx[j] = all_x[j : j + 1, :]
        cy[j] = all_y[j : j + 1, :]
    for f in range(2):
        for l in range(levels):
            for j in (0, rows + 1):
                mm[f, l, j] = jnp.zeros((snaps, width), jnp.float32)
    column = lax.broadcasted_iota(jnp.int32, (snaps, 2 * HALF), 1)
    valid = ((column >= HALF) | (t > 0)) & ((column < HALF) | (t < n_tm - 1))
    own_w = own_ref[...]
    halo_w = jnp.where(valid, halo_w_ref[...], 0.0)
    weight_sum = jnp.sum(own_w, axis=1, keepdims=True) + jnp.sum(halo_w, axis=1, keepdims=True)
    own_w = own_w / weight_sum
    halo_w = halo_w / weight_sum
    near_side = 1 - lax.rem(t, 2)
    far_side = lax.rem(t, 2)
    near_half = jnp.where(even, halo_w[:, HALF:], halo_w[:, :HALF])
    far_half = jnp.where(even, halo_w[:, :HALF], halo_w[:, HALF:])
    near_w[...] = stacked_weights(jnp.concatenate([own_w, near_half], axis=1))
    far_w[...] = stacked_weights(far_half)

    for c in range(chunks):
        for f in range(2):
            for h in range(2):
                local(c, f, h).wait()

    def series(ref, count, j):
        return ref.reshape(count * CHUNK, LANES)[pl.ds(j, count, stride=CHUNK), :]

    def both(ref, count, j):
        return jnp.concatenate([series(ref.at[h], count, j) for h in range(2)], axis=1)

    lane = lax.broadcasted_iota(jnp.int32, (snaps, LANES), 1)

    def pack(r, acc):
        c, j = r // CHUNK, lax.rem(r, CHUNK)
        for f in range(2):
            q = f * cells + r
            first = series(x.at[c, f, 0], snaps, j) * wet[r][:, :LANES]
            acc = jnp.where(lane == q, pltpu.roll(first, q, 1), acc)
            q = (2 + f) * cells + r
            last = series(x.at[c, f, 1], snaps, j) * wet[r][:, width - LANES :]
            acc = jnp.where(lane == q, pltpu.roll(last, lax.rem(q + 1, LANES), 1), acc)
        return acc

    edge[...] = lax.fori_loop(0, cells, pack, jnp.zeros((snaps, LANES), jnp.float32), unroll=4)
    for side in range(2):

        @pl.when(sends[side])
        def _():
            edge_copy(side).start()

    pass_on(0)

    for side in range(2):

        @pl.when(receives[side] & near[side])
        def _():
            for c in range(chunks):
                for f in range(2):
                    for h in range(2):
                        bulk(side, c, f, h).wait_recv()

    def near_part(r, carry):
        l, j = r // rows, lax.rem(r, rows)
        c, i = r // CHUNK, lax.rem(r, CHUNK)
        for f in range(2):
            pieces = [both(x.at[c, f], snaps, i), both(halo.at[near_side, c, f], HALF, i)]
            mm[f, l, j + 1] = split_dot(near_w[...], pieces)
        return carry

    lax.fori_loop(0, cells, near_part, 0, unroll=8)
    for c in range(1, DEPTH):
        pass_on(c)

    for side in range(2):

        @pl.when(receives[side])
        def _():
            edge_copy(side).wait_recv()

    edge_mean[...] = dot(own_w, edge[...]) + dot(
        halo_w, jnp.concatenate([edge_halo[0], edge_halo[1]], axis=0)
    )
    for side in range(2):

        @pl.when(z_sends[side])
        def _():
            mean_copy(side).start()

    wide = lax.broadcasted_iota(jnp.int32, (snaps, width), 1)

    def far_part(r, carry):
        l, j = r // rows, lax.rem(r, rows)
        c, i = r // CHUNK, lax.rem(r, CHUNK)
        mask = wet[r]
        for f in range(2):
            pieces = [both(halo.at[far_side, c, f], HALF, i)]
            mm[f, l, j + 1] = (mm[f, l, j + 1] + split_dot(far_w[...], pieces)) * mask
        return carry

    def grad_x(f, r, masked, scale):
        q = (2 + f) * cells + r
        before = pltpu.roll(edge_in[0], lax.rem(2 * LANES - q, LANES), 1)
        q = f * cells + r
        after = pltpu.roll(edge_in[1], lax.rem(2 * LANES - 1 - q, LANES), 1)
        before = jnp.concatenate([before, before], axis=1)
        after = jnp.concatenate([after, after], axis=1)
        behind = jnp.where(wide == 0, before, pltpu.roll(masked, 1, 1))
        ahead = jnp.where(wide == width - 1, after, pltpu.roll(masked, width - 1, 1))
        return (ahead - behind) * scale

    def convert(l):
        def body(j, carry):
            r = l * rows + j
            c, i = r // CHUNK, lax.rem(r, CHUNK)
            mask = wet[r]
            scale_x = cx[j]
            scale_y = cy[j]
            eddy, gx, gy = [], [], []
            for f in range(2):
                masked = mm[f, l, j + 1]
                eddy.append(both(x.at[c, f], snaps, i) - masked)
                gx.append(grad_x(f, r, masked, scale_x))
                gy.append((mm[f, l, j + 2] - mm[f, l, j]) * scale_y)
            eu, ev = eddy
            total = eu * eu * gx[0] + eu * ev * (gy[0] + gx[1]) + ev * ev * gy[1]
            conversion = -mask * total
            for h in range(2):
                cf.at[c, h].reshape(snaps * CHUNK, LANES)[pl.ds(i, snaps, stride=CHUNK), :] = conversion[
                    :, h * LANES : (h + 1) * LANES
                ]
            part[t, r] = jnp.sum(conversion, axis=0, keepdims=True)
            return carry

        return body

    for c in range(chunks):
        finish_send(c, send_far)
        if c + DEPTH < chunks:
            start_far(c + DEPTH)
        for side in range(2):

            @pl.when(receives[side] & far[side])
            def _():
                for f in range(2):
                    for h in range(2):
                        bulk(side, c, f, h).wait_recv()

        lax.fori_loop(c * CHUNK, (c + 1) * CHUNK, far_part, 0, unroll=8)
        if c + DEPTH < chunks:
            pass_on(c + DEPTH)
        if c == 0:
            for side in range(2):

                @pl.when(z_receives[side])
                def _():
                    mean_copy(side).wait_recv()

        l, low, high = converted(c)
        lax.fori_loop(low, high, convert(l), 0, unroll=2)
        for k in range(1, n_tm):
            part_copy(c, k, t).start()
        if c % per_level == per_level - 1:

            def narrow(s, carry):
                for h in range(2):
                    block = jnp.concatenate([cf[l * per_level + p, h, s] for p in range(per_level)], axis=0)
                    conv_ref[s, pl.ds(l * rows, rows), pl.ds(h * LANES, LANES)] = block.astype(jnp.bfloat16)
                return carry

            lax.fori_loop(0, snaps, narrow, 0, unroll=4)

    for c in range(chunks):
        for k in range(1, n_tm):
            part_copy(c, k, lax.rem(t + n_tm - k, n_tm)).wait_recv()
        l, low, high = converted(c)
        for j in range(low, high):
            total = part[0, l * rows + j]
            for s in range(1, n_tm):
                total = total + part[s, l * rows + j]
            mean_ref[l, j : j + 1, :] = total / (snaps * n_tm)

    for c in range(chunks):
        finish_send(c, send_near)
    for side in range(2):

        @pl.when(sends[side])
        def _():
            edge_copy(side).wait_send()

        @pl.when(z_sends[side])
        def _():
            mean_copy(side).wait_send()

        if n_tm >= 4:

            @pl.when(t == via[side])
            def _():
                for c in range(chunks):
                    for h in range(2):
                        from_relay(side, c, h).wait_send()

    for c in range(chunks):
        for k in range(1, n_tm):
            part_copy(c, k, t).wait_send()


def fast_kernel(
    n_tm, n_tile, levels,
    u_ref, v_ref, land_in, bottom_in, sx_in, sy_in, own_in, halo_in,
    conv_ref, mean_ref, flag_ref,
    land_ref, bottom_ref, sx_ref, sy_ref, own_ref, halo_w_ref, small_sem,
    x, near, mm, cf, wet, key, cx, cy, part, edge, edge_halo, edge_mean, edge_in,
    near_w, far_w, place, packed, far, relayed, flags,
    relay_send, relay_recv, x_sem, near_sem, far_send, far_recv, edge_send, edge_recv, em_send, em_recv,
    part_send, part_recv, flag_send, flag_recv,
):
    snaps, cells, width = u_ref.shape
    rows = cells // levels
    t = lax.axis_index("tm")
    z = lax.axis_index("tile")
    chunks = cells // CHUNK
    per_level = rows // CHUNK
    fields = (u_ref, v_ref)
    even = lax.rem(t, 2) == 0
    odd = jnp.logical_not(even)

    barrier = pltpu.get_barrier_semaphore()
    for k in range(1, n_tm):
        pl.semaphore_signal(barrier, inc=1, device_id={"tm": lax.rem(t + k, n_tm)}, device_id_type=MESH)
    for k in range(1, n_tile):
        pl.semaphore_signal(barrier, inc=1, device_id={"tile": lax.rem(z + k, n_tile)}, device_id_type=MESH)

    def local(c, f, h):
        return pltpu.make_async_copy(
            fields[f].at[:, pl.ds(c * CHUNK, CHUNK), pl.ds(h * LANES, LANES)], x.at[c, f, h], x_sem.at[c, f, h]
        )

    small = (
        (land_in, land_ref), (bottom_in, bottom_ref), (sx_in, sx_ref),
        (sy_in, sy_ref), (own_in, own_ref), (halo_in, halo_w_ref),
    )
    for i, (src, dst) in enumerate(small):
        pltpu.make_async_copy(src, dst, small_sem.at[i]).start()
    for c in range(chunks):
        for f in range(2):
            for h in range(2):
                local(c, f, h).start()

    first_far = jnp.where(even, 0, snaps - HALF)
    first_near = jnp.where(even, snaps - HALF, 0)
    has_far = (t > 0) & (t < n_tm - 1)
    at_end = jnp.logical_not(has_far)
    is_middle = (t == n_tm // 2 - 1) | (t == n_tm // 2)
    far_to = jnp.where(even, t - 1, t + 1)
    via_to = jnp.where(t < n_tm // 2, n_tm - 1, 0)
    forward_to = jnp.where(t == 0, n_tm // 2 - 1, n_tm // 2)

    def tiles(c):
        wide = CHUNK * 3 // 2
        l = c // per_level
        start = c * wide if l == 0 else per_level * wide + (c - per_level) * CHUNK
        return start, wide if l == 0 else CHUNK

    def near_copy():
        return pltpu.make_async_remote_copy(
            src_ref=x.at[:, :, :, pl.ds(first_near, HALF)],
            dst_ref=near,
            send_sem=near_sem.at[0],
            recv_sem=near_sem.at[1],
            device_id={"tm": t + 1 - 2 * lax.rem(t, 2)},
            device_id_type=MESH,
        )

    def far_copy(c, f):
        start, count = tiles(c)
        return pltpu.make_async_remote_copy(
            src_ref=packed.at[f, pl.ds(start, count)],
            dst_ref=far.at[f, pl.ds(start, count)],
            send_sem=far_send.at[c, f],
            recv_sem=far_recv.at[c, f],
            device_id={"tm": far_to},
            device_id_type=MESH,
        )

    def to_relay(c):
        start, count = tiles(c)
        return pltpu.make_async_remote_copy(
            src_ref=packed.at[1, pl.ds(start, count)],
            dst_ref=relayed.at[pl.ds(start, count)],
            send_sem=far_send.at[c, 1],
            recv_sem=relay_recv.at[c],
            device_id={"tm": via_to},
            device_id_type=MESH,
        )

    def from_relay(c):
        start, count = tiles(c)
        return pltpu.make_async_remote_copy(
            src_ref=relayed.at[pl.ds(start, count)],
            dst_ref=far.at[1, pl.ds(start, count)],
            send_sem=relay_send.at[c],
            recv_sem=far_recv.at[c, 1],
            device_id={"tm": forward_to},
            device_id_type=MESH,
        )

    def pass_on(c):
        @pl.when(at_end)
        def _():
            to_relay(c).wait_recv()
            from_relay(c).start()

    def start_far(c):
        @pl.when(has_far)
        def _():
            far_copy(c, 0).start()

        @pl.when(is_middle)
        def _():
            to_relay(c).start()

        @pl.when(has_far & jnp.logical_not(is_middle))
        def _():
            far_copy(c, 1).start()

    def edge_copy(side):
        first = snaps - HALF if side == 0 else 0
        to = t + 1 if side == 0 else t - 1
        return pltpu.make_async_remote_copy(
            src_ref=edge.at[pl.ds(first, HALF), :],
            dst_ref=edge_halo.at[side],
            send_sem=edge_send.at[side],
            recv_sem=edge_recv.at[side],
            device_id={"tm": to},
            device_id_type=MESH,
        )

    def mean_copy(side):
        to = z + 1 if side == 0 else z - 1
        return pltpu.make_async_remote_copy(
            src_ref=edge_mean,
            dst_ref=edge_in.at[side],
            send_sem=em_send.at[side],
            recv_sem=em_recv.at[side],
            device_id={"tile": to},
            device_id_type=MESH,
        )

    def flag_copy(k, slot):
        return pltpu.make_async_remote_copy(
            src_ref=flags.at[slot],
            dst_ref=flags.at[slot],
            send_sem=flag_send.at[k],
            recv_sem=flag_recv.at[k],
            device_id={"tile": lax.rem(z + k, n_tile)},
            device_id_type=MESH,
        )

    def converted(c):
        piece = c % per_level
        low = piece * CHUNK - (1 if piece else 0)
        high = rows if piece == per_level - 1 else (piece + 1) * CHUNK - 1
        return c // per_level, low, high

    def part_copy(c, k, slot):
        l, low, high = converted(c)
        return pltpu.make_async_remote_copy(
            src_ref=part.at[slot, pl.ds(l * rows + low, high - low)],
            dst_ref=part.at[slot, pl.ds(l * rows + low, high - low)],
            send_sem=part_send.at[c, k],
            recv_sem=part_recv.at[c, k],
            device_id={"tm": lax.rem(t + k, n_tm)},
            device_id_type=MESH,
        )

    sends = (t < n_tm - 1, t > 0)
    receives = (t > 0, t < n_tm - 1)
    z_sends = (z < n_tile - 1, z > 0)
    z_receives = (z > 0, z < n_tile - 1)

    for i, (src, dst) in enumerate(small):
        pltpu.make_async_copy(src, dst, small_sem.at[i]).wait()

    levels_wet = []
    for l in range(levels):
        is_wet = (land_ref[...] == 1) & (l < bottom_ref[...])
        levels_wet.append(jnp.where(is_wet, 1.0, 0.0).astype(jnp.float32))
    all_wet = jnp.concatenate(levels_wet, axis=0)
    lower = lax.broadcasted_iota(jnp.int32, (width, width), 0)
    upper = lax.broadcasted_iota(jnp.int32, (width, width), 1)
    before = jnp.where(lower < upper, 1.0, 0.0).astype(jnp.bfloat16)
    order = jnp.dot(all_wet.astype(jnp.bfloat16), before, preferred_element_type=jnp.float32)
    row = lax.broadcasted_iota(jnp.int32, (cells, width), 0)
    room = jnp.where(row < rows, float(width * 3 // 4), float(width // 2))
    shift = jnp.where((row < rows) & (lax.rem(row, 2) == 1), float(width // 4), 0.0)
    all_key = jnp.where((all_wet > 0.0) & (order < room), order + shift, -1.0)
    over = jnp.max(order + all_wet - room, axis=0, keepdims=True)
    flags[z] = jnp.broadcast_to(jnp.maximum(over[:, :LANES], over[:, LANES:]), (8, LANES))
    for r in range(cells):
        wet[r] = all_wet[r : r + 1, :]
        key[r] = all_key[r : r + 1, :]

    def series(ref, count, j):
        return ref.reshape(count * CHUNK, LANES)[pl.ds(j, count, stride=CHUNK), :]

    def both(ref, count, j):
        return jnp.concatenate([series(ref.at[h], count, j) for h in range(2)], axis=1)

    def put(size):
        index = lax.broadcasted_iota(jnp.int32, (size, width), 0).astype(jnp.float32)

        def body(r, carry):
            place[r, :size] = jnp.where(index == key[r], 1.0, 0.0).astype(jnp.bfloat16)
            return carry

        return body

    def gather(c, i, size):
        split = []
        for f in range(2):
            block = [x.at[c, f, h].reshape(snaps * CHUNK, LANES) for h in range(2)]
            at = pl.ds(first_far * CHUNK + i, HALF, stride=CHUNK)
            split.extend(halves(jnp.concatenate([b[at, :] for b in block], axis=1)))
        split = jnp.concatenate(split, axis=0).astype(jnp.bfloat16)
        out = lax.dot_general(
            split, place[c * CHUNK + i, :size], (((1,), (1,)), ((), ())), preferred_element_type=jnp.float32
        )
        return [out[2 * f * HALF : (2 * f + 1) * HALF] + out[(2 * f + 1) * HALF : (2 * f + 2) * HALF] for f in range(2)]

    def compact(c):
        start, _ = tiles(c)
        if c < per_level:
            lax.fori_loop(c * CHUNK, (c + 1) * CHUNK, put(width), 0, unroll=2)

            def body(m, carry):
                one, two = gather(c, 2 * m, width), gather(c, 2 * m + 1, width)
                for f in range(2):
                    packed[f, start + 3 * m] = one[f][:, :LANES]
                    packed[f, start + 3 * m + 1] = one[f][:, LANES:] + two[f][:, :LANES]
                    packed[f, start + 3 * m + 2] = two[f][:, LANES:]
                return carry

            lax.fori_loop(0, CHUNK // 2, body, 0, unroll=2)
        else:
            lax.fori_loop(c * CHUNK, (c + 1) * CHUNK, put(LANES), 0, unroll=4)

            def body(i, carry):
                one = gather(c, i, LANES)
                for f in range(2):
                    packed[f, start + i] = one[f]
                return carry

            lax.fori_loop(0, CHUNK, body, 0, unroll=4)

    def wait_local(c):
        for f in range(2):
            for h in range(2):
                local(c, f, h).wait()

    wait_local(0)
    compact(0)
    pl.semaphore_wait(barrier, n_tm - 1 + n_tile - 1)
    start_far(0)
    for k in range(1, n_tile):
        flag_copy(k, z).start()
    for c in range(1, chunks):
        wait_local(c)
    near_copy().start()
    compact(1)
    if DEPTH > 1:
        start_far(1)

    @pl.when(at_end)
    def _():
        far[...] = jnp.zeros(far.shape, jnp.float32)

    for side in range(2):

        @pl.when(jnp.logical_not(receives[side]))
        def _():
            edge_halo[side] = jnp.zeros(edge_halo.shape[1:], jnp.float32)

        @pl.when(jnp.logical_not(z_receives[side]))
        def _():
            edge_in[side] = jnp.zeros(edge_in.shape[1:], jnp.float32)

    all_x, all_y = 0.5 / sx_ref[...], 0.5 / sy_ref[...]
    for j in range(rows):
        cx[j] = all_x[j : j + 1, :]
        cy[j] = all_y[j : j + 1, :]
    for f in range(2):
        for l in range(levels):
            for j in (0, rows + 1):
                mm[f, l, j] = jnp.zeros((snaps, width), jnp.float32)
    column = lax.broadcasted_iota(jnp.int32, (snaps, 2 * HALF), 1)
    valid = ((column >= HALF) | (t > 0)) & ((column < HALF) | (t < n_tm - 1))
    own_w = own_ref[...]
    halo_w = jnp.where(valid, halo_w_ref[...], 0.0)
    weight_sum = jnp.sum(own_w, axis=1, keepdims=True) + jnp.sum(halo_w, axis=1, keepdims=True)
    own_w = own_w / weight_sum
    halo_w = halo_w / weight_sum
    near_half = jnp.where(even, halo_w[:, HALF:], halo_w[:, :HALF])
    far_half = jnp.where(even, halo_w[:, :HALF], halo_w[:, HALF:])
    near_w[...] = stacked_weights(jnp.concatenate([own_w, near_half], axis=1))
    far_w[...] = stacked_weights(far_half)

    lane = lax.broadcasted_iota(jnp.int32, (snaps, LANES), 1)

    def pack(r, acc):
        c, j = r // CHUNK, lax.rem(r, CHUNK)
        for f in range(2):
            q = f * cells + r
            first = series(x.at[c, f, 0], snaps, j) * wet[r][:, :LANES]
            acc = jnp.where(lane == q, pltpu.roll(first, q, 1), acc)
            q = (2 + f) * cells + r
            last = series(x.at[c, f, 1], snaps, j) * wet[r][:, width - LANES :]
            acc = jnp.where(lane == q, pltpu.roll(last, lax.rem(q + 1, LANES), 1), acc)
        return acc

    edge[...] = lax.fori_loop(0, cells, pack, jnp.zeros((snaps, LANES), jnp.float32), unroll=4)
    for side in range(2):

        @pl.when(sends[side])
        def _():
            edge_copy(side).start()

    pass_on(0)
    near_copy().wait_recv()

    def near_part(r, carry):
        l, j = r // rows, lax.rem(r, rows)
        c, i = r // CHUNK, lax.rem(r, CHUNK)
        for f in range(2):
            pieces = [both(x.at[c, f], snaps, i), both(near.at[c, f], HALF, i)]
            mm[f, l, j + 1] = split_dot(near_w[...], pieces)
        return carry

    lax.fori_loop(0, cells, near_part, 0, unroll=8)
    for c in range(2, chunks):
        compact(c)
        if c < DEPTH:
            start_far(c)
    for c in range(1, DEPTH):
        pass_on(c)

    for side in range(2):

        @pl.when(receives[side])
        def _():
            edge_copy(side).wait_recv()

    edge_mean[...] = dot(own_w, edge[...]) + dot(
        halo_w, jnp.concatenate([edge_halo[0], edge_halo[1]], axis=0)
    )
    for side in range(2):

        @pl.when(z_sends[side])
        def _():
            mean_copy(side).start()

    wide = lax.broadcasted_iota(jnp.int32, (snaps, width), 1)

    def spread(r, blocks):
        l, j = r // rows, lax.rem(r, rows)
        size = blocks[0].shape[1]
        split = []
        for block in blocks:
            split.extend(halves(block))
        out = jnp.dot(
            jnp.concatenate(split, axis=0).astype(jnp.bfloat16), place[r, :size], preferred_element_type=jnp.float32
        ).astype(jnp.bfloat16)
        mask = wet[r]
        for f in range(2):
            both_halves = jnp.dot(
                far_w[...], out[2 * f * HALF : 2 * (f + 1) * HALF], preferred_element_type=jnp.float32
            )
            mm[f, l, j + 1] = (mm[f, l, j + 1] + both_halves[:snaps] + both_halves[snaps:]) * mask

    def far_part(c):
        start, _ = tiles(c)
        if c < per_level:

            def body(m, carry):
                base = start + 3 * m
                for k in range(2):
                    spread(
                        c * CHUNK + 2 * m + k,
                        [jnp.concatenate([far[f, base + k], far[f, base + k + 1]], axis=1) for f in range(2)],
                    )
                return carry

            lax.fori_loop(0, CHUNK // 2, body, 0, unroll=2)
        else:

            def body(i, carry):
                spread(c * CHUNK + i, [far[f, start + i] for f in range(2)])
                return carry

            lax.fori_loop(0, CHUNK, body, 0, unroll=4)

    def grad_x(f, r, masked, scale):
        q = (2 + f) * cells + r
        before = pltpu.roll(edge_in[0], lax.rem(2 * LANES - q, LANES), 1)
        q = f * cells + r
        after = pltpu.roll(edge_in[1], lax.rem(2 * LANES - 1 - q, LANES), 1)
        before = jnp.concatenate([before, before], axis=1)
        after = jnp.concatenate([after, after], axis=1)
        behind = jnp.where(wide == 0, before, pltpu.roll(masked, 1, 1))
        ahead = jnp.where(wide == width - 1, after, pltpu.roll(masked, width - 1, 1))
        return (ahead - behind) * scale

    def convert(l):
        def body(j, carry):
            r = l * rows + j
            c, i = r // CHUNK, lax.rem(r, CHUNK)
            mask = wet[r]
            scale_x = cx[j]
            scale_y = cy[j]
            eddy, gx, gy = [], [], []
            for f in range(2):
                masked = mm[f, l, j + 1]
                eddy.append(both(x.at[c, f], snaps, i) - masked)
                gx.append(grad_x(f, r, masked, scale_x))
                gy.append((mm[f, l, j + 2] - mm[f, l, j]) * scale_y)
            eu, ev = eddy
            total = eu * eu * gx[0] + eu * ev * (gy[0] + gx[1]) + ev * ev * gy[1]
            conversion = -mask * total
            for h in range(2):
                cf.at[c, h].reshape(snaps * CHUNK, LANES)[pl.ds(i, snaps, stride=CHUNK), :] = conversion[
                    :, h * LANES : (h + 1) * LANES
                ]
            part[t, r] = jnp.sum(conversion, axis=0, keepdims=True)
            return carry

        return body

    def finish(c):
        for k in range(1, n_tm):
            part_copy(c, k, lax.rem(t + n_tm - k, n_tm)).wait_recv()
        l, low, high = converted(c)
        for j in range(low, high):
            total = part[0, l * rows + j]
            for s in range(1, n_tm):
                total = total + part[s, l * rows + j]
            mean_ref[l, j : j + 1, :] = total / (snaps * n_tm)

    for c in range(chunks):
        @pl.when(has_far)
        def _():
            for f in range(2):
                far_copy(c, f).wait_send()

        if c + DEPTH < chunks:
            start_far(c + DEPTH)

        @pl.when(has_far)
        def _():
            for f in range(2):
                far_copy(c, f).wait_recv()

        far_part(c)
        if c + DEPTH < chunks:
            pass_on(c + DEPTH)
        if c == 0:
            for side in range(2):

                @pl.when(z_receives[side])
                def _():
                    mean_copy(side).wait_recv()

        l, low, high = converted(c)
        lax.fori_loop(low, high, convert(l), 0, unroll=4)
        for k in range(1, n_tm):
            part_copy(c, k, t).start()
        if c % per_level == per_level - 1:

            def narrow(s, carry):
                for h in range(2):
                    block = jnp.concatenate([cf[l * per_level + p, h, s] for p in range(per_level)], axis=0)
                    conv_ref[s, pl.ds(l * rows, rows), pl.ds(h * LANES, LANES)] = block.astype(jnp.bfloat16)
                return carry

            lax.fori_loop(0, snaps, narrow, 0, unroll=4)

    for k in range(1, n_tile):
        flag_copy(k, lax.rem(z + n_tile - k, n_tile)).wait_recv()
    worst = flags[0]
    for s in range(1, n_tile):
        worst = jnp.maximum(worst, flags[s])
    flag_ref[0] = jnp.max(worst[:, LANES - 1 :])
    for c in range(chunks):
        finish(c)

    near_copy().wait_send()
    for side in range(2):

        @pl.when(sends[side])
        def _():
            edge_copy(side).wait_send()

        @pl.when(z_sends[side])
        def _():
            mean_copy(side).wait_send()

    @pl.when(at_end)
    def _():
        for c in range(chunks):
            from_relay(c).wait_send()

    for k in range(1, n_tile):
        flag_copy(k, z).wait_send()
    for c in range(chunks):
        for k in range(1, n_tm):
            part_copy(c, k, t).wait_send()


def full(own, halo, velocity_u, velocity_v, land_sea, bottom_level, spacing_x, spacing_y):
    snaps, cells, width = velocity_u.shape
    rows = land_sea.shape[0]
    levels = cells // rows
    n_tm, n_tile = lax.axis_size("tm"), lax.axis_size("tile")
    chunks = cells // CHUNK
    vmem = pl.BlockSpec(memory_space=pltpu.VMEM)
    hbm = pl.BlockSpec(memory_space=pltpu.HBM)
    f32, bf16 = jnp.float32, jnp.bfloat16
    dma = pltpu.SemaphoreType.DMA
    return pl.pallas_call(
        functools.partial(kernel, n_tm, n_tile, levels),
        out_shape=(
            jax.ShapeDtypeStruct((snaps, cells, width), bf16),
            jax.ShapeDtypeStruct((levels, rows, width), f32),
        ),
        in_specs=[hbm] * 8,
        out_specs=(vmem, vmem),
        scratch_shapes=[
            pltpu.VMEM((rows, width), jnp.int32),
            pltpu.VMEM((rows, width), jnp.int32),
            pltpu.VMEM((rows, width), f32),
            pltpu.VMEM((rows, width), f32),
            pltpu.VMEM(own.shape, f32),
            pltpu.VMEM(halo.shape, f32),
            dma((6,)),
            pltpu.VMEM((chunks, 2, 2, snaps, CHUNK, LANES), f32),
            pltpu.VMEM((2, chunks, 2, 2, HALF, CHUNK, LANES), f32),
            pltpu.VMEM((2, levels, rows + 2, snaps, width), f32),
            pltpu.VMEM((chunks, 2, snaps, CHUNK, LANES), f32),
            pltpu.VMEM((cells, 1, width), f32),
            pltpu.VMEM((rows, 1, width), f32),
            pltpu.VMEM((rows, 1, width), f32),
            pltpu.VMEM((n_tm, cells, 1, width), f32),
            pltpu.VMEM((snaps, LANES), f32),
            pltpu.VMEM((2, HALF, LANES), f32),
            pltpu.VMEM((snaps, LANES), f32),
            pltpu.VMEM((2, snaps, LANES), f32),
            pltpu.VMEM((2 * snaps, 2 * (snaps + HALF)), bf16),
            pltpu.VMEM((2 * snaps, 2 * HALF), bf16),
            pltpu.VMEM((chunks, 2, HALF, CHUNK, LANES), f32),
            dma((chunks, 2)),
            dma((chunks, 2)),
            dma((chunks, 2, 2)),
            dma((2, chunks, 2, 2)),
            dma((2, chunks, 2, 2)),
            dma((2,)),
            dma((2,)),
            dma((2,)),
            dma((2,)),
            dma((chunks, n_tm)),
            dma((chunks, n_tm)),
        ],
        compiler_params=pltpu.CompilerParams(
            collective_id=1, has_side_effects=True, vmem_limit_bytes=60 * 1024 * 1024
        ),
        cost_estimate=pl.CostEstimate(flops=10**9, bytes_accessed=4 * 10**6, transcendentals=0),
    )(
        velocity_u, velocity_v, land_sea, bottom_level, spacing_x, spacing_y, own, halo,
    )


def quick(own, halo, velocity_u, velocity_v, land_sea, bottom_level, spacing_x, spacing_y):
    snaps, cells, width = velocity_u.shape
    rows = land_sea.shape[0]
    levels = cells // rows
    n_tm, n_tile = lax.axis_size("tm"), lax.axis_size("tile")
    chunks = cells // CHUNK
    packs = rows * 3 // 2 + (levels - 1) * rows
    vmem = pl.BlockSpec(memory_space=pltpu.VMEM)
    hbm = pl.BlockSpec(memory_space=pltpu.HBM)
    f32, bf16 = jnp.float32, jnp.bfloat16
    dma = pltpu.SemaphoreType.DMA
    return pl.pallas_call(
        functools.partial(fast_kernel, n_tm, n_tile, levels),
        out_shape=(
            jax.ShapeDtypeStruct((snaps, cells, width), bf16),
            jax.ShapeDtypeStruct((levels, rows, width), f32),
            jax.ShapeDtypeStruct((1,), f32),
        ),
        in_specs=[hbm] * 8,
        out_specs=(vmem, vmem, pl.BlockSpec(memory_space=pltpu.SMEM)),
        scratch_shapes=[
            pltpu.VMEM((rows, width), jnp.int32),
            pltpu.VMEM((rows, width), jnp.int32),
            pltpu.VMEM((rows, width), f32),
            pltpu.VMEM((rows, width), f32),
            pltpu.VMEM(own.shape, f32),
            pltpu.VMEM(halo.shape, f32),
            dma((6,)),
            pltpu.VMEM((chunks, 2, 2, snaps, CHUNK, LANES), f32),
            pltpu.VMEM((chunks, 2, 2, HALF, CHUNK, LANES), f32),
            pltpu.VMEM((2, levels, rows + 2, snaps, width), f32),
            pltpu.VMEM((chunks, 2, snaps, CHUNK, LANES), f32),
            pltpu.VMEM((cells, 1, width), f32),
            pltpu.VMEM((cells, 1, width), f32),
            pltpu.VMEM((rows, 1, width), f32),
            pltpu.VMEM((rows, 1, width), f32),
            pltpu.VMEM((n_tm, cells, 1, width), f32),
            pltpu.VMEM((snaps, LANES), f32),
            pltpu.VMEM((2, HALF, LANES), f32),
            pltpu.VMEM((snaps, LANES), f32),
            pltpu.VMEM((2, snaps, LANES), f32),
            pltpu.VMEM((2 * snaps, 2 * (snaps + HALF)), bf16),
            pltpu.VMEM((2 * snaps, 2 * HALF), bf16),
            pltpu.VMEM((cells, width, width), bf16),
            pltpu.VMEM((2, packs, HALF, LANES), f32),
            pltpu.VMEM((2, packs, HALF, LANES), f32),
            pltpu.VMEM((packs, HALF, LANES), f32),
            pltpu.VMEM((n_tile, 8, LANES), f32),
            dma((chunks,)),
            dma((chunks,)),
            dma((chunks, 2, 2)),
            dma((2,)),
            dma((chunks, 2)),
            dma((chunks, 2)),
            dma((2,)),
            dma((2,)),
            dma((2,)),
            dma((2,)),
            dma((chunks, n_tm)),
            dma((chunks, n_tm)),
            dma((n_tile,)),
            dma((n_tile,)),
        ],
        compiler_params=pltpu.CompilerParams(
            collective_id=0, has_side_effects=True, vmem_limit_bytes=60 * 1024 * 1024
        ),
        cost_estimate=pl.CostEstimate(flops=10**9, bytes_accessed=4 * 10**6, transcendentals=0),
    )(
        velocity_u, velocity_v, land_sea, bottom_level, spacing_x, spacing_y, own, halo,
    )


def shards(velocity_u, velocity_v, land_sea, bottom_level, spacing_x, spacing_y):
    snaps, levels, rows, width = velocity_u.shape
    cells = levels * rows
    n_tm = lax.axis_size("tm")
    assert width == 2 * LANES and 4 * cells == LANES and snaps == 2 * HALF
    assert rows % (2 * CHUNK) == 0 and n_tm % 4 == 0 and n_tm >= 8
    own, halo = band_parts(snaps)
    args = (
        jnp.asarray(own), jnp.asarray(halo),
        velocity_u.reshape(snaps, cells, width), velocity_v.reshape(snaps, cells, width),
        land_sea, bottom_level, spacing_x, spacing_y,
    )
    conversion, mean_map, excess = quick(*args)
    conversion, mean_map = lax.cond(
        excess[0] > 0.0, lambda args, done: full(*args), lambda args, done: done, args, (conversion, mean_map)
    )
    conversion, mean_map = store(conversion, mean_map)
    return conversion.reshape(velocity_u.shape), mean_map


def store_kernel(a_ref, b_ref, a_out, b_out, sem):
    copies = [
        pltpu.make_async_copy(a_ref, a_out, sem.at[0]),
        pltpu.make_async_copy(b_ref, b_out, sem.at[1]),
    ]
    for copy in copies:
        copy.start()
    for copy in copies:
        copy.wait()


def store(a, b):
    place = pl.BlockSpec(memory_space=pl.ANY)
    return pl.pallas_call(
        store_kernel,
        out_shape=(jax.ShapeDtypeStruct(a.shape, a.dtype), jax.ShapeDtypeStruct(b.shape, b.dtype)),
        in_specs=[place, place],
        out_specs=(pl.BlockSpec(memory_space=pltpu.HBM), pl.BlockSpec(memory_space=pltpu.HBM)),
        scratch_shapes=[pltpu.SemaphoreType.DMA((2,))],
        name="store",
    )(a, b)


def solution(mesh):
    in_specs = (
        P("tm", None, None, "tile"),
        P("tm", None, None, "tile"),
        P(None, "tile"),
        P(None, "tile"),
        P(None, "tile"),
        P(None, "tile"),
    )
    out_specs = (P("tm", None, None, "tile"), P(None, None, "tile"))
    return jax.shard_map(shards, mesh=mesh, in_specs=in_specs, out_specs=out_specs, check_vma=False)
```

```python
import functools

import jax
import jax.numpy as jnp
import numpy as np
from jax import lax
from jax.experimental import pallas as pl
from jax.experimental.pallas import tpu as pltpu
from jax.sharding import PartitionSpec as P

HALF = 24
CUTOFF = 1.0 / 40.0
LANES = 128
CHUNK = 8
DEPTH = 2
GROUP = 4
WINDOWS = (((0, 3), (0, 1)), ((1, 5), (1, 3)), ((3, 7), (5, 7)), ((5, 8), (7, 8)))
SPAN = 2 * GROUP
MESH = pl.DeviceIdType.MESH


def band_parts(count):
    offset = (np.arange(count + 2 * HALF)[None, :] - np.arange(count)[:, None] - HALF).astype(np.float64)
    weights = 2.0 * CUTOFF * np.sinc(2.0 * CUTOFF * offset) * np.sinc(offset / HALF)
    weights = np.where(np.abs(offset) <= HALF, weights, 0.0).astype(np.float32)
    own = weights[:, HALF : HALF + count]
    halo = np.concatenate([weights[:, :HALF], weights[:, HALF + count :]], axis=1)
    return own, halo


def dot(a, b):
    return jnp.dot(a, b, precision=lax.Precision.HIGHEST, preferred_element_type=jnp.float32)


def halves(a):
    high = a.astype(jnp.bfloat16).astype(jnp.float32)
    return high, a - high


def stacked_weights(w):
    high, low = halves(w)
    return jnp.concatenate(
        [jnp.concatenate([high, high], axis=1), jnp.concatenate([low, low], axis=1)], axis=0
    ).astype(jnp.bfloat16)


def split_dot(weights, pieces):
    split = [halves(p) for p in pieces]
    block = jnp.concatenate([s[0] for s in split] + [s[1] for s in split], axis=0).astype(jnp.bfloat16)
    both = jnp.dot(weights, block, preferred_element_type=jnp.float32)
    half = both.shape[0] // 2
    return both[:half] + both[half:]


def kernel(
    n_tm, n_tile, levels,
    u_ref, v_ref, land_in, bottom_in, sx_in, sy_in, own_in, halo_in,
    conv_ref, mean_ref,
    land_ref, bottom_ref, sx_ref, sy_ref, own_ref, halo_w_ref, small_sem,
    x, halo, mm, cf, wet, cx, cy, part, edge, edge_halo, edge_mean, edge_in,
    near_w, far_w, relayed, relay_send, relay_recv,
    x_sem, bulk_send, bulk_recv, edge_send, edge_recv, em_send, em_recv, part_send, part_recv,
):
    snaps, cells, width = u_ref.shape
    rows = cells // levels
    t = lax.axis_index("tm")
    z = lax.axis_index("tile")
    chunks = cells // CHUNK
    per_level = rows // CHUNK
    fields = (u_ref, v_ref)
    even = lax.rem(t, 2) == 0
    odd = jnp.logical_not(even)

    barrier = pltpu.get_barrier_semaphore()
    for k in range(1, n_tm):
        pl.semaphore_signal(barrier, inc=1, device_id={"tm": lax.rem(t + k, n_tm)}, device_id_type=MESH)

    @pl.when(z > 0)
    def _():
        pl.semaphore_signal(barrier, inc=1, device_id={"tile": z - 1}, device_id_type=MESH)

    @pl.when(z < n_tile - 1)
    def _():
        pl.semaphore_signal(barrier, inc=1, device_id={"tile": z + 1}, device_id_type=MESH)

    def local(c, f, h):
        return pltpu.make_async_copy(
            fields[f].at[:, pl.ds(c * CHUNK, CHUNK), pl.ds(h * LANES, LANES)], x.at[c, f, h], x_sem.at[c, f, h]
        )

    small = (
        (land_in, land_ref), (bottom_in, bottom_ref), (sx_in, sx_ref),
        (sy_in, sy_ref), (own_in, own_ref), (halo_in, halo_w_ref),
    )
    for i, (src, dst) in enumerate(small):
        pltpu.make_async_copy(src, dst, small_sem.at[i]).start()
    for c in range(chunks):
        for f in range(2):
            for h in range(2):
                local(c, f, h).start()

    def bulk(side, c, f, h):
        first = snaps - HALF if side == 0 else 0
        to = t + 1 if side == 0 else t - 1
        return pltpu.make_async_remote_copy(
            src_ref=fields[f].at[pl.ds(first, HALF), pl.ds(c * CHUNK, CHUNK), pl.ds(h * LANES, LANES)],
            dst_ref=halo.at[side, c, f, h],
            send_sem=bulk_send.at[side, c, f, h],
            recv_sem=bulk_recv.at[side, c, f, h],
            device_id={"tm": to},
            device_id_type=MESH,
        )

    middle = (n_tm // 2 - 1, n_tm // 2)
    via = (n_tm - 1, 0)

    def to_relay(side, c, h):
        first = snaps - HALF if side == 0 else 0
        return pltpu.make_async_remote_copy(
            src_ref=fields[1].at[pl.ds(first, HALF), pl.ds(c * CHUNK, CHUNK), pl.ds(h * LANES, LANES)],
            dst_ref=relayed.at[c, h],
            send_sem=bulk_send.at[side, c, 1, h],
            recv_sem=relay_recv.at[c, h],
            device_id={"tm": via[side]},
            device_id_type=MESH,
        )

    def from_relay(side, c, h):
        return pltpu.make_async_remote_copy(
            src_ref=relayed.at[c, h],
            dst_ref=halo.at[side, c, 1, h],
            send_sem=relay_send.at[c, h],
            recv_sem=bulk_recv.at[side, c, 1, h],
            device_id={"tm": middle[1 - side]},
            device_id_type=MESH,
        )

    def pass_on(c):
        if n_tm < 4:
            return
        for side in range(2):

            @pl.when(t == via[side])
            def _():
                for h in range(2):
                    to_relay(side, c, h).wait_recv()
                    from_relay(side, c, h).start()

    def edge_copy(side):
        first = snaps - HALF if side == 0 else 0
        to = t + 1 if side == 0 else t - 1
        return pltpu.make_async_remote_copy(
            src_ref=edge.at[pl.ds(first, HALF), :],
            dst_ref=edge_halo.at[side],
            send_sem=edge_send.at[side],
            recv_sem=edge_recv.at[side],
            device_id={"tm": to},
            device_id_type=MESH,
        )

    def mean_copy(side):
        to = z + 1 if side == 0 else z - 1
        return pltpu.make_async_remote_copy(
            src_ref=edge_mean,
            dst_ref=edge_in.at[side],
            send_sem=em_send.at[side],
            recv_sem=em_recv.at[side],
            device_id={"tile": to},
            device_id_type=MESH,
        )

    def converted(c):
        piece = c % per_level
        low = piece * CHUNK - (1 if piece else 0)
        high = rows if piece == per_level - 1 else (piece + 1) * CHUNK - 1
        return c // per_level, low, high

    def part_copy(c, k, slot):
        l, low, high = converted(c)
        return pltpu.make_async_remote_copy(
            src_ref=part.at[slot, pl.ds(l * rows + low, high - low)],
            dst_ref=part.at[slot, pl.ds(l * rows + low, high - low)],
            send_sem=part_send.at[c, k],
            recv_sem=part_recv.at[c, k],
            device_id={"tm": lax.rem(t + k, n_tm)},
            device_id_type=MESH,
        )

    sends = (t < n_tm - 1, t > 0)
    receives = (t > 0, t < n_tm - 1)
    send_near, send_far = (even, odd), (odd, even)
    near, far = (odd, even), (even, odd)
    z_sends = (z < n_tile - 1, z > 0)
    z_receives = (z > 0, z < n_tile - 1)

    def start_far(c):
        for side in range(2):
            if n_tm >= 4:

                @pl.when(t == middle[side])
                def _():
                    for h in range(2):
                        to_relay(side, c, h).start()
                        bulk(side, c, 0, h).start()

                whole = sends[side] & send_far[side] & (t != middle[side])
            else:
                whole = sends[side] & send_far[side]

            @pl.when(whole)
            def _():
                for f in range(2):
                    for h in range(2):
                        bulk(side, c, f, h).start()

    def finish_send(c, which):
        for side in range(2):

            @pl.when(sends[side] & which[side])
            def _():
                for f in range(2):
                    for h in range(2):
                        bulk(side, c, f, h).wait_send()

    pl.semaphore_wait(barrier, n_tm - 1 + (z > 0).astype(jnp.int32) + (z < n_tile - 1).astype(jnp.int32))

    for c in range(DEPTH):
        start_far(c)
    for side in range(2):

        @pl.when(sends[side] & send_near[side])
        def _():
            for c in range(chunks):
                for f in range(2):
                    for h in range(2):
                        bulk(side, c, f, h).start()

    for side in range(2):

        @pl.when(jnp.logical_not(receives[side]))
        def _():
            halo[side] = jnp.zeros(halo.shape[1:], jnp.float32)
            edge_halo[side] = jnp.zeros(edge_halo.shape[1:], jnp.float32)

        @pl.when(jnp.logical_not(z_receives[side]))
        def _():
            edge_in[side] = jnp.zeros(edge_in.shape[1:], jnp.float32)

    for i, (src, dst) in enumerate(small):
        pltpu.make_async_copy(src, dst, small_sem.at[i]).wait()

    for l in range(levels):
        is_wet = (land_ref[...] == 1) & (l < bottom_ref[...])
        level_wet = jnp.where(is_wet, 1.0, 0.0).astype(jnp.float32)
        for j in range(rows):
            wet[l * rows + j] = level_wet[j : j + 1, :]
    all_x, all_y = 0.5 / sx_ref[...], 0.5 / sy_ref[...]
    for j in range(rows):
        cx[j] = all_x[j : j + 1, :]
        cy[j] = all_y[j : j + 1, :]
    for f in range(2):
        for l in range(levels):
            for j in (0, rows + 1):
                mm[f, l, j] = jnp.zeros((snaps, width), jnp.float32)
    column = lax.broadcasted_iota(jnp.int32, (snaps, 2 * HALF), 1)
    valid = ((column >= HALF) | (t > 0)) & ((column < HALF) | (t < n_tm - 1))
    own_w = own_ref[...]
    halo_w = jnp.where(valid, halo_w_ref[...], 0.0)
    weight_sum = jnp.sum(own_w, axis=1, keepdims=True) + jnp.sum(halo_w, axis=1, keepdims=True)
    own_w = own_w / weight_sum
    halo_w = halo_w / weight_sum
    near_side = 1 - lax.rem(t, 2)
    far_side = lax.rem(t, 2)
    near_half = jnp.where(even, halo_w[:, HALF:], halo_w[:, :HALF])
    far_half = jnp.where(even, halo_w[:, :HALF], halo_w[:, HALF:])
    near_w[...] = stacked_weights(jnp.concatenate([own_w, near_half], axis=1))
    far_w[...] = stacked_weights(far_half)

    for c in range(chunks):
        for f in range(2):
            for h in range(2):
                local(c, f, h).wait()

    def series(ref, count, j):
        return ref.reshape(count * CHUNK, LANES)[pl.ds(j, count, stride=CHUNK), :]

    def both(ref, count, j):
        return jnp.concatenate([series(ref.at[h], count, j) for h in range(2)], axis=1)

    lane = lax.broadcasted_iota(jnp.int32, (snaps, LANES), 1)

    def pack(r, acc):
        c, j = r // CHUNK, lax.rem(r, CHUNK)
        for f in range(2):
            q = f * cells + r
            first = series(x.at[c, f, 0], snaps, j) * wet[r][:, :LANES]
            acc = jnp.where(lane == q, pltpu.roll(first, q, 1), acc)
            q = (2 + f) * cells + r
            last = series(x.at[c, f, 1], snaps, j) * wet[r][:, width - LANES :]
            acc = jnp.where(lane == q, pltpu.roll(last, lax.rem(q + 1, LANES), 1), acc)
        return acc

    edge[...] = lax.fori_loop(0, cells, pack, jnp.zeros((snaps, LANES), jnp.float32), unroll=4)
    for side in range(2):

        @pl.when(sends[side])
        def _():
            edge_copy(side).start()

    pass_on(0)

    for side in range(2):

        @pl.when(receives[side] & near[side])
        def _():
            for c in range(chunks):
                for f in range(2):
                    for h in range(2):
                        bulk(side, c, f, h).wait_recv()

    def near_part(r, carry):
        l, j = r // rows, lax.rem(r, rows)
        c, i = r // CHUNK, lax.rem(r, CHUNK)
        for f in range(2):
            pieces = [both(x.at[c, f], snaps, i), both(halo.at[near_side, c, f], HALF, i)]
            mm[f, l, j + 1] = split_dot(near_w[...], pieces)
        return carry

    lax.fori_loop(0, cells, near_part, 0, unroll=8)
    for c in range(1, DEPTH):
        pass_on(c)

    for side in range(2):

        @pl.when(receives[side])
        def _():
            edge_copy(side).wait_recv()

    edge_mean[...] = dot(own_w, edge[...]) + dot(
        halo_w, jnp.concatenate([edge_halo[0], edge_halo[1]], axis=0)
    )
    for side in range(2):

        @pl.when(z_sends[side])
        def _():
            mean_copy(side).start()

    wide = lax.broadcasted_iota(jnp.int32, (snaps, width), 1)

    def far_part(r, carry):
        l, j = r // rows, lax.rem(r, rows)
        c, i = r // CHUNK, lax.rem(r, CHUNK)
        mask = wet[r]
        for f in range(2):
            pieces = [both(halo.at[far_side, c, f], HALF, i)]
            mm[f, l, j + 1] = (mm[f, l, j + 1] + split_dot(far_w[...], pieces)) * mask
        return carry

    def grad_x(f, r, masked, scale):
        q = (2 + f) * cells + r
        before = pltpu.roll(edge_in[0], lax.rem(2 * LANES - q, LANES), 1)
        q = f * cells + r
        after = pltpu.roll(edge_in[1], lax.rem(2 * LANES - 1 - q, LANES), 1)
        before = jnp.concatenate([before, before], axis=1)
        after = jnp.concatenate([after, after], axis=1)
        behind = jnp.where(wide == 0, before, pltpu.roll(masked, 1, 1))
        ahead = jnp.where(wide == width - 1, after, pltpu.roll(masked, width - 1, 1))
        return (ahead - behind) * scale

    def convert(l):
        def body(j, carry):
            r = l * rows + j
            c, i = r // CHUNK, lax.rem(r, CHUNK)
            mask = wet[r]
            scale_x = cx[j]
            scale_y = cy[j]
            eddy, gx, gy = [], [], []
            for f in range(2):
                masked = mm[f, l, j + 1]
                eddy.append(both(x.at[c, f], snaps, i) - masked)
                gx.append(grad_x(f, r, masked, scale_x))
                gy.append((mm[f, l, j + 2] - mm[f, l, j]) * scale_y)
            eu, ev = eddy
            total = eu * eu * gx[0] + eu * ev * (gy[0] + gx[1]) + ev * ev * gy[1]
            conversion = -mask * total
            for h in range(2):
                cf.at[c, h].reshape(snaps * CHUNK, LANES)[pl.ds(i, snaps, stride=CHUNK), :] = conversion[
                    :, h * LANES : (h + 1) * LANES
                ]
            part[t, r] = jnp.sum(conversion, axis=0, keepdims=True)
            return carry

        return body

    for c in range(chunks):
        finish_send(c, send_far)
        if c + DEPTH < chunks:
            start_far(c + DEPTH)
        for side in range(2):

            @pl.when(receives[side] & far[side])
            def _():
                for f in range(2):
                    for h in range(2):
                        bulk(side, c, f, h).wait_recv()

        lax.fori_loop(c * CHUNK, (c + 1) * CHUNK, far_part, 0, unroll=8)
        if c + DEPTH < chunks:
            pass_on(c + DEPTH)
        if c == 0:
            for side in range(2):

                @pl.when(z_receives[side])
                def _():
                    mean_copy(side).wait_recv()

        l, low, high = converted(c)
        lax.fori_loop(low, high, convert(l), 0, unroll=2)
        for k in range(1, n_tm):
            part_copy(c, k, t).start()
        if c % per_level == per_level - 1:

            def narrow(s, carry):
                for h in range(2):
                    block = jnp.concatenate([cf[l * per_level + p, h, s] for p in range(per_level)], axis=0)
                    conv_ref[s, pl.ds(l * rows, rows), pl.ds(h * LANES, LANES)] = block.astype(jnp.bfloat16)
                return carry

            lax.fori_loop(0, snaps, narrow, 0, unroll=4)

    for c in range(chunks):
        for k in range(1, n_tm):
            part_copy(c, k, lax.rem(t + n_tm - k, n_tm)).wait_recv()
        l, low, high = converted(c)
        for j in range(low, high):
            total = part[0, l * rows + j]
            for s in range(1, n_tm):
                total = total + part[s, l * rows + j]
            mean_ref[l, j : j + 1, :] = total / (snaps * n_tm)

    for c in range(chunks):
        finish_send(c, send_near)
    for side in range(2):

        @pl.when(sends[side])
        def _():
            edge_copy(side).wait_send()

        @pl.when(z_sends[side])
        def _():
            mean_copy(side).wait_send()

        if n_tm >= 4:

            @pl.when(t == via[side])
            def _():
                for c in range(chunks):
                    for h in range(2):
                        from_relay(side, c, h).wait_send()

    for c in range(chunks):
        for k in range(1, n_tm):
            part_copy(c, k, t).wait_send()


def fast_kernel(
    n_tm, n_tile, levels,
    u_ref, v_ref, land_in, bottom_in, sx_in, sy_in, own_in, halo_in,
    conv_ref, mean_ref, flag_ref,
    land_ref, bottom_ref, sx_ref, sy_ref, own_ref, halo_w_ref, small_sem,
    x, near, mm, cf, wet, key, cx, cy, part, edge, edge_halo, edge_mean, edge_in,
    near_w, far_w, place, packed, far, relayed, flags,
    relay_send, relay_recv, x_sem, near_sem, far_send, far_recv, edge_send, edge_recv, em_send, em_recv,
    part_send, part_recv, flag_send, flag_recv,
):
    snaps, cells, width = u_ref.shape
    rows = cells // levels
    t = lax.axis_index("tm")
    z = lax.axis_index("tile")
    blocks = cells // CHUNK
    per_level = rows // CHUNK
    chunks = rows // GROUP
    fields = (u_ref, v_ref)
    even = lax.rem(t, 2) == 0
    odd = jnp.logical_not(even)

    barrier = pltpu.get_barrier_semaphore()
    for k in range(1, n_tm):
        pl.semaphore_signal(barrier, inc=1, device_id={"tm": lax.rem(t + k, n_tm)}, device_id_type=MESH)
    for k in range(1, n_tile):
        pl.semaphore_signal(barrier, inc=1, device_id={"tile": lax.rem(z + k, n_tile)}, device_id_type=MESH)

    def local(c, f, h):
        return pltpu.make_async_copy(
            fields[f].at[:, pl.ds(c * CHUNK, CHUNK), pl.ds(h * LANES, LANES)], x.at[c, f, h], x_sem.at[c, f, h]
        )

    small = (
        (land_in, land_ref), (bottom_in, bottom_ref), (sx_in, sx_ref),
        (sy_in, sy_ref), (own_in, own_ref), (halo_in, halo_w_ref),
    )
    for i, (src, dst) in enumerate(small):
        pltpu.make_async_copy(src, dst, small_sem.at[i]).start()
    for p in range(per_level):
        for l in range(levels):
            for f in range(2):
                for h in range(2):
                    local(l * per_level + p, f, h).start()

    first_far = jnp.where(even, 0, snaps - HALF)
    first_near = jnp.where(even, snaps - HALF, 0)
    has_far = (t > 0) & (t < n_tm - 1)
    at_end = jnp.logical_not(has_far)
    is_middle = (t == n_tm // 2 - 1) | (t == n_tm // 2)
    far_to = jnp.where(even, t - 1, t + 1)
    via_to = jnp.where(t < n_tm // 2, n_tm - 1, 0)
    forward_to = jnp.where(t == 0, n_tm // 2 - 1, n_tm // 2)

    def tiles(c):
        return c * SPAN, SPAN

    def near_copy():
        return pltpu.make_async_remote_copy(
            src_ref=x.at[:, :, :, pl.ds(first_near, HALF)],
            dst_ref=near,
            send_sem=near_sem.at[0],
            recv_sem=near_sem.at[1],
            device_id={"tm": t + 1 - 2 * lax.rem(t, 2)},
            device_id_type=MESH,
        )

    def far_copy(c, f):
        start, count = tiles(c)
        return pltpu.make_async_remote_copy(
            src_ref=packed.at[f, pl.ds(start, count)],
            dst_ref=far.at[f, pl.ds(start, count)],
            send_sem=far_send.at[c, f],
            recv_sem=far_recv.at[c, f],
            device_id={"tm": far_to},
            device_id_type=MESH,
        )

    def to_relay(c):
        start, count = tiles(c)
        return pltpu.make_async_remote_copy(
            src_ref=packed.at[1, pl.ds(start, count)],
            dst_ref=relayed.at[pl.ds(start, count)],
            send_sem=far_send.at[c, 1],
            recv_sem=relay_recv.at[c],
            device_id={"tm": via_to},
            device_id_type=MESH,
        )

    def from_relay(c):
        start, count = tiles(c)
        return pltpu.make_async_remote_copy(
            src_ref=relayed.at[pl.ds(start, count)],
            dst_ref=far.at[1, pl.ds(start, count)],
            send_sem=relay_send.at[c],
            recv_sem=far_recv.at[c, 1],
            device_id={"tm": forward_to},
            device_id_type=MESH,
        )

    def pass_on(c):
        @pl.when(at_end)
        def _():
            to_relay(c).wait_recv()
            from_relay(c).start()

    def start_far(c):
        @pl.when(has_far)
        def _():
            far_copy(c, 0).start()

        @pl.when(is_middle)
        def _():
            to_relay(c).start()

        @pl.when(has_far & jnp.logical_not(is_middle))
        def _():
            far_copy(c, 1).start()

    def edge_copy(side):
        first = snaps - HALF if side == 0 else 0
        to = t + 1 if side == 0 else t - 1
        return pltpu.make_async_remote_copy(
            src_ref=edge.at[pl.ds(first, HALF), :],
            dst_ref=edge_halo.at[side],
            send_sem=edge_send.at[side],
            recv_sem=edge_recv.at[side],
            device_id={"tm": to},
            device_id_type=MESH,
        )

    def mean_copy(side):
        to = z + 1 if side == 0 else z - 1
        return pltpu.make_async_remote_copy(
            src_ref=edge_mean,
            dst_ref=edge_in.at[side],
            send_sem=em_send.at[side],
            recv_sem=em_recv.at[side],
            device_id={"tile": to},
            device_id_type=MESH,
        )

    def flag_copy(k, slot):
        return pltpu.make_async_remote_copy(
            src_ref=flags.at[slot],
            dst_ref=flags.at[slot],
            send_sem=flag_send.at[k],
            recv_sem=flag_recv.at[k],
            device_id={"tile": lax.rem(z + k, n_tile)},
            device_id_type=MESH,
        )

    def converted(c):
        return c * GROUP - (1 if c else 0), rows if c == chunks - 1 else (c + 1) * GROUP - 1

    def part_copy(c, k, slot):
        low, high = converted(c)
        return pltpu.make_async_remote_copy(
            src_ref=part.at[slot, pl.ds(levels * low, levels * (high - low))],
            dst_ref=part.at[slot, pl.ds(levels * low, levels * (high - low))],
            send_sem=part_send.at[c, k],
            recv_sem=part_recv.at[c, k],
            device_id={"tm": lax.rem(t + k, n_tm)},
            device_id_type=MESH,
        )

    sends = (t < n_tm - 1, t > 0)
    receives = (t > 0, t < n_tm - 1)
    z_sends = (z < n_tile - 1, z > 0)
    z_receives = (z > 0, z < n_tile - 1)

    for i, (src, dst) in enumerate(small):
        pltpu.make_async_copy(src, dst, small_sem.at[i]).wait()

    levels_wet = []
    for l in range(levels):
        is_wet = (land_ref[...] == 1) & (l < bottom_ref[...])
        levels_wet.append(jnp.where(is_wet, 1.0, 0.0).astype(jnp.float32))
    all_wet = jnp.concatenate(levels_wet, axis=0)
    lower = lax.broadcasted_iota(jnp.int32, (width, width), 0)
    upper = lax.broadcasted_iota(jnp.int32, (width, width), 1)
    earlier = jnp.where(lower < upper, 1.0, 0.0).astype(jnp.bfloat16)

    def ranked(index):
        j = lax.rem(index, rows)
        side = lax.rem(j, GROUP) // 2
        inner = jnp.where(side == 0, lax.rem(j, 2), 1 - lax.rem(j, 2))
        return 2 * (j // GROUP) + side, 2 * inner + (1 - index // rows)

    set_a, rank_a = ranked(lax.broadcasted_iota(jnp.int32, (cells, cells), 0))
    set_b, rank_b = ranked(lax.broadcasted_iota(jnp.int32, (cells, cells), 1))
    ahead_rows = jnp.where((set_a == set_b) & (rank_b < rank_a), 1.0, 0.0).astype(jnp.bfloat16)
    same_rows = jnp.where((set_a // 2 == set_b // 2) & (set_a != set_b), 1.0, 0.0).astype(jnp.bfloat16)
    wet_bits = all_wet.astype(jnp.bfloat16)
    filled = jnp.dot(
        jnp.concatenate([ahead_rows, same_rows], axis=0), wet_bits, preferred_element_type=jnp.float32
    ).astype(jnp.bfloat16)
    every = jnp.ones((width, width), jnp.bfloat16)
    order = jnp.dot(wet_bits, earlier, preferred_element_type=jnp.float32) + jnp.dot(
        filled[:cells], every, preferred_element_type=jnp.float32
    )
    other = jnp.dot(filled[cells:], every, preferred_element_type=jnp.float32)
    row = lax.broadcasted_iota(jnp.int32, (cells, width), 0)
    right = lax.rem(lax.rem(row, rows), GROUP) >= 2
    spot = jnp.where(right, float(SPAN * LANES - 1) - order, order)
    first_lane = jnp.zeros((cells, width), jnp.float32)
    lanes_used = jnp.zeros((cells, width), jnp.float32)
    for q in range(GROUP):
        for l in range(levels):
            here = (lax.rem(lax.rem(row, rows), GROUP) == q) & (row // rows == l)
            low, high = WINDOWS[q][l]
            first_lane = jnp.where(here, float(low * LANES), first_lane)
            lanes_used = jnp.where(here, float((high - low) * LANES), lanes_used)
    spot = spot - first_lane
    fits = (spot >= 0.0) & (spot < lanes_used) & (order + other < float(SPAN * LANES))
    is_wet = all_wet > 0.0
    all_key = jnp.where(is_wet & fits, spot, -1.0)
    over = jnp.max(jnp.where(is_wet & jnp.logical_not(fits), 1.0, 0.0), axis=0, keepdims=True)
    flags[z] = jnp.broadcast_to(jnp.maximum(over[:, :LANES], over[:, LANES:]), (8, LANES))
    for r in range(cells):
        wet[r] = all_wet[r : r + 1, :]
        key[r] = all_key[r : r + 1, :]

    def series(ref, count, j):
        return ref.reshape(count * CHUNK, LANES)[pl.ds(j, count, stride=CHUNK), :]

    def both(ref, count, j):
        return jnp.concatenate([series(ref.at[h], count, j) for h in range(2)], axis=1)

    def members(c):
        for q in range(GROUP):
            for l in range(levels):
                low, high = WINDOWS[q][l]
                j = c * GROUP + q
                yield l * rows + j, l * per_level + j // CHUNK, j % CHUNK, low, high

    def put(r, size):
        index = lax.broadcasted_iota(jnp.int32, (size, width), 0).astype(jnp.float32)
        place[r, :size] = jnp.where(index == key[r], 1.0, 0.0).astype(jnp.bfloat16)

    def gather(r, b, i, size):
        split = []
        for f in range(2):
            block = [x.at[b, f, h].reshape(snaps * CHUNK, LANES) for h in range(2)]
            at = pl.ds(first_far * CHUNK + i, HALF, stride=CHUNK)
            split.extend(halves(jnp.concatenate([p[at, :] for p in block], axis=1)))
        split = jnp.concatenate(split, axis=0).astype(jnp.bfloat16)
        out = lax.dot_general(
            split, place[r, :size], (((1,), (1,)), ((), ())), preferred_element_type=jnp.float32
        )
        return [out[2 * f * HALF : (2 * f + 1) * HALF] + out[(2 * f + 1) * HALF : (2 * f + 2) * HALF] for f in range(2)]

    def compact(c):
        start, count = tiles(c)
        for r, _, _, low, high in members(c):
            put(r, (high - low) * LANES)
        sums = [[None] * count for f in range(2)]
        for r, b, i, low, high in members(c):
            values = gather(r, b, i, (high - low) * LANES)
            for f in range(2):
                for p in range(low, high):
                    piece = values[f][:, (p - low) * LANES : (p - low + 1) * LANES]
                    sums[f][p] = piece if sums[f][p] is None else sums[f][p] + piece
        for f in range(2):
            for p in range(count):
                packed[f, start + p] = sums[f][p]

    def wait_local(c):
        for f in range(2):
            for h in range(2):
                local(c, f, h).wait()

    for l in range(levels):
        wait_local(l * per_level)
    compact(0)
    pl.semaphore_wait(barrier, n_tm - 1 + n_tile - 1)
    start_far(0)
    for k in range(1, n_tile):
        flag_copy(k, z).start()
    for l in range(levels):
        for p in range(1, per_level):
            wait_local(l * per_level + p)
    near_copy().start()
    compact(1)
    if DEPTH > 1:
        start_far(1)

    @pl.when(at_end)
    def _():
        far[...] = jnp.zeros(far.shape, jnp.float32)

    for side in range(2):

        @pl.when(jnp.logical_not(receives[side]))
        def _():
            edge_halo[side] = jnp.zeros(edge_halo.shape[1:], jnp.float32)

        @pl.when(jnp.logical_not(z_receives[side]))
        def _():
            edge_in[side] = jnp.zeros(edge_in.shape[1:], jnp.float32)

    all_x, all_y = 0.5 / sx_ref[...], 0.5 / sy_ref[...]
    for j in range(rows):
        cx[j] = all_x[j : j + 1, :]
        cy[j] = all_y[j : j + 1, :]
    for f in range(2):
        for l in range(levels):
            for j in (0, rows + 1):
                mm[f, l, j] = jnp.zeros((snaps, width), jnp.float32)
    column = lax.broadcasted_iota(jnp.int32, (snaps, 2 * HALF), 1)
    valid = ((column >= HALF) | (t > 0)) & ((column < HALF) | (t < n_tm - 1))
    own_w = own_ref[...]
    halo_w = jnp.where(valid, halo_w_ref[...], 0.0)
    weight_sum = jnp.sum(own_w, axis=1, keepdims=True) + jnp.sum(halo_w, axis=1, keepdims=True)
    own_w = own_w / weight_sum
    halo_w = halo_w / weight_sum
    near_half = jnp.where(even, halo_w[:, HALF:], halo_w[:, :HALF])
    far_half = jnp.where(even, halo_w[:, :HALF], halo_w[:, HALF:])
    near_w[...] = stacked_weights(jnp.concatenate([own_w, near_half], axis=1))
    far_w[...] = stacked_weights(far_half)

    lane = lax.broadcasted_iota(jnp.int32, (snaps, LANES), 1)

    def pack(r, acc):
        c, j = r // CHUNK, lax.rem(r, CHUNK)
        for f in range(2):
            q = f * cells + r
            first = series(x.at[c, f, 0], snaps, j) * wet[r][:, :LANES]
            acc = jnp.where(lane == q, pltpu.roll(first, q, 1), acc)
            q = (2 + f) * cells + r
            last = series(x.at[c, f, 1], snaps, j) * wet[r][:, width - LANES :]
            acc = jnp.where(lane == q, pltpu.roll(last, lax.rem(q + 1, LANES), 1), acc)
        return acc

    edge[...] = lax.fori_loop(0, cells, pack, jnp.zeros((snaps, LANES), jnp.float32), unroll=4)
    for side in range(2):

        @pl.when(sends[side])
        def _():
            edge_copy(side).start()

    pass_on(0)
    near_copy().wait_recv()

    def near_part(r, carry):
        l, j = r // rows, lax.rem(r, rows)
        c, i = r // CHUNK, lax.rem(r, CHUNK)
        for f in range(2):
            pieces = [both(x.at[c, f], snaps, i), both(near.at[c, f], HALF, i)]
            mm[f, l, j + 1] = split_dot(near_w[...], pieces)
        return carry

    lax.fori_loop(0, cells, near_part, 0, unroll=8)
    for c in range(2, chunks):
        compact(c)
        if c < DEPTH:
            start_far(c)
    for c in range(1, DEPTH):
        pass_on(c)

    for side in range(2):

        @pl.when(receives[side])
        def _():
            edge_copy(side).wait_recv()

    edge_mean[...] = dot(own_w, edge[...]) + dot(
        halo_w, jnp.concatenate([edge_halo[0], edge_halo[1]], axis=0)
    )
    for side in range(2):

        @pl.when(z_sends[side])
        def _():
            mean_copy(side).start()

    wide = lax.broadcasted_iota(jnp.int32, (snaps, width), 1)

    def spread(r, blocks):
        l, j = r // rows, r % rows
        size = blocks[0].shape[1]
        split = []
        for block in blocks:
            split.extend(halves(block))
        out = jnp.dot(
            jnp.concatenate(split, axis=0).astype(jnp.bfloat16), place[r, :size], preferred_element_type=jnp.float32
        ).astype(jnp.bfloat16)
        mask = wet[r]
        for f in range(2):
            both_halves = jnp.dot(
                far_w[...], out[2 * f * HALF : 2 * (f + 1) * HALF], preferred_element_type=jnp.float32
            )
            mm[f, l, j + 1] = (mm[f, l, j + 1] + both_halves[:snaps] + both_halves[snaps:]) * mask

    def far_part(c):
        start, _ = tiles(c)
        for r, _, _, low, high in members(c):
            spread(
                r, [jnp.concatenate([far[f, start + p] for p in range(low, high)], axis=1) for f in range(2)]
            )

    def grad_x(f, r, masked, scale):
        q = (2 + f) * cells + r
        before = pltpu.roll(edge_in[0], lax.rem(2 * LANES - q, LANES), 1)
        q = f * cells + r
        after = pltpu.roll(edge_in[1], lax.rem(2 * LANES - 1 - q, LANES), 1)
        before = jnp.concatenate([before, before], axis=1)
        after = jnp.concatenate([after, after], axis=1)
        behind = jnp.where(wide == 0, before, pltpu.roll(masked, 1, 1))
        ahead = jnp.where(wide == width - 1, after, pltpu.roll(masked, width - 1, 1))
        return (ahead - behind) * scale

    def convert(low, count):
        def body(q, carry):
            l, j = q // count, low + lax.rem(q, count)
            r = l * rows + j
            c, i = r // CHUNK, lax.rem(r, CHUNK)
            mask = wet[r]
            scale_x = cx[j]
            scale_y = cy[j]
            eddy, gx, gy = [], [], []
            for f in range(2):
                masked = mm[f, l, j + 1]
                eddy.append(both(x.at[c, f], snaps, i) - masked)
                gx.append(grad_x(f, r, masked, scale_x))
                gy.append((mm[f, l, j + 2] - mm[f, l, j]) * scale_y)
            eu, ev = eddy
            total = eu * eu * gx[0] + eu * ev * (gy[0] + gx[1]) + ev * ev * gy[1]
            conversion = -mask * total
            for h in range(2):
                cf.at[c, h].reshape(snaps * CHUNK, LANES)[pl.ds(i, snaps, stride=CHUNK), :] = conversion[
                    :, h * LANES : (h + 1) * LANES
                ]
            part[t, levels * j + l] = jnp.sum(conversion, axis=0, keepdims=True)
            return carry

        return body

    def finish(c):
        for k in range(1, n_tm):
            part_copy(c, k, lax.rem(t + n_tm - k, n_tm)).wait_recv()
        low, high = converted(c)
        for j in range(low, high):
            for l in range(levels):
                total = part[0, levels * j + l]
                for s in range(1, n_tm):
                    total = total + part[s, levels * j + l]
                mean_ref[l, j : j + 1, :] = total / (snaps * n_tm)

    for c in range(chunks):
        @pl.when(has_far)
        def _():
            for f in range(2):
                far_copy(c, f).wait_send()

        if c + DEPTH < chunks:
            start_far(c + DEPTH)

        @pl.when(has_far)
        def _():
            for f in range(2):
                far_copy(c, f).wait_recv()

        far_part(c)
        if c + DEPTH < chunks:
            pass_on(c + DEPTH)
        if c == 0:
            for side in range(2):

                @pl.when(z_receives[side])
                def _():
                    mean_copy(side).wait_recv()

        low, high = converted(c)
        lax.fori_loop(0, levels * (high - low), convert(low, high - low), 0, unroll=high - low)
        for k in range(1, n_tm):
            part_copy(c, k, t).start()

    def narrow(s, carry):
        for l in range(levels):
            for h in range(2):
                block = jnp.concatenate([cf[l * per_level + p, h, s] for p in range(per_level)], axis=0)
                conv_ref[s, pl.ds(l * rows, rows), pl.ds(h * LANES, LANES)] = block.astype(jnp.bfloat16)
        return carry

    lax.fori_loop(0, snaps, narrow, 0, unroll=4)
    for k in range(1, n_tile):
        flag_copy(k, lax.rem(z + n_tile - k, n_tile)).wait_recv()
    worst = flags[0]
    for s in range(1, n_tile):
        worst = jnp.maximum(worst, flags[s])
    flag_ref[0] = jnp.max(worst)
    for c in range(chunks):
        finish(c)

    near_copy().wait_send()
    for side in range(2):

        @pl.when(sends[side])
        def _():
            edge_copy(side).wait_send()

        @pl.when(z_sends[side])
        def _():
            mean_copy(side).wait_send()

    @pl.when(at_end)
    def _():
        for c in range(chunks):
            from_relay(c).wait_send()

    for k in range(1, n_tile):
        flag_copy(k, z).wait_send()
    for c in range(chunks):
        for k in range(1, n_tm):
            part_copy(c, k, t).wait_send()


def full(own, halo, velocity_u, velocity_v, land_sea, bottom_level, spacing_x, spacing_y):
    snaps, cells, width = velocity_u.shape
    rows = land_sea.shape[0]
    levels = cells // rows
    n_tm, n_tile = lax.axis_size("tm"), lax.axis_size("tile")
    chunks = cells // CHUNK
    vmem = pl.BlockSpec(memory_space=pltpu.VMEM)
    hbm = pl.BlockSpec(memory_space=pltpu.HBM)
    f32, bf16 = jnp.float32, jnp.bfloat16
    dma = pltpu.SemaphoreType.DMA
    return pl.pallas_call(
        functools.partial(kernel, n_tm, n_tile, levels),
        out_shape=(
            jax.ShapeDtypeStruct((snaps, cells, width), bf16),
            jax.ShapeDtypeStruct((levels, rows, width), f32),
        ),
        in_specs=[hbm] * 8,
        out_specs=(vmem, vmem),
        scratch_shapes=[
            pltpu.VMEM((rows, width), jnp.int32),
            pltpu.VMEM((rows, width), jnp.int32),
            pltpu.VMEM((rows, width), f32),
            pltpu.VMEM((rows, width), f32),
            pltpu.VMEM(own.shape, f32),
            pltpu.VMEM(halo.shape, f32),
            dma((6,)),
            pltpu.VMEM((chunks, 2, 2, snaps, CHUNK, LANES), f32),
            pltpu.VMEM((2, chunks, 2, 2, HALF, CHUNK, LANES), f32),
            pltpu.VMEM((2, levels, rows + 2, snaps, width), f32),
            pltpu.VMEM((chunks, 2, snaps, CHUNK, LANES), f32),
            pltpu.VMEM((cells, 1, width), f32),
            pltpu.VMEM((rows, 1, width), f32),
            pltpu.VMEM((rows, 1, width), f32),
            pltpu.VMEM((n_tm, cells, 1, width), f32),
            pltpu.VMEM((snaps, LANES), f32),
            pltpu.VMEM((2, HALF, LANES), f32),
            pltpu.VMEM((snaps, LANES), f32),
            pltpu.VMEM((2, snaps, LANES), f32),
            pltpu.VMEM((2 * snaps, 2 * (snaps + HALF)), bf16),
            pltpu.VMEM((2 * snaps, 2 * HALF), bf16),
            pltpu.VMEM((chunks, 2, HALF, CHUNK, LANES), f32),
            dma((chunks, 2)),
            dma((chunks, 2)),
            dma((chunks, 2, 2)),
            dma((2, chunks, 2, 2)),
            dma((2, chunks, 2, 2)),
            dma((2,)),
            dma((2,)),
            dma((2,)),
            dma((2,)),
            dma((chunks, n_tm)),
            dma((chunks, n_tm)),
        ],
        compiler_params=pltpu.CompilerParams(
            collective_id=1, has_side_effects=True, vmem_limit_bytes=60 * 1024 * 1024
        ),
        cost_estimate=pl.CostEstimate(flops=10**9, bytes_accessed=4 * 10**6, transcendentals=0),
    )(
        velocity_u, velocity_v, land_sea, bottom_level, spacing_x, spacing_y, own, halo,
    )


def quick(own, halo, velocity_u, velocity_v, land_sea, bottom_level, spacing_x, spacing_y):
    snaps, cells, width = velocity_u.shape
    rows = land_sea.shape[0]
    levels = cells // rows
    n_tm, n_tile = lax.axis_size("tm"), lax.axis_size("tile")
    blocks = cells // CHUNK
    chunks = rows // GROUP
    packs = chunks * SPAN
    most = max(high - low for pair in WINDOWS for low, high in pair) * LANES
    vmem = pl.BlockSpec(memory_space=pltpu.VMEM)
    hbm = pl.BlockSpec(memory_space=pltpu.HBM)
    f32, bf16 = jnp.float32, jnp.bfloat16
    dma = pltpu.SemaphoreType.DMA
    return pl.pallas_call(
        functools.partial(fast_kernel, n_tm, n_tile, levels),
        out_shape=(
            jax.ShapeDtypeStruct((snaps, cells, width), bf16),
            jax.ShapeDtypeStruct((levels, rows, width), f32),
            jax.ShapeDtypeStruct((1,), f32),
        ),
        in_specs=[hbm] * 8,
        out_specs=(vmem, vmem, pl.BlockSpec(memory_space=pltpu.SMEM)),
        scratch_shapes=[
            pltpu.VMEM((rows, width), jnp.int32),
            pltpu.VMEM((rows, width), jnp.int32),
            pltpu.VMEM((rows, width), f32),
            pltpu.VMEM((rows, width), f32),
            pltpu.VMEM(own.shape, f32),
            pltpu.VMEM(halo.shape, f32),
            dma((6,)),
            pltpu.VMEM((blocks, 2, 2, snaps, CHUNK, LANES), f32),
            pltpu.VMEM((blocks, 2, 2, HALF, CHUNK, LANES), f32),
            pltpu.VMEM((2, levels, rows + 2, snaps, width), f32),
            pltpu.VMEM((blocks, 2, snaps, CHUNK, LANES), f32),
            pltpu.VMEM((cells, 1, width), f32),
            pltpu.VMEM((cells, 1, width), f32),
            pltpu.VMEM((rows, 1, width), f32),
            pltpu.VMEM((rows, 1, width), f32),
            pltpu.VMEM((n_tm, cells, 1, width), f32),
            pltpu.VMEM((snaps, LANES), f32),
            pltpu.VMEM((2, HALF, LANES), f32),
            pltpu.VMEM((snaps, LANES), f32),
            pltpu.VMEM((2, snaps, LANES), f32),
            pltpu.VMEM((2 * snaps, 2 * (snaps + HALF)), bf16),
            pltpu.VMEM((2 * snaps, 2 * HALF), bf16),
            pltpu.VMEM((cells, most, width), bf16),
            pltpu.VMEM((2, packs, HALF, LANES), f32),
            pltpu.VMEM((2, packs, HALF, LANES), f32),
            pltpu.VMEM((packs, HALF, LANES), f32),
            pltpu.VMEM((n_tile, 8, LANES), f32),
            dma((chunks,)),
            dma((chunks,)),
            dma((blocks, 2, 2)),
            dma((2,)),
            dma((chunks, 2)),
            dma((chunks, 2)),
            dma((2,)),
            dma((2,)),
            dma((2,)),
            dma((2,)),
            dma((chunks, n_tm)),
            dma((chunks, n_tm)),
            dma((n_tile,)),
            dma((n_tile,)),
        ],
        compiler_params=pltpu.CompilerParams(
            collective_id=0, has_side_effects=True, vmem_limit_bytes=60 * 1024 * 1024
        ),
        cost_estimate=pl.CostEstimate(flops=10**9, bytes_accessed=4 * 10**6, transcendentals=0),
    )(
        velocity_u, velocity_v, land_sea, bottom_level, spacing_x, spacing_y, own, halo,
    )


def shards(velocity_u, velocity_v, land_sea, bottom_level, spacing_x, spacing_y):
    snaps, levels, rows, width = velocity_u.shape
    cells = levels * rows
    n_tm = lax.axis_size("tm")
    assert width == 2 * LANES and 4 * cells == LANES and snaps == 2 * HALF
    assert rows % (2 * CHUNK) == 0 and levels == 2 and n_tm % 4 == 0 and n_tm >= 8
    own, halo = band_parts(snaps)
    args = (
        jnp.asarray(own), jnp.asarray(halo),
        velocity_u.reshape(snaps, cells, width), velocity_v.reshape(snaps, cells, width),
        land_sea, bottom_level, spacing_x, spacing_y,
    )
    conversion, mean_map, excess = quick(*args)
    conversion, mean_map = lax.cond(
        excess[0] > 0.0, lambda args, done: full(*args), lambda args, done: done, args, (conversion, mean_map)
    )
    conversion, mean_map = store(conversion, mean_map)
    return conversion.reshape(velocity_u.shape), mean_map


def store_kernel(a_ref, b_ref, a_out, b_out, sem):
    copies = [
        pltpu.make_async_copy(a_ref, a_out, sem.at[0]),
        pltpu.make_async_copy(b_ref, b_out, sem.at[1]),
    ]
    for copy in copies:
        copy.start()
    for copy in copies:
        copy.wait()


def store(a, b):
    place = pl.BlockSpec(memory_space=pl.ANY)
    return pl.pallas_call(
        store_kernel,
        out_shape=(jax.ShapeDtypeStruct(a.shape, a.dtype), jax.ShapeDtypeStruct(b.shape, b.dtype)),
        in_specs=[place, place],
        out_specs=(pl.BlockSpec(memory_space=pltpu.HBM), pl.BlockSpec(memory_space=pltpu.HBM)),
        scratch_shapes=[pltpu.SemaphoreType.DMA((2,))],
        name="store",
    )(a, b)


def solution(mesh):
    in_specs = (
        P("tm", None, None, "tile"),
        P("tm", None, None, "tile"),
        P(None, "tile"),
        P(None, "tile"),
        P(None, "tile"),
        P(None, "tile"),
    )
    out_specs = (P("tm", None, None, "tile"), P(None, None, "tile"))
    return jax.shard_map(shards, mesh=mesh, in_specs=in_specs, out_specs=out_specs, check_vma=False)
```

```python
import functools

import jax
import jax.numpy as jnp
import numpy as np
from jax import lax
from jax.experimental import pallas as pl
from jax.experimental.pallas import tpu as pltpu
from jax.sharding import PartitionSpec as P

HALF = 24
CUTOFF = 1.0 / 40.0
LANES = 128
CHUNK = 8
DEPTH = 2
AHEAD = 3
GROUP = 4
WINDOWS = (((0, 3), (0, 1)), ((1, 5), (1, 3)), ((3, 7), (5, 7)), ((5, 8), (7, 8)))
SPAN = 2 * GROUP
MESH = pl.DeviceIdType.MESH


def band_parts(count):
    offset = (np.arange(count + 2 * HALF)[None, :] - np.arange(count)[:, None] - HALF).astype(np.float64)
    weights = 2.0 * CUTOFF * np.sinc(2.0 * CUTOFF * offset) * np.sinc(offset / HALF)
    weights = np.where(np.abs(offset) <= HALF, weights, 0.0).astype(np.float32)
    own = weights[:, HALF : HALF + count]
    halo = np.concatenate([weights[:, :HALF], weights[:, HALF + count :]], axis=1)
    return own, halo


def dot(a, b):
    return jnp.dot(a, b, precision=lax.Precision.HIGHEST, preferred_element_type=jnp.float32)


def halves(a):
    high = a.astype(jnp.bfloat16).astype(jnp.float32)
    return high, a - high


def stacked_weights(w):
    high, low = halves(w)
    return jnp.concatenate(
        [jnp.concatenate([high, high], axis=1), jnp.concatenate([low, low], axis=1)], axis=0
    ).astype(jnp.bfloat16)


def split_dot(weights, pieces):
    split = [halves(p) for p in pieces]
    block = jnp.concatenate([s[0] for s in split] + [s[1] for s in split], axis=0).astype(jnp.bfloat16)
    both = jnp.dot(weights, block, preferred_element_type=jnp.float32)
    half = both.shape[0] // 2
    return both[:half] + both[half:]


def kernel(
    n_tm, n_tile, levels,
    u_ref, v_ref, land_in, bottom_in, sx_in, sy_in, own_in, halo_in,
    conv_ref, mean_ref,
    land_ref, bottom_ref, sx_ref, sy_ref, own_ref, halo_w_ref, small_sem,
    x, halo, mm, cf, wet, cx, cy, part, edge, edge_halo, edge_mean, edge_in,
    near_w, far_w, relayed, relay_send, relay_recv,
    x_sem, bulk_send, bulk_recv, edge_send, edge_recv, em_send, em_recv, part_send, part_recv,
):
    snaps, cells, width = u_ref.shape
    rows = cells // levels
    t = lax.axis_index("tm")
    z = lax.axis_index("tile")
    chunks = cells // CHUNK
    per_level = rows // CHUNK
    fields = (u_ref, v_ref)
    even = lax.rem(t, 2) == 0
    odd = jnp.logical_not(even)

    barrier = pltpu.get_barrier_semaphore()
    for k in range(1, n_tm):
        pl.semaphore_signal(barrier, inc=1, device_id={"tm": lax.rem(t + k, n_tm)}, device_id_type=MESH)

    @pl.when(z > 0)
    def _():
        pl.semaphore_signal(barrier, inc=1, device_id={"tile": z - 1}, device_id_type=MESH)

    @pl.when(z < n_tile - 1)
    def _():
        pl.semaphore_signal(barrier, inc=1, device_id={"tile": z + 1}, device_id_type=MESH)

    def local(c, f, h):
        return pltpu.make_async_copy(
            fields[f].at[:, pl.ds(c * CHUNK, CHUNK), pl.ds(h * LANES, LANES)], x.at[c, f, h], x_sem.at[c, f, h]
        )

    small = (
        (land_in, land_ref), (bottom_in, bottom_ref), (sx_in, sx_ref),
        (sy_in, sy_ref), (own_in, own_ref), (halo_in, halo_w_ref),
    )
    for i, (src, dst) in enumerate(small):
        pltpu.make_async_copy(src, dst, small_sem.at[i]).start()
    for c in range(chunks):
        for f in range(2):
            for h in range(2):
                local(c, f, h).start()

    def bulk(side, c, f, h):
        first = snaps - HALF if side == 0 else 0
        to = t + 1 if side == 0 else t - 1
        return pltpu.make_async_remote_copy(
            src_ref=fields[f].at[pl.ds(first, HALF), pl.ds(c * CHUNK, CHUNK), pl.ds(h * LANES, LANES)],
            dst_ref=halo.at[side, c, f, h],
            send_sem=bulk_send.at[side, c, f, h],
            recv_sem=bulk_recv.at[side, c, f, h],
            device_id={"tm": to},
            device_id_type=MESH,
        )

    middle = (n_tm // 2 - 1, n_tm // 2)
    via = (n_tm - 1, 0)

    def to_relay(side, c, h):
        first = snaps - HALF if side == 0 else 0
        return pltpu.make_async_remote_copy(
            src_ref=fields[1].at[pl.ds(first, HALF), pl.ds(c * CHUNK, CHUNK), pl.ds(h * LANES, LANES)],
            dst_ref=relayed.at[c, h],
            send_sem=bulk_send.at[side, c, 1, h],
            recv_sem=relay_recv.at[c, h],
            device_id={"tm": via[side]},
            device_id_type=MESH,
        )

    def from_relay(side, c, h):
        return pltpu.make_async_remote_copy(
            src_ref=relayed.at[c, h],
            dst_ref=halo.at[side, c, 1, h],
            send_sem=relay_send.at[c, h],
            recv_sem=bulk_recv.at[side, c, 1, h],
            device_id={"tm": middle[1 - side]},
            device_id_type=MESH,
        )

    def pass_on(c):
        if n_tm < 4:
            return
        for side in range(2):

            @pl.when(t == via[side])
            def _():
                for h in range(2):
                    to_relay(side, c, h).wait_recv()
                    from_relay(side, c, h).start()

    def edge_copy(side):
        first = snaps - HALF if side == 0 else 0
        to = t + 1 if side == 0 else t - 1
        return pltpu.make_async_remote_copy(
            src_ref=edge.at[pl.ds(first, HALF), :],
            dst_ref=edge_halo.at[side],
            send_sem=edge_send.at[side],
            recv_sem=edge_recv.at[side],
            device_id={"tm": to},
            device_id_type=MESH,
        )

    def mean_copy(side):
        to = z + 1 if side == 0 else z - 1
        return pltpu.make_async_remote_copy(
            src_ref=edge_mean,
            dst_ref=edge_in.at[side],
            send_sem=em_send.at[side],
            recv_sem=em_recv.at[side],
            device_id={"tile": to},
            device_id_type=MESH,
        )

    def converted(c):
        piece = c % per_level
        low = piece * CHUNK - (1 if piece else 0)
        high = rows if piece == per_level - 1 else (piece + 1) * CHUNK - 1
        return c // per_level, low, high

    def part_copy(c, k, slot):
        l, low, high = converted(c)
        return pltpu.make_async_remote_copy(
            src_ref=part.at[slot, pl.ds(l * rows + low, high - low)],
            dst_ref=part.at[slot, pl.ds(l * rows + low, high - low)],
            send_sem=part_send.at[c, k],
            recv_sem=part_recv.at[c, k],
            device_id={"tm": lax.rem(t + k, n_tm)},
            device_id_type=MESH,
        )

    sends = (t < n_tm - 1, t > 0)
    receives = (t > 0, t < n_tm - 1)
    send_near, send_far = (even, odd), (odd, even)
    near, far = (odd, even), (even, odd)
    z_sends = (z < n_tile - 1, z > 0)
    z_receives = (z > 0, z < n_tile - 1)

    def start_far(c):
        for side in range(2):
            if n_tm >= 4:

                @pl.when(t == middle[side])
                def _():
                    for h in range(2):
                        to_relay(side, c, h).start()
                        bulk(side, c, 0, h).start()

                whole = sends[side] & send_far[side] & (t != middle[side])
            else:
                whole = sends[side] & send_far[side]

            @pl.when(whole)
            def _():
                for f in range(2):
                    for h in range(2):
                        bulk(side, c, f, h).start()

    def finish_send(c, which):
        for side in range(2):

            @pl.when(sends[side] & which[side])
            def _():
                for f in range(2):
                    for h in range(2):
                        bulk(side, c, f, h).wait_send()

    pl.semaphore_wait(barrier, n_tm - 1 + (z > 0).astype(jnp.int32) + (z < n_tile - 1).astype(jnp.int32))

    for c in range(DEPTH):
        start_far(c)
    for side in range(2):

        @pl.when(sends[side] & send_near[side])
        def _():
            for c in range(chunks):
                for f in range(2):
                    for h in range(2):
                        bulk(side, c, f, h).start()

    for side in range(2):

        @pl.when(jnp.logical_not(receives[side]))
        def _():
            halo[side] = jnp.zeros(halo.shape[1:], jnp.float32)
            edge_halo[side] = jnp.zeros(edge_halo.shape[1:], jnp.float32)

        @pl.when(jnp.logical_not(z_receives[side]))
        def _():
            edge_in[side] = jnp.zeros(edge_in.shape[1:], jnp.float32)

    for i, (src, dst) in enumerate(small):
        pltpu.make_async_copy(src, dst, small_sem.at[i]).wait()

    for l in range(levels):
        is_wet = (land_ref[...] == 1) & (l < bottom_ref[...])
        level_wet = jnp.where(is_wet, 1.0, 0.0).astype(jnp.float32)
        for j in range(rows):
            wet[l * rows + j] = level_wet[j : j + 1, :]
    all_x, all_y = 0.5 / sx_ref[...], 0.5 / sy_ref[...]
    for j in range(rows):
        cx[j] = all_x[j : j + 1, :]
        cy[j] = all_y[j : j + 1, :]
    for f in range(2):
        for l in range(levels):
            for j in (0, rows + 1):
                mm[f, l, j] = jnp.zeros((snaps, width), jnp.float32)
    column = lax.broadcasted_iota(jnp.int32, (snaps, 2 * HALF), 1)
    valid = ((column >= HALF) | (t > 0)) & ((column < HALF) | (t < n_tm - 1))
    own_w = own_ref[...]
    halo_w = jnp.where(valid, halo_w_ref[...], 0.0)
    weight_sum = jnp.sum(own_w, axis=1, keepdims=True) + jnp.sum(halo_w, axis=1, keepdims=True)
    own_w = own_w / weight_sum
    halo_w = halo_w / weight_sum
    near_side = 1 - lax.rem(t, 2)
    far_side = lax.rem(t, 2)
    near_half = jnp.where(even, halo_w[:, HALF:], halo_w[:, :HALF])
    far_half = jnp.where(even, halo_w[:, :HALF], halo_w[:, HALF:])
    near_w[...] = stacked_weights(jnp.concatenate([own_w, near_half], axis=1))
    far_w[...] = stacked_weights(far_half)

    for c in range(chunks):
        for f in range(2):
            for h in range(2):
                local(c, f, h).wait()

    def series(ref, count, j):
        return ref.reshape(count * CHUNK, LANES)[pl.ds(j, count, stride=CHUNK), :]

    def both(ref, count, j):
        return jnp.concatenate([series(ref.at[h], count, j) for h in range(2)], axis=1)

    lane = lax.broadcasted_iota(jnp.int32, (snaps, LANES), 1)

    def pack(r, acc):
        c, j = r // CHUNK, lax.rem(r, CHUNK)
        for f in range(2):
            q = f * cells + r
            first = series(x.at[c, f, 0], snaps, j) * wet[r][:, :LANES]
            acc = jnp.where(lane == q, pltpu.roll(first, q, 1), acc)
            q = (2 + f) * cells + r
            last = series(x.at[c, f, 1], snaps, j) * wet[r][:, width - LANES :]
            acc = jnp.where(lane == q, pltpu.roll(last, lax.rem(q + 1, LANES), 1), acc)
        return acc

    edge[...] = lax.fori_loop(0, cells, pack, jnp.zeros((snaps, LANES), jnp.float32), unroll=4)
    for side in range(2):

        @pl.when(sends[side])
        def _():
            edge_copy(side).start()

    pass_on(0)

    for side in range(2):

        @pl.when(receives[side] & near[side])
        def _():
            for c in range(chunks):
                for f in range(2):
                    for h in range(2):
                        bulk(side, c, f, h).wait_recv()

    def near_part(r, carry):
        l, j = r // rows, lax.rem(r, rows)
        c, i = r // CHUNK, lax.rem(r, CHUNK)
        for f in range(2):
            pieces = [both(x.at[c, f], snaps, i), both(halo.at[near_side, c, f], HALF, i)]
            mm[f, l, j + 1] = split_dot(near_w[...], pieces)
        return carry

    lax.fori_loop(0, cells, near_part, 0, unroll=8)
    for c in range(1, DEPTH):
        pass_on(c)

    for side in range(2):

        @pl.when(receives[side])
        def _():
            edge_copy(side).wait_recv()

    edge_mean[...] = dot(own_w, edge[...]) + dot(
        halo_w, jnp.concatenate([edge_halo[0], edge_halo[1]], axis=0)
    )
    for side in range(2):

        @pl.when(z_sends[side])
        def _():
            mean_copy(side).start()

    wide = lax.broadcasted_iota(jnp.int32, (snaps, width), 1)

    def far_part(r, carry):
        l, j = r // rows, lax.rem(r, rows)
        c, i = r // CHUNK, lax.rem(r, CHUNK)
        mask = wet[r]
        for f in range(2):
            pieces = [both(halo.at[far_side, c, f], HALF, i)]
            mm[f, l, j + 1] = (mm[f, l, j + 1] + split_dot(far_w[...], pieces)) * mask
        return carry

    def grad_x(f, r, masked, scale):
        q = (2 + f) * cells + r
        before = pltpu.roll(edge_in[0], lax.rem(2 * LANES - q, LANES), 1)
        q = f * cells + r
        after = pltpu.roll(edge_in[1], lax.rem(2 * LANES - 1 - q, LANES), 1)
        before = jnp.concatenate([before, before], axis=1)
        after = jnp.concatenate([after, after], axis=1)
        behind = jnp.where(wide == 0, before, pltpu.roll(masked, 1, 1))
        ahead = jnp.where(wide == width - 1, after, pltpu.roll(masked, width - 1, 1))
        return (ahead - behind) * scale

    def convert(l):
        def body(j, carry):
            r = l * rows + j
            c, i = r // CHUNK, lax.rem(r, CHUNK)
            mask = wet[r]
            scale_x = cx[j]
            scale_y = cy[j]
            eddy, gx, gy = [], [], []
            for f in range(2):
                masked = mm[f, l, j + 1]
                eddy.append(both(x.at[c, f], snaps, i) - masked)
                gx.append(grad_x(f, r, masked, scale_x))
                gy.append((mm[f, l, j + 2] - mm[f, l, j]) * scale_y)
            eu, ev = eddy
            total = eu * eu * gx[0] + eu * ev * (gy[0] + gx[1]) + ev * ev * gy[1]
            conversion = -mask * total
            for h in range(2):
                cf.at[c, h].reshape(snaps * CHUNK, LANES)[pl.ds(i, snaps, stride=CHUNK), :] = conversion[
                    :, h * LANES : (h + 1) * LANES
                ]
            part[t, r] = jnp.sum(conversion, axis=0, keepdims=True)
            return carry

        return body

    for c in range(chunks):
        finish_send(c, send_far)
        if c + DEPTH < chunks:
            start_far(c + DEPTH)
        for side in range(2):

            @pl.when(receives[side] & far[side])
            def _():
                for f in range(2):
                    for h in range(2):
                        bulk(side, c, f, h).wait_recv()

        lax.fori_loop(c * CHUNK, (c + 1) * CHUNK, far_part, 0, unroll=8)
        if c + DEPTH < chunks:
            pass_on(c + DEPTH)
        if c == 0:
            for side in range(2):

                @pl.when(z_receives[side])
                def _():
                    mean_copy(side).wait_recv()

        l, low, high = converted(c)
        lax.fori_loop(low, high, convert(l), 0, unroll=2)
        for k in range(1, n_tm):
            part_copy(c, k, t).start()
        if c % per_level == per_level - 1:

            def narrow(s, carry):
                for h in range(2):
                    block = jnp.concatenate([cf[l * per_level + p, h, s] for p in range(per_level)], axis=0)
                    conv_ref[s, pl.ds(l * rows, rows), pl.ds(h * LANES, LANES)] = block.astype(jnp.bfloat16)
                return carry

            lax.fori_loop(0, snaps, narrow, 0, unroll=4)

    for c in range(chunks):
        for k in range(1, n_tm):
            part_copy(c, k, lax.rem(t + n_tm - k, n_tm)).wait_recv()
        l, low, high = converted(c)
        for j in range(low, high):
            total = part[0, l * rows + j]
            for s in range(1, n_tm):
                total = total + part[s, l * rows + j]
            mean_ref[l, j : j + 1, :] = total / (snaps * n_tm)

    for c in range(chunks):
        finish_send(c, send_near)
    for side in range(2):

        @pl.when(sends[side])
        def _():
            edge_copy(side).wait_send()

        @pl.when(z_sends[side])
        def _():
            mean_copy(side).wait_send()

        if n_tm >= 4:

            @pl.when(t == via[side])
            def _():
                for c in range(chunks):
                    for h in range(2):
                        from_relay(side, c, h).wait_send()

    for c in range(chunks):
        for k in range(1, n_tm):
            part_copy(c, k, t).wait_send()


def fast_kernel(
    n_tm, n_tile, levels,
    u_ref, v_ref, land_in, bottom_in, sx_in, sy_in, own_in, halo_in,
    conv_ref, mean_ref, flag_ref,
    land_ref, bottom_ref, sx_ref, sy_ref, own_ref, halo_w_ref, small_sem,
    x, near, mm, cf, wet, key, cx, cy, part, edge, edge_halo, edge_mean, edge_in,
    near_w, far_w, place, packed, far, relayed, flags,
    relay_send, relay_recv, x_sem, near_sem, far_send, far_recv, edge_send, edge_recv, em_send, em_recv,
    part_send, part_recv, flag_send, flag_recv,
):
    snaps, cells, width = u_ref.shape
    rows = cells // levels
    t = lax.axis_index("tm")
    z = lax.axis_index("tile")
    blocks = cells // CHUNK
    per_level = rows // CHUNK
    chunks = rows // GROUP
    fields = (u_ref, v_ref)
    even = lax.rem(t, 2) == 0
    odd = jnp.logical_not(even)

    barrier = pltpu.get_barrier_semaphore()
    for k in range(1, n_tm):
        pl.semaphore_signal(barrier, inc=1, device_id={"tm": lax.rem(t + k, n_tm)}, device_id_type=MESH)
    for k in range(1, n_tile):
        pl.semaphore_signal(barrier, inc=1, device_id={"tile": lax.rem(z + k, n_tile)}, device_id_type=MESH)

    def local(c, f, h):
        return pltpu.make_async_copy(
            fields[f].at[:, pl.ds(c * CHUNK, CHUNK), pl.ds(h * LANES, LANES)], x.at[c, f, h], x_sem.at[c, f, h]
        )

    small = (
        (land_in, land_ref), (bottom_in, bottom_ref), (sx_in, sx_ref),
        (sy_in, sy_ref), (own_in, own_ref), (halo_in, halo_w_ref),
    )
    for i, (src, dst) in enumerate(small):
        pltpu.make_async_copy(src, dst, small_sem.at[i]).start()
    for p in range(per_level):
        for l in range(levels):
            for f in range(2):
                for h in range(2):
                    local(l * per_level + p, f, h).start()

    first_far = jnp.where(even, 0, snaps - HALF)
    first_near = jnp.where(even, snaps - HALF, 0)
    has_far = (t > 0) & (t < n_tm - 1)
    at_end = jnp.logical_not(has_far)
    is_middle = (t == n_tm // 2 - 1) | (t == n_tm // 2)
    far_to = jnp.where(even, t - 1, t + 1)
    via_to = jnp.where(t < n_tm // 2, n_tm - 1, 0)
    forward_to = jnp.where(t == 0, n_tm // 2 - 1, n_tm // 2)

    def tiles(c):
        return c * SPAN, SPAN

    def near_copy():
        return pltpu.make_async_remote_copy(
            src_ref=x.at[:, :, :, pl.ds(first_near, HALF)],
            dst_ref=near,
            send_sem=near_sem.at[0],
            recv_sem=near_sem.at[1],
            device_id={"tm": t + 1 - 2 * lax.rem(t, 2)},
            device_id_type=MESH,
        )

    def far_copy(c, f):
        start, count = tiles(c)
        return pltpu.make_async_remote_copy(
            src_ref=packed.at[f, pl.ds(start, count)],
            dst_ref=far.at[f, pl.ds(start, count)],
            send_sem=far_send.at[c, f],
            recv_sem=far_recv.at[c, f],
            device_id={"tm": far_to},
            device_id_type=MESH,
        )

    def to_relay(c):
        start, count = tiles(c)
        return pltpu.make_async_remote_copy(
            src_ref=packed.at[1, pl.ds(start, count)],
            dst_ref=relayed.at[pl.ds(start, count)],
            send_sem=far_send.at[c, 1],
            recv_sem=relay_recv.at[c],
            device_id={"tm": via_to},
            device_id_type=MESH,
        )

    def from_relay(c):
        start, count = tiles(c)
        return pltpu.make_async_remote_copy(
            src_ref=relayed.at[pl.ds(start, count)],
            dst_ref=far.at[1, pl.ds(start, count)],
            send_sem=relay_send.at[c],
            recv_sem=far_recv.at[c, 1],
            device_id={"tm": forward_to},
            device_id_type=MESH,
        )

    def pass_on(c):
        @pl.when(at_end)
        def _():
            to_relay(c).wait_recv()
            from_relay(c).start()

    def start_far(c):
        @pl.when(has_far)
        def _():
            far_copy(c, 0).start()

        @pl.when(is_middle)
        def _():
            to_relay(c).start()

        @pl.when(has_far & jnp.logical_not(is_middle))
        def _():
            far_copy(c, 1).start()

    def edge_copy(side):
        first = snaps - HALF if side == 0 else 0
        to = t + 1 if side == 0 else t - 1
        return pltpu.make_async_remote_copy(
            src_ref=edge.at[pl.ds(first, HALF), :],
            dst_ref=edge_halo.at[side],
            send_sem=edge_send.at[side],
            recv_sem=edge_recv.at[side],
            device_id={"tm": to},
            device_id_type=MESH,
        )

    def mean_copy(side):
        to = z + 1 if side == 0 else z - 1
        return pltpu.make_async_remote_copy(
            src_ref=edge_mean,
            dst_ref=edge_in.at[side],
            send_sem=em_send.at[side],
            recv_sem=em_recv.at[side],
            device_id={"tile": to},
            device_id_type=MESH,
        )

    def flag_copy(k, slot):
        return pltpu.make_async_remote_copy(
            src_ref=flags.at[slot],
            dst_ref=flags.at[slot],
            send_sem=flag_send.at[k],
            recv_sem=flag_recv.at[k],
            device_id={"tile": lax.rem(z + k, n_tile)},
            device_id_type=MESH,
        )

    def converted(c):
        return c * GROUP - (1 if c else 0), rows if c == chunks - 1 else (c + 1) * GROUP - 1

    def part_copy(c, k, slot):
        low, high = converted(c)
        return pltpu.make_async_remote_copy(
            src_ref=part.at[slot, pl.ds(levels * low, levels * (high - low))],
            dst_ref=part.at[slot, pl.ds(levels * low, levels * (high - low))],
            send_sem=part_send.at[c, k],
            recv_sem=part_recv.at[c, k],
            device_id={"tm": lax.rem(t + k, n_tm)},
            device_id_type=MESH,
        )

    sends = (t < n_tm - 1, t > 0)
    receives = (t > 0, t < n_tm - 1)
    z_sends = (z < n_tile - 1, z > 0)
    z_receives = (z > 0, z < n_tile - 1)

    for i, (src, dst) in enumerate(small):
        pltpu.make_async_copy(src, dst, small_sem.at[i]).wait()

    levels_wet = []
    for l in range(levels):
        is_wet = (land_ref[...] == 1) & (l < bottom_ref[...])
        levels_wet.append(jnp.where(is_wet, 1.0, 0.0).astype(jnp.float32))
    all_wet = jnp.concatenate(levels_wet, axis=0)
    lower = lax.broadcasted_iota(jnp.int32, (width, width), 0)
    upper = lax.broadcasted_iota(jnp.int32, (width, width), 1)
    earlier = jnp.where(lower < upper, 1.0, 0.0).astype(jnp.bfloat16)

    def ranked(index):
        j = lax.rem(index, rows)
        side = lax.rem(j, GROUP) // 2
        inner = jnp.where(side == 0, lax.rem(j, 2), 1 - lax.rem(j, 2))
        return 2 * (j // GROUP) + side, 2 * inner + (1 - index // rows)

    set_a, rank_a = ranked(lax.broadcasted_iota(jnp.int32, (cells, cells), 0))
    set_b, rank_b = ranked(lax.broadcasted_iota(jnp.int32, (cells, cells), 1))
    ahead_rows = jnp.where((set_a == set_b) & (rank_b < rank_a), 1.0, 0.0).astype(jnp.bfloat16)
    same_rows = jnp.where((set_a // 2 == set_b // 2) & (set_a != set_b), 1.0, 0.0).astype(jnp.bfloat16)
    wet_bits = all_wet.astype(jnp.bfloat16)
    filled = jnp.dot(
        jnp.concatenate([ahead_rows, same_rows], axis=0), wet_bits, preferred_element_type=jnp.float32
    ).astype(jnp.bfloat16)
    every = jnp.ones((width, width), jnp.bfloat16)
    order = jnp.dot(wet_bits, earlier, preferred_element_type=jnp.float32) + jnp.dot(
        filled[:cells], every, preferred_element_type=jnp.float32
    )
    other = jnp.dot(filled[cells:], every, preferred_element_type=jnp.float32)
    row = lax.broadcasted_iota(jnp.int32, (cells, width), 0)
    right = lax.rem(lax.rem(row, rows), GROUP) >= 2
    spot = jnp.where(right, float(SPAN * LANES - 1) - order, order)
    first_lane = jnp.zeros((cells, width), jnp.float32)
    lanes_used = jnp.zeros((cells, width), jnp.float32)
    for q in range(GROUP):
        for l in range(levels):
            here = (lax.rem(lax.rem(row, rows), GROUP) == q) & (row // rows == l)
            low, high = WINDOWS[q][l]
            first_lane = jnp.where(here, float(low * LANES), first_lane)
            lanes_used = jnp.where(here, float((high - low) * LANES), lanes_used)
    spot = spot - first_lane
    fits = (spot >= 0.0) & (spot < lanes_used) & (order + other < float(SPAN * LANES))
    is_wet = all_wet > 0.0
    all_key = jnp.where(is_wet & fits, spot, -1.0)
    over = jnp.max(jnp.where(is_wet & jnp.logical_not(fits), 1.0, 0.0), axis=0, keepdims=True)
    flags[z] = jnp.broadcast_to(jnp.maximum(over[:, :LANES], over[:, LANES:]), (8, LANES))
    for r in range(cells):
        wet[r] = all_wet[r : r + 1, :]
        key[r] = all_key[r : r + 1, :]

    def series(ref, count, j):
        return ref.reshape(count * CHUNK, LANES)[pl.ds(j, count, stride=CHUNK), :]

    def both(ref, count, j):
        return jnp.concatenate([series(ref.at[h], count, j) for h in range(2)], axis=1)

    def members(c):
        for q in range(GROUP):
            for l in range(levels):
                low, high = WINDOWS[q][l]
                j = c * GROUP + q
                yield l * rows + j, l * per_level + j // CHUNK, j % CHUNK, low, high

    def put(r, size):
        index = lax.broadcasted_iota(jnp.int32, (size, width), 0).astype(jnp.float32)
        place[r, :size] = jnp.where(index == key[r], 1.0, 0.0).astype(jnp.bfloat16)

    def gather(r, b, i, size):
        split = []
        for f in range(2):
            block = [x.at[b, f, h].reshape(snaps * CHUNK, LANES) for h in range(2)]
            at = pl.ds(first_far * CHUNK + i, HALF, stride=CHUNK)
            split.extend(halves(jnp.concatenate([p[at, :] for p in block], axis=1)))
        split = jnp.concatenate(split, axis=0).astype(jnp.bfloat16)
        out = lax.dot_general(
            split, place[r, :size], (((1,), (1,)), ((), ())), preferred_element_type=jnp.float32
        )
        return [out[2 * f * HALF : (2 * f + 1) * HALF] + out[(2 * f + 1) * HALF : (2 * f + 2) * HALF] for f in range(2)]

    def compact(c):
        @pl.when(has_far)
        def _():
            compact_far(c)

    def compact_far(c):
        start, count = tiles(c)
        for r, _, _, low, high in members(c):
            put(r, (high - low) * LANES)
        sums = [[None] * count for f in range(2)]
        for r, b, i, low, high in members(c):
            values = gather(r, b, i, (high - low) * LANES)
            for f in range(2):
                for p in range(low, high):
                    piece = values[f][:, (p - low) * LANES : (p - low + 1) * LANES]
                    sums[f][p] = piece if sums[f][p] is None else sums[f][p] + piece
        for f in range(2):
            for p in range(count):
                packed[f, start + p] = sums[f][p]

    def wait_local(c):
        for f in range(2):
            for h in range(2):
                local(c, f, h).wait()

    for c in range(blocks):
        wait_local(c)
    lane = lax.broadcasted_iota(jnp.int32, (snaps, LANES), 1)

    def pack(r, acc):
        c, j = r // CHUNK, lax.rem(r, CHUNK)
        for f in range(2):
            q = f * cells + r
            first = series(x.at[c, f, 0], snaps, j) * wet[r][:, :LANES]
            acc = jnp.where(lane == q, pltpu.roll(first, q, 1), acc)
            q = (2 + f) * cells + r
            last = series(x.at[c, f, 1], snaps, j) * wet[r][:, width - LANES :]
            acc = jnp.where(lane == q, pltpu.roll(last, lax.rem(q + 1, LANES), 1), acc)
        return acc

    compact(0)
    pl.semaphore_wait(barrier, n_tm - 1 + n_tile - 1)
    start_far(0)
    edge[...] = lax.fori_loop(0, cells, pack, jnp.zeros((snaps, LANES), jnp.float32), unroll=4)
    for side in range(2):

        @pl.when(sends[side])
        def _():
            edge_copy(side).start()

    for k in range(1, n_tile):
        flag_copy(k, z).start()
    near_copy().start()
    compact(1)
    start_far(1)
    for side in range(2):

        @pl.when(jnp.logical_not(receives[side]))
        def _():
            edge_halo[side] = jnp.zeros(edge_halo.shape[1:], jnp.float32)

        @pl.when(jnp.logical_not(z_receives[side]))
        def _():
            edge_in[side] = jnp.zeros(edge_in.shape[1:], jnp.float32)

    all_x, all_y = 0.5 / sx_ref[...], 0.5 / sy_ref[...]
    for j in range(rows):
        cx[j] = all_x[j : j + 1, :]
        cy[j] = all_y[j : j + 1, :]
    for f in range(2):
        for l in range(levels):
            for j in (0, rows + 1):
                mm[f, l, j] = jnp.zeros((snaps, width), jnp.float32)
    column = lax.broadcasted_iota(jnp.int32, (snaps, 2 * HALF), 1)
    valid = ((column >= HALF) | (t > 0)) & ((column < HALF) | (t < n_tm - 1))
    own_w = own_ref[...]
    halo_w = jnp.where(valid, halo_w_ref[...], 0.0)
    weight_sum = jnp.sum(own_w, axis=1, keepdims=True) + jnp.sum(halo_w, axis=1, keepdims=True)
    own_w = own_w / weight_sum
    halo_w = halo_w / weight_sum
    near_half = jnp.where(even, halo_w[:, HALF:], halo_w[:, :HALF])
    far_half = jnp.where(even, halo_w[:, :HALF], halo_w[:, HALF:])
    near_w[...] = stacked_weights(jnp.concatenate([own_w, near_half], axis=1))
    far_w[...] = stacked_weights(far_half)

    pass_on(0)
    for side in range(2):

        @pl.when(receives[side])
        def _():
            edge_copy(side).wait_recv()

    edge_mean[...] = dot(own_w, edge[...]) + dot(
        halo_w, jnp.concatenate([edge_halo[0], edge_halo[1]], axis=0)
    )
    for side in range(2):

        @pl.when(z_sends[side])
        def _():
            mean_copy(side).start()

    compact(2)
    start_far(2)
    def near_part(r, carry):
        l, j = r // rows, lax.rem(r, rows)
        c, i = r // CHUNK, lax.rem(r, CHUNK)
        for f in range(2):
            pieces = [both(x.at[c, f], snaps, i), both(near.at[c, f], HALF, i)]
            mm[f, l, j + 1] = split_dot(near_w[...], pieces)
        return carry

    near_copy().wait_recv()
    lax.fori_loop(0, cells, near_part, 0, unroll=8)
    compact(3)
    pass_on(1)
    pass_on(2)
    wide = lax.broadcasted_iota(jnp.int32, (snaps, width), 1)

    def spread(r, blocks):
        l, j = r // rows, r % rows
        size = blocks[0].shape[1]
        split = []
        for block in blocks:
            split.extend(halves(block))
        out = jnp.dot(
            jnp.concatenate(split, axis=0).astype(jnp.bfloat16), place[r, :size], preferred_element_type=jnp.float32
        ).astype(jnp.bfloat16)
        mask = wet[r]
        for f in range(2):
            both_halves = jnp.dot(
                far_w[...], out[2 * f * HALF : 2 * (f + 1) * HALF], preferred_element_type=jnp.float32
            )
            mm[f, l, j + 1] = (mm[f, l, j + 1] + both_halves[:snaps] + both_halves[snaps:]) * mask

    def far_part(c):
        start, _ = tiles(c)

        @pl.when(has_far)
        def _():
            for f in range(2):
                far_copy(c, f).wait_recv()
            for r, _, _, low, high in members(c):
                spread(
                    r, [jnp.concatenate([far[f, start + p] for p in range(low, high)], axis=1) for f in range(2)]
                )

        @pl.when(at_end)
        def _():
            for r, _, _, _, _ in members(c):
                for f in range(2):
                    mm[f, r // rows, r % rows + 1] = mm[f, r // rows, r % rows + 1] * wet[r]

    def grad_x(f, r, masked, scale):
        q = (2 + f) * cells + r
        before = pltpu.roll(edge_in[0], lax.rem(2 * LANES - q, LANES), 1)
        q = f * cells + r
        after = pltpu.roll(edge_in[1], lax.rem(2 * LANES - 1 - q, LANES), 1)
        before = jnp.concatenate([before, before], axis=1)
        after = jnp.concatenate([after, after], axis=1)
        behind = jnp.where(wide == 0, before, pltpu.roll(masked, 1, 1))
        ahead = jnp.where(wide == width - 1, after, pltpu.roll(masked, width - 1, 1))
        return (ahead - behind) * scale

    def convert(low, count):
        def body(q, carry):
            l, j = q // count, low + lax.rem(q, count)
            r = l * rows + j
            c, i = r // CHUNK, lax.rem(r, CHUNK)
            mask = wet[r]
            scale_x = cx[j]
            scale_y = cy[j]
            eddy, gx, gy = [], [], []
            for f in range(2):
                masked = mm[f, l, j + 1]
                eddy.append(both(x.at[c, f], snaps, i) - masked)
                gx.append(grad_x(f, r, masked, scale_x))
                gy.append((mm[f, l, j + 2] - mm[f, l, j]) * scale_y)
            eu, ev = eddy
            total = eu * eu * gx[0] + eu * ev * (gy[0] + gx[1]) + ev * ev * gy[1]
            conversion = -mask * total
            for h in range(2):
                cf.at[c, h].reshape(snaps * CHUNK, LANES)[pl.ds(i, snaps, stride=CHUNK), :] = conversion[
                    :, h * LANES : (h + 1) * LANES
                ]
            part[t, levels * j + l] = jnp.sum(conversion, axis=0, keepdims=True)
            return carry

        return body

    def finish(c):
        for k in range(1, n_tm):
            part_copy(c, k, lax.rem(t + n_tm - k, n_tm)).wait_recv()
        low, high = converted(c)
        for j in range(low, high):
            for l in range(levels):
                total = part[0, levels * j + l]
                for s in range(1, n_tm):
                    total = total + part[s, levels * j + l]
                mean_ref[l, j : j + 1, :] = total / (snaps * n_tm)

    for c in range(chunks):
        @pl.when(has_far)
        def _():
            for f in range(2):
                far_copy(c, f).wait_send()

        if c + AHEAD < chunks:
            start_far(c + AHEAD)

        far_part(c)
        if c + AHEAD < chunks:
            pass_on(c + AHEAD)
        if c == 0:
            for side in range(2):

                @pl.when(z_receives[side])
                def _():
                    mean_copy(side).wait_recv()

        low, high = converted(c)
        lax.fori_loop(0, levels * (high - low), convert(low, high - low), 0, unroll=high - low)
        for k in range(1, n_tm):
            part_copy(c, k, t).start()

    def narrow(s, carry):
        for l in range(levels):
            for h in range(2):
                block = jnp.concatenate([cf[l * per_level + p, h, s] for p in range(per_level)], axis=0)
                conv_ref[s, pl.ds(l * rows, rows), pl.ds(h * LANES, LANES)] = block.astype(jnp.bfloat16)
        return carry

    lax.fori_loop(0, snaps, narrow, 0, unroll=4)
    for k in range(1, n_tile):
        flag_copy(k, lax.rem(z + n_tile - k, n_tile)).wait_recv()
    worst = flags[0]
    for s in range(1, n_tile):
        worst = jnp.maximum(worst, flags[s])
    flag_ref[0] = jnp.max(worst)
    for c in range(chunks):
        finish(c)

    near_copy().wait_send()
    for side in range(2):

        @pl.when(sends[side])
        def _():
            edge_copy(side).wait_send()

        @pl.when(z_sends[side])
        def _():
            mean_copy(side).wait_send()

    @pl.when(at_end)
    def _():
        for c in range(chunks):
            from_relay(c).wait_send()

    for k in range(1, n_tile):
        flag_copy(k, z).wait_send()
    for c in range(chunks):
        for k in range(1, n_tm):
            part_copy(c, k, t).wait_send()


def full(own, halo, velocity_u, velocity_v, land_sea, bottom_level, spacing_x, spacing_y):
    snaps, cells, width = velocity_u.shape
    rows = land_sea.shape[0]
    levels = cells // rows
    n_tm, n_tile = lax.axis_size("tm"), lax.axis_size("tile")
    chunks = cells // CHUNK
    vmem = pl.BlockSpec(memory_space=pltpu.VMEM)
    hbm = pl.BlockSpec(memory_space=pltpu.HBM)
    f32, bf16 = jnp.float32, jnp.bfloat16
    dma = pltpu.SemaphoreType.DMA
    return pl.pallas_call(
        functools.partial(kernel, n_tm, n_tile, levels),
        out_shape=(
            jax.ShapeDtypeStruct((snaps, cells, width), bf16),
            jax.ShapeDtypeStruct((levels, rows, width), f32),
        ),
        in_specs=[hbm] * 8,
        out_specs=(vmem, vmem),
        scratch_shapes=[
            pltpu.VMEM((rows, width), jnp.int32),
            pltpu.VMEM((rows, width), jnp.int32),
            pltpu.VMEM((rows, width), f32),
            pltpu.VMEM((rows, width), f32),
            pltpu.VMEM(own.shape, f32),
            pltpu.VMEM(halo.shape, f32),
            dma((6,)),
            pltpu.VMEM((chunks, 2, 2, snaps, CHUNK, LANES), f32),
            pltpu.VMEM((2, chunks, 2, 2, HALF, CHUNK, LANES), f32),
            pltpu.VMEM((2, levels, rows + 2, snaps, width), f32),
            pltpu.VMEM((chunks, 2, snaps, CHUNK, LANES), f32),
            pltpu.VMEM((cells, 1, width), f32),
            pltpu.VMEM((rows, 1, width), f32),
            pltpu.VMEM((rows, 1, width), f32),
            pltpu.VMEM((n_tm, cells, 1, width), f32),
            pltpu.VMEM((snaps, LANES), f32),
            pltpu.VMEM((2, HALF, LANES), f32),
            pltpu.VMEM((snaps, LANES), f32),
            pltpu.VMEM((2, snaps, LANES), f32),
            pltpu.VMEM((2 * snaps, 2 * (snaps + HALF)), bf16),
            pltpu.VMEM((2 * snaps, 2 * HALF), bf16),
            pltpu.VMEM((chunks, 2, HALF, CHUNK, LANES), f32),
            dma((chunks, 2)),
            dma((chunks, 2)),
            dma((chunks, 2, 2)),
            dma((2, chunks, 2, 2)),
            dma((2, chunks, 2, 2)),
            dma((2,)),
            dma((2,)),
            dma((2,)),
            dma((2,)),
            dma((chunks, n_tm)),
            dma((chunks, n_tm)),
        ],
        compiler_params=pltpu.CompilerParams(
            collective_id=1, has_side_effects=True, vmem_limit_bytes=60 * 1024 * 1024
        ),
        cost_estimate=pl.CostEstimate(flops=10**9, bytes_accessed=4 * 10**6, transcendentals=0),
    )(
        velocity_u, velocity_v, land_sea, bottom_level, spacing_x, spacing_y, own, halo,
    )


def quick(own, halo, velocity_u, velocity_v, land_sea, bottom_level, spacing_x, spacing_y):
    snaps, cells, width = velocity_u.shape
    rows = land_sea.shape[0]
    levels = cells // rows
    n_tm, n_tile = lax.axis_size("tm"), lax.axis_size("tile")
    blocks = cells // CHUNK
    chunks = rows // GROUP
    packs = chunks * SPAN
    most = max(high - low for pair in WINDOWS for low, high in pair) * LANES
    vmem = pl.BlockSpec(memory_space=pltpu.VMEM)
    hbm = pl.BlockSpec(memory_space=pltpu.HBM)
    f32, bf16 = jnp.float32, jnp.bfloat16
    dma = pltpu.SemaphoreType.DMA
    return pl.pallas_call(
        functools.partial(fast_kernel, n_tm, n_tile, levels),
        out_shape=(
            jax.ShapeDtypeStruct((snaps, cells, width), bf16),
            jax.ShapeDtypeStruct((levels, rows, width), f32),
            jax.ShapeDtypeStruct((1,), f32),
        ),
        in_specs=[hbm] * 8,
        out_specs=(vmem, vmem, pl.BlockSpec(memory_space=pltpu.SMEM)),
        scratch_shapes=[
            pltpu.VMEM((rows, width), jnp.int32),
            pltpu.VMEM((rows, width), jnp.int32),
            pltpu.VMEM((rows, width), f32),
            pltpu.VMEM((rows, width), f32),
            pltpu.VMEM(own.shape, f32),
            pltpu.VMEM(halo.shape, f32),
            dma((6,)),
            pltpu.VMEM((blocks, 2, 2, snaps, CHUNK, LANES), f32),
            pltpu.VMEM((blocks, 2, 2, HALF, CHUNK, LANES), f32),
            pltpu.VMEM((2, levels, rows + 2, snaps, width), f32),
            pltpu.VMEM((blocks, 2, snaps, CHUNK, LANES), f32),
            pltpu.VMEM((cells, 1, width), f32),
            pltpu.VMEM((cells, 1, width), f32),
            pltpu.VMEM((rows, 1, width), f32),
            pltpu.VMEM((rows, 1, width), f32),
            pltpu.VMEM((n_tm, cells, 1, width), f32),
            pltpu.VMEM((snaps, LANES), f32),
            pltpu.VMEM((2, HALF, LANES), f32),
            pltpu.VMEM((snaps, LANES), f32),
            pltpu.VMEM((2, snaps, LANES), f32),
            pltpu.VMEM((2 * snaps, 2 * (snaps + HALF)), bf16),
            pltpu.VMEM((2 * snaps, 2 * HALF), bf16),
            pltpu.VMEM((cells, most, width), bf16),
            pltpu.VMEM((2, packs, HALF, LANES), f32),
            pltpu.VMEM((2, packs, HALF, LANES), f32),
            pltpu.VMEM((packs, HALF, LANES), f32),
            pltpu.VMEM((n_tile, 8, LANES), f32),
            dma((chunks,)),
            dma((chunks,)),
            dma((blocks, 2, 2)),
            dma((2,)),
            dma((chunks, 2)),
            dma((chunks, 2)),
            dma((2,)),
            dma((2,)),
            dma((2,)),
            dma((2,)),
            dma((chunks, n_tm)),
            dma((chunks, n_tm)),
            dma((n_tile,)),
            dma((n_tile,)),
        ],
        compiler_params=pltpu.CompilerParams(
            collective_id=0, has_side_effects=True, vmem_limit_bytes=60 * 1024 * 1024
        ),
        cost_estimate=pl.CostEstimate(flops=10**9, bytes_accessed=4 * 10**6, transcendentals=0),
    )(
        velocity_u, velocity_v, land_sea, bottom_level, spacing_x, spacing_y, own, halo,
    )


def shards(velocity_u, velocity_v, land_sea, bottom_level, spacing_x, spacing_y):
    snaps, levels, rows, width = velocity_u.shape
    cells = levels * rows
    n_tm = lax.axis_size("tm")
    assert width == 2 * LANES and 4 * cells == LANES and snaps == 2 * HALF
    assert rows % (2 * CHUNK) == 0 and levels == 2 and n_tm % 4 == 0 and n_tm >= 8
    own, halo = band_parts(snaps)
    args = (
        jnp.asarray(own), jnp.asarray(halo),
        velocity_u.reshape(snaps, cells, width), velocity_v.reshape(snaps, cells, width),
        land_sea, bottom_level, spacing_x, spacing_y,
    )
    conversion, mean_map, excess = quick(*args)
    conversion, mean_map = lax.cond(
        excess[0] > 0.0, lambda args, done: full(*args), lambda args, done: done, args, (conversion, mean_map)
    )
    conversion, mean_map = store(conversion, mean_map)
    return conversion.reshape(velocity_u.shape), mean_map


def store_kernel(a_ref, b_ref, a_out, b_out, sem):
    copies = [
        pltpu.make_async_copy(a_ref, a_out, sem.at[0]),
        pltpu.make_async_copy(b_ref, b_out, sem.at[1]),
    ]
    for copy in copies:
        copy.start()
    for copy in copies:
        copy.wait()


def store(a, b):
    place = pl.BlockSpec(memory_space=pl.ANY)
    return pl.pallas_call(
        store_kernel,
        out_shape=(jax.ShapeDtypeStruct(a.shape, a.dtype), jax.ShapeDtypeStruct(b.shape, b.dtype)),
        in_specs=[place, place],
        out_specs=(pl.BlockSpec(memory_space=pltpu.HBM), pl.BlockSpec(memory_space=pltpu.HBM)),
        scratch_shapes=[pltpu.SemaphoreType.DMA((2,))],
        name="store",
    )(a, b)


def solution(mesh):
    in_specs = (
        P("tm", None, None, "tile"),
        P("tm", None, None, "tile"),
        P(None, "tile"),
        P(None, "tile"),
        P(None, "tile"),
        P(None, "tile"),
    )
    out_specs = (P("tm", None, None, "tile"), P(None, None, "tile"))
    return jax.shard_map(shards, mesh=mesh, in_specs=in_specs, out_specs=out_specs, check_vma=False)
```

```python
import functools

import jax
import jax.numpy as jnp
import numpy as np
from jax import lax
from jax.experimental import pallas as pl
from jax.experimental.pallas import tpu as pltpu
from jax.sharding import PartitionSpec as P

HALF = 24
CUTOFF = 1.0 / 40.0
LANES = 128
CHUNK = 8
DEPTH = 2
AHEAD = 3
GROUP = 4
WINDOWS = (((0, 3), (0, 1)), ((1, 5), (1, 3)), ((3, 7), (5, 7)), ((5, 8), (7, 8)))
SPAN = 2 * GROUP
MESH = pl.DeviceIdType.MESH


def band_parts(count):
    offset = (np.arange(count + 2 * HALF)[None, :] - np.arange(count)[:, None] - HALF).astype(np.float64)
    weights = 2.0 * CUTOFF * np.sinc(2.0 * CUTOFF * offset) * np.sinc(offset / HALF)
    weights = np.where(np.abs(offset) <= HALF, weights, 0.0).astype(np.float32)
    own = weights[:, HALF : HALF + count]
    halo = np.concatenate([weights[:, :HALF], weights[:, HALF + count :]], axis=1)
    return own, halo


def dot(a, b):
    return jnp.dot(a, b, precision=lax.Precision.HIGHEST, preferred_element_type=jnp.float32)


def halves(a):
    high = a.astype(jnp.bfloat16).astype(jnp.float32)
    return high, a - high


def stacked_weights(w):
    high, low = halves(w)
    return jnp.concatenate(
        [jnp.concatenate([high, high], axis=1), jnp.concatenate([low, low], axis=1)], axis=0
    ).astype(jnp.bfloat16)


def split_dot(weights, pieces):
    split = [halves(p) for p in pieces]
    block = jnp.concatenate([s[0] for s in split] + [s[1] for s in split], axis=0).astype(jnp.bfloat16)
    both = jnp.dot(weights, block, preferred_element_type=jnp.float32)
    half = both.shape[0] // 2
    return both[:half] + both[half:]


def kernel(
    n_tm, n_tile, levels,
    u_ref, v_ref, land_in, bottom_in, sx_in, sy_in, own_in, halo_in,
    conv_ref, mean_ref,
    land_ref, bottom_ref, sx_ref, sy_ref, own_ref, halo_w_ref, small_sem,
    x, halo, mm, cf, wet, cx, cy, part, edge, edge_halo, edge_mean, edge_in,
    near_w, far_w, relayed, relay_send, relay_recv,
    x_sem, bulk_send, bulk_recv, edge_send, edge_recv, em_send, em_recv, part_send, part_recv,
):
    snaps, cells, width = u_ref.shape
    rows = cells // levels
    t = lax.axis_index("tm")
    z = lax.axis_index("tile")
    chunks = cells // CHUNK
    per_level = rows // CHUNK
    fields = (u_ref, v_ref)
    even = lax.rem(t, 2) == 0
    odd = jnp.logical_not(even)

    barrier = pltpu.get_barrier_semaphore()
    for k in range(1, n_tm):
        pl.semaphore_signal(barrier, inc=1, device_id={"tm": lax.rem(t + k, n_tm)}, device_id_type=MESH)

    @pl.when(z > 0)
    def _():
        pl.semaphore_signal(barrier, inc=1, device_id={"tile": z - 1}, device_id_type=MESH)

    @pl.when(z < n_tile - 1)
    def _():
        pl.semaphore_signal(barrier, inc=1, device_id={"tile": z + 1}, device_id_type=MESH)

    def local(c, f, h):
        return pltpu.make_async_copy(
            fields[f].at[:, pl.ds(c * CHUNK, CHUNK), pl.ds(h * LANES, LANES)], x.at[c, f, h], x_sem.at[c, f, h]
        )

    small = (
        (land_in, land_ref), (bottom_in, bottom_ref), (sx_in, sx_ref),
        (sy_in, sy_ref), (own_in, own_ref), (halo_in, halo_w_ref),
    )
    for i, (src, dst) in enumerate(small):
        pltpu.make_async_copy(src, dst, small_sem.at[i]).start()
    for c in range(chunks):
        for f in range(2):
            for h in range(2):
                local(c, f, h).start()

    def bulk(side, c, f, h):
        first = snaps - HALF if side == 0 else 0
        to = t + 1 if side == 0 else t - 1
        return pltpu.make_async_remote_copy(
            src_ref=fields[f].at[pl.ds(first, HALF), pl.ds(c * CHUNK, CHUNK), pl.ds(h * LANES, LANES)],
            dst_ref=halo.at[side, c, f, h],
            send_sem=bulk_send.at[side, c, f, h],
            recv_sem=bulk_recv.at[side, c, f, h],
            device_id={"tm": to},
            device_id_type=MESH,
        )

    middle = (n_tm // 2 - 1, n_tm // 2)
    via = (n_tm - 1, 0)

    def to_relay(side, c, h):
        first = snaps - HALF if side == 0 else 0
        return pltpu.make_async_remote_copy(
            src_ref=fields[1].at[pl.ds(first, HALF), pl.ds(c * CHUNK, CHUNK), pl.ds(h * LANES, LANES)],
            dst_ref=relayed.at[c, h],
            send_sem=bulk_send.at[side, c, 1, h],
            recv_sem=relay_recv.at[c, h],
            device_id={"tm": via[side]},
            device_id_type=MESH,
        )

    def from_relay(side, c, h):
        return pltpu.make_async_remote_copy(
            src_ref=relayed.at[c, h],
            dst_ref=halo.at[side, c, 1, h],
            send_sem=relay_send.at[c, h],
            recv_sem=bulk_recv.at[side, c, 1, h],
            device_id={"tm": middle[1 - side]},
            device_id_type=MESH,
        )

    def pass_on(c):
        if n_tm < 4:
            return
        for side in range(2):

            @pl.when(t == via[side])
            def _():
                for h in range(2):
                    to_relay(side, c, h).wait_recv()
                    from_relay(side, c, h).start()

    def edge_copy(side):
        first = snaps - HALF if side == 0 else 0
        to = t + 1 if side == 0 else t - 1
        return pltpu.make_async_remote_copy(
            src_ref=edge.at[pl.ds(first, HALF), :],
            dst_ref=edge_halo.at[side],
            send_sem=edge_send.at[side],
            recv_sem=edge_recv.at[side],
            device_id={"tm": to},
            device_id_type=MESH,
        )

    def mean_copy(side):
        to = z + 1 if side == 0 else z - 1
        return pltpu.make_async_remote_copy(
            src_ref=edge_mean,
            dst_ref=edge_in.at[side],
            send_sem=em_send.at[side],
            recv_sem=em_recv.at[side],
            device_id={"tile": to},
            device_id_type=MESH,
        )

    def converted(c):
        piece = c % per_level
        low = piece * CHUNK - (1 if piece else 0)
        high = rows if piece == per_level - 1 else (piece + 1) * CHUNK - 1
        return c // per_level, low, high

    def part_copy(c, k, slot):
        l, low, high = converted(c)
        return pltpu.make_async_remote_copy(
            src_ref=part.at[slot, pl.ds(l * rows + low, high - low)],
            dst_ref=part.at[slot, pl.ds(l * rows + low, high - low)],
            send_sem=part_send.at[c, k],
            recv_sem=part_recv.at[c, k],
            device_id={"tm": lax.rem(t + k, n_tm)},
            device_id_type=MESH,
        )

    sends = (t < n_tm - 1, t > 0)
    receives = (t > 0, t < n_tm - 1)
    send_near, send_far = (even, odd), (odd, even)
    near, far = (odd, even), (even, odd)
    z_sends = (z < n_tile - 1, z > 0)
    z_receives = (z > 0, z < n_tile - 1)

    def start_far(c):
        for side in range(2):
            if n_tm >= 4:

                @pl.when(t == middle[side])
                def _():
                    for h in range(2):
                        to_relay(side, c, h).start()
                        bulk(side, c, 0, h).start()

                whole = sends[side] & send_far[side] & (t != middle[side])
            else:
                whole = sends[side] & send_far[side]

            @pl.when(whole)
            def _():
                for f in range(2):
                    for h in range(2):
                        bulk(side, c, f, h).start()

    def finish_send(c, which):
        for side in range(2):

            @pl.when(sends[side] & which[side])
            def _():
                for f in range(2):
                    for h in range(2):
                        bulk(side, c, f, h).wait_send()

    pl.semaphore_wait(barrier, n_tm - 1 + (z > 0).astype(jnp.int32) + (z < n_tile - 1).astype(jnp.int32))

    for c in range(DEPTH):
        start_far(c)
    for side in range(2):

        @pl.when(sends[side] & send_near[side])
        def _():
            for c in range(chunks):
                for f in range(2):
                    for h in range(2):
                        bulk(side, c, f, h).start()

    for side in range(2):

        @pl.when(jnp.logical_not(receives[side]))
        def _():
            halo[side] = jnp.zeros(halo.shape[1:], jnp.float32)
            edge_halo[side] = jnp.zeros(edge_halo.shape[1:], jnp.float32)

        @pl.when(jnp.logical_not(z_receives[side]))
        def _():
            edge_in[side] = jnp.zeros(edge_in.shape[1:], jnp.float32)

    for i, (src, dst) in enumerate(small):
        pltpu.make_async_copy(src, dst, small_sem.at[i]).wait()

    for l in range(levels):
        is_wet = (land_ref[...] == 1) & (l < bottom_ref[...])
        level_wet = jnp.where(is_wet, 1.0, 0.0).astype(jnp.float32)
        for j in range(rows):
            wet[l * rows + j] = level_wet[j : j + 1, :]
    all_x, all_y = 0.5 / sx_ref[...], 0.5 / sy_ref[...]
    for j in range(rows):
        cx[j] = all_x[j : j + 1, :]
        cy[j] = all_y[j : j + 1, :]
    for f in range(2):
        for l in range(levels):
            for j in (0, rows + 1):
                mm[f, l, j] = jnp.zeros((snaps, width), jnp.float32)
    column = lax.broadcasted_iota(jnp.int32, (snaps, 2 * HALF), 1)
    valid = ((column >= HALF) | (t > 0)) & ((column < HALF) | (t < n_tm - 1))
    own_w = own_ref[...]
    halo_w = jnp.where(valid, halo_w_ref[...], 0.0)
    weight_sum = jnp.sum(own_w, axis=1, keepdims=True) + jnp.sum(halo_w, axis=1, keepdims=True)
    own_w = own_w / weight_sum
    halo_w = halo_w / weight_sum
    near_side = 1 - lax.rem(t, 2)
    far_side = lax.rem(t, 2)
    near_half = jnp.where(even, halo_w[:, HALF:], halo_w[:, :HALF])
    far_half = jnp.where(even, halo_w[:, :HALF], halo_w[:, HALF:])
    near_w[...] = stacked_weights(jnp.concatenate([own_w, near_half], axis=1))
    far_w[...] = stacked_weights(far_half)

    for c in range(chunks):
        for f in range(2):
            for h in range(2):
                local(c, f, h).wait()

    def series(ref, count, j):
        return ref.reshape(count * CHUNK, LANES)[pl.ds(j, count, stride=CHUNK), :]

    def both(ref, count, j):
        return jnp.concatenate([series(ref.at[h], count, j) for h in range(2)], axis=1)

    lane = lax.broadcasted_iota(jnp.int32, (snaps, LANES), 1)

    def pack(r, acc):
        c, j = r // CHUNK, lax.rem(r, CHUNK)
        for f in range(2):
            q = f * cells + r
            first = series(x.at[c, f, 0], snaps, j) * wet[r][:, :LANES]
            acc = jnp.where(lane == q, pltpu.roll(first, q, 1), acc)
            q = (2 + f) * cells + r
            last = series(x.at[c, f, 1], snaps, j) * wet[r][:, width - LANES :]
            acc = jnp.where(lane == q, pltpu.roll(last, lax.rem(q + 1, LANES), 1), acc)
        return acc

    edge[...] = lax.fori_loop(0, cells, pack, jnp.zeros((snaps, LANES), jnp.float32), unroll=4)
    for side in range(2):

        @pl.when(sends[side])
        def _():
            edge_copy(side).start()

    pass_on(0)

    for side in range(2):

        @pl.when(receives[side] & near[side])
        def _():
            for c in range(chunks):
                for f in range(2):
                    for h in range(2):
                        bulk(side, c, f, h).wait_recv()

    def near_part(r, carry):
        l, j = r // rows, lax.rem(r, rows)
        c, i = r // CHUNK, lax.rem(r, CHUNK)
        for f in range(2):
            pieces = [both(x.at[c, f], snaps, i), both(halo.at[near_side, c, f], HALF, i)]
            mm[f, l, j + 1] = split_dot(near_w[...], pieces)
        return carry

    lax.fori_loop(0, cells, near_part, 0, unroll=8)
    for c in range(1, DEPTH):
        pass_on(c)

    for side in range(2):

        @pl.when(receives[side])
        def _():
            edge_copy(side).wait_recv()

    edge_mean[...] = dot(own_w, edge[...]) + dot(
        halo_w, jnp.concatenate([edge_halo[0], edge_halo[1]], axis=0)
    )
    for side in range(2):

        @pl.when(z_sends[side])
        def _():
            mean_copy(side).start()

    wide = lax.broadcasted_iota(jnp.int32, (snaps, width), 1)

    def far_part(r, carry):
        l, j = r // rows, lax.rem(r, rows)
        c, i = r // CHUNK, lax.rem(r, CHUNK)
        mask = wet[r]
        for f in range(2):
            pieces = [both(halo.at[far_side, c, f], HALF, i)]
            mm[f, l, j + 1] = (mm[f, l, j + 1] + split_dot(far_w[...], pieces)) * mask
        return carry

    def grad_x(f, r, masked, scale):
        q = (2 + f) * cells + r
        before = pltpu.roll(edge_in[0], lax.rem(2 * LANES - q, LANES), 1)
        q = f * cells + r
        after = pltpu.roll(edge_in[1], lax.rem(2 * LANES - 1 - q, LANES), 1)
        before = jnp.concatenate([before, before], axis=1)
        after = jnp.concatenate([after, after], axis=1)
        behind = jnp.where(wide == 0, before, pltpu.roll(masked, 1, 1))
        ahead = jnp.where(wide == width - 1, after, pltpu.roll(masked, width - 1, 1))
        return (ahead - behind) * scale

    def convert(l):
        def body(j, carry):
            r = l * rows + j
            c, i = r // CHUNK, lax.rem(r, CHUNK)
            mask = wet[r]
            scale_x = cx[j]
            scale_y = cy[j]
            eddy, gx, gy = [], [], []
            for f in range(2):
                masked = mm[f, l, j + 1]
                eddy.append(both(x.at[c, f], snaps, i) - masked)
                gx.append(grad_x(f, r, masked, scale_x))
                gy.append((mm[f, l, j + 2] - mm[f, l, j]) * scale_y)
            eu, ev = eddy
            total = eu * eu * gx[0] + eu * ev * (gy[0] + gx[1]) + ev * ev * gy[1]
            conversion = -mask * total
            for h in range(2):
                cf.at[c, h].reshape(snaps * CHUNK, LANES)[pl.ds(i, snaps, stride=CHUNK), :] = conversion[
                    :, h * LANES : (h + 1) * LANES
                ]
            part[t, r] = jnp.sum(conversion, axis=0, keepdims=True)
            return carry

        return body

    for c in range(chunks):
        finish_send(c, send_far)
        if c + DEPTH < chunks:
            start_far(c + DEPTH)
        for side in range(2):

            @pl.when(receives[side] & far[side])
            def _():
                for f in range(2):
                    for h in range(2):
                        bulk(side, c, f, h).wait_recv()

        lax.fori_loop(c * CHUNK, (c + 1) * CHUNK, far_part, 0, unroll=8)
        if c + DEPTH < chunks:
            pass_on(c + DEPTH)
        if c == 0:
            for side in range(2):

                @pl.when(z_receives[side])
                def _():
                    mean_copy(side).wait_recv()

        l, low, high = converted(c)
        lax.fori_loop(low, high, convert(l), 0, unroll=2)
        for k in range(1, n_tm):
            part_copy(c, k, t).start()
        if c % per_level == per_level - 1:

            def narrow(s, carry):
                for h in range(2):
                    block = jnp.concatenate([cf[l * per_level + p, h, s] for p in range(per_level)], axis=0)
                    conv_ref[s, pl.ds(l * rows, rows), pl.ds(h * LANES, LANES)] = block.astype(jnp.bfloat16)
                return carry

            lax.fori_loop(0, snaps, narrow, 0, unroll=4)

    for c in range(chunks):
        for k in range(1, n_tm):
            part_copy(c, k, lax.rem(t + n_tm - k, n_tm)).wait_recv()
        l, low, high = converted(c)
        for j in range(low, high):
            total = part[0, l * rows + j]
            for s in range(1, n_tm):
                total = total + part[s, l * rows + j]
            mean_ref[l, j : j + 1, :] = total / (snaps * n_tm)

    for c in range(chunks):
        finish_send(c, send_near)
    for side in range(2):

        @pl.when(sends[side])
        def _():
            edge_copy(side).wait_send()

        @pl.when(z_sends[side])
        def _():
            mean_copy(side).wait_send()

        if n_tm >= 4:

            @pl.when(t == via[side])
            def _():
                for c in range(chunks):
                    for h in range(2):
                        from_relay(side, c, h).wait_send()

    for c in range(chunks):
        for k in range(1, n_tm):
            part_copy(c, k, t).wait_send()


def fast_kernel(
    n_tm, n_tile, levels,
    u_ref, v_ref, land_in, bottom_in, sx_in, sy_in, own_in, halo_in,
    conv_ref, mean_ref, flag_ref,
    land_ref, bottom_ref, sx_ref, sy_ref, own_ref, halo_w_ref, small_sem,
    x, near, mm, cf, wet, key, cx, cy, part, edge, edge_halo, edge_mean, edge_in,
    near_w, far_w, place, packed, far, relayed, flags, flags_in,
    relay_send, relay_recv, x_sem, near_sem, far_send, far_recv, edge_send, edge_recv, em_send, em_recv,
    part_send, part_recv, flag_send, flag_recv,
):
    snaps, cells, width = u_ref.shape
    rows = cells // levels
    t = lax.axis_index("tm")
    z = lax.axis_index("tile")
    blocks = cells // CHUNK
    per_level = rows // CHUNK
    chunks = rows // GROUP
    fields = (u_ref, v_ref)
    even = lax.rem(t, 2) == 0
    odd = jnp.logical_not(even)

    barrier = pltpu.get_barrier_semaphore()
    for k in range(1, n_tm):
        pl.semaphore_signal(barrier, inc=1, device_id={"tm": lax.rem(t + k, n_tm)}, device_id_type=MESH)
    @pl.when(z > 0)
    def _():
        pl.semaphore_signal(barrier, inc=1, device_id={"tile": z - 1}, device_id_type=MESH)

    @pl.when(z < n_tile - 1)
    def _():
        pl.semaphore_signal(barrier, inc=1, device_id={"tile": z + 1}, device_id_type=MESH)


    def local(c, f, h):
        return pltpu.make_async_copy(
            fields[f].at[:, pl.ds(c * CHUNK, CHUNK), pl.ds(h * LANES, LANES)], x.at[c, f, h], x_sem.at[c, f, h]
        )

    small = (
        (land_in, land_ref), (bottom_in, bottom_ref), (sx_in, sx_ref),
        (sy_in, sy_ref), (own_in, own_ref), (halo_in, halo_w_ref),
    )
    for i, (src, dst) in enumerate(small):
        pltpu.make_async_copy(src, dst, small_sem.at[i]).start()
    for p in range(per_level):
        for l in range(levels):
            for f in range(2):
                for h in range(2):
                    local(l * per_level + p, f, h).start()

    first_far = jnp.where(even, 0, snaps - HALF)
    first_near = jnp.where(even, snaps - HALF, 0)
    has_far = (t > 0) & (t < n_tm - 1)
    at_end = jnp.logical_not(has_far)
    is_middle = (t == n_tm // 2 - 1) | (t == n_tm // 2)
    far_to = jnp.where(even, t - 1, t + 1)
    via_to = jnp.where(t < n_tm // 2, n_tm - 1, 0)
    forward_to = jnp.where(t == 0, n_tm // 2 - 1, n_tm // 2)

    def tiles(c):
        return c * SPAN, SPAN

    def near_copy():
        return pltpu.make_async_remote_copy(
            src_ref=x.at[:, :, :, pl.ds(first_near, HALF)],
            dst_ref=near,
            send_sem=near_sem.at[0],
            recv_sem=near_sem.at[1],
            device_id={"tm": t + 1 - 2 * lax.rem(t, 2)},
            device_id_type=MESH,
        )

    def far_copy(c, f):
        start, count = tiles(c)
        return pltpu.make_async_remote_copy(
            src_ref=packed.at[f, pl.ds(start, count)],
            dst_ref=far.at[f, pl.ds(start, count)],
            send_sem=far_send.at[c, f],
            recv_sem=far_recv.at[c, f],
            device_id={"tm": far_to},
            device_id_type=MESH,
        )

    def to_relay(c):
        start, count = tiles(c)
        return pltpu.make_async_remote_copy(
            src_ref=packed.at[1, pl.ds(start, count)],
            dst_ref=relayed.at[pl.ds(start, count)],
            send_sem=far_send.at[c, 1],
            recv_sem=relay_recv.at[c],
            device_id={"tm": via_to},
            device_id_type=MESH,
        )

    def from_relay(c):
        start, count = tiles(c)
        return pltpu.make_async_remote_copy(
            src_ref=relayed.at[pl.ds(start, count)],
            dst_ref=far.at[1, pl.ds(start, count)],
            send_sem=relay_send.at[c],
            recv_sem=far_recv.at[c, 1],
            device_id={"tm": forward_to},
            device_id_type=MESH,
        )

    def pass_on(c):
        @pl.when(at_end)
        def _():
            to_relay(c).wait_recv()
            from_relay(c).start()

    def start_far(c):
        @pl.when(has_far)
        def _():
            far_copy(c, 0).start()

        @pl.when(is_middle)
        def _():
            to_relay(c).start()

        @pl.when(has_far & jnp.logical_not(is_middle))
        def _():
            far_copy(c, 1).start()

    def edge_copy(side):
        first = snaps - HALF if side == 0 else 0
        to = t + 1 if side == 0 else t - 1
        return pltpu.make_async_remote_copy(
            src_ref=edge.at[pl.ds(first, HALF), :],
            dst_ref=edge_halo.at[side],
            send_sem=edge_send.at[side],
            recv_sem=edge_recv.at[side],
            device_id={"tm": to},
            device_id_type=MESH,
        )

    def mean_copy(side):
        to = z + 1 if side == 0 else z - 1
        return pltpu.make_async_remote_copy(
            src_ref=edge_mean,
            dst_ref=edge_in.at[side],
            send_sem=em_send.at[side],
            recv_sem=em_recv.at[side],
            device_id={"tile": to},
            device_id_type=MESH,
        )

    def flag_copy(s, side):
        to = z + 1 if side == 0 else z - 1
        return pltpu.make_async_remote_copy(
            src_ref=flags.at[s],
            dst_ref=flags_in.at[side, s],
            send_sem=flag_send.at[s, side],
            recv_sem=flag_recv.at[s, side],
            device_id={"tile": to},
            device_id_type=MESH,
        )

    def start_flag(s):
        for side in range(2):

            @pl.when(z_sends[side])
            def _():
                flag_copy(s, side).start()

    def finish_flag(s):
        for side in range(2):

            @pl.when(z_receives[side])
            def _():
                flag_copy(s, side).wait_recv()

        flags[s + 1] = jnp.maximum(flags[s], jnp.maximum(flags_in[0, s], flags_in[1, s]))

    def converted(c):
        return c * GROUP - (1 if c else 0), rows if c == chunks - 1 else (c + 1) * GROUP - 1

    def part_copy(c, k, slot):
        low, high = converted(c)
        return pltpu.make_async_remote_copy(
            src_ref=part.at[slot, pl.ds(levels * low, levels * (high - low))],
            dst_ref=part.at[slot, pl.ds(levels * low, levels * (high - low))],
            send_sem=part_send.at[c, k],
            recv_sem=part_recv.at[c, k],
            device_id={"tm": lax.rem(t + k, n_tm)},
            device_id_type=MESH,
        )

    sends = (t < n_tm - 1, t > 0)
    receives = (t > 0, t < n_tm - 1)
    z_sends = (z < n_tile - 1, z > 0)
    z_receives = (z > 0, z < n_tile - 1)

    for i, (src, dst) in enumerate(small):
        pltpu.make_async_copy(src, dst, small_sem.at[i]).wait()

    levels_wet = []
    for l in range(levels):
        is_wet = (land_ref[...] == 1) & (l < bottom_ref[...])
        levels_wet.append(jnp.where(is_wet, 1.0, 0.0).astype(jnp.float32))
    all_wet = jnp.concatenate(levels_wet, axis=0)
    lower = lax.broadcasted_iota(jnp.int32, (width, width), 0)
    upper = lax.broadcasted_iota(jnp.int32, (width, width), 1)
    earlier = jnp.where(lower < upper, 1.0, 0.0).astype(jnp.bfloat16)

    def ranked(index):
        j = lax.rem(index, rows)
        side = lax.rem(j, GROUP) // 2
        inner = jnp.where(side == 0, lax.rem(j, 2), 1 - lax.rem(j, 2))
        return 2 * (j // GROUP) + side, 2 * inner + (1 - index // rows)

    set_a, rank_a = ranked(lax.broadcasted_iota(jnp.int32, (cells, cells), 0))
    set_b, rank_b = ranked(lax.broadcasted_iota(jnp.int32, (cells, cells), 1))
    ahead_rows = jnp.where((set_a == set_b) & (rank_b < rank_a), 1.0, 0.0).astype(jnp.bfloat16)
    same_rows = jnp.where((set_a // 2 == set_b // 2) & (set_a != set_b), 1.0, 0.0).astype(jnp.bfloat16)
    wet_bits = all_wet.astype(jnp.bfloat16)
    filled = jnp.dot(
        jnp.concatenate([ahead_rows, same_rows], axis=0), wet_bits, preferred_element_type=jnp.float32
    ).astype(jnp.bfloat16)
    every = jnp.ones((width, width), jnp.bfloat16)
    order = jnp.dot(wet_bits, earlier, preferred_element_type=jnp.float32) + jnp.dot(
        filled[:cells], every, preferred_element_type=jnp.float32
    )
    other = jnp.dot(filled[cells:], every, preferred_element_type=jnp.float32)
    row = lax.broadcasted_iota(jnp.int32, (cells, width), 0)
    right = lax.rem(lax.rem(row, rows), GROUP) >= 2
    spot = jnp.where(right, float(SPAN * LANES - 1) - order, order)
    first_lane = jnp.zeros((cells, width), jnp.float32)
    lanes_used = jnp.zeros((cells, width), jnp.float32)
    for q in range(GROUP):
        for l in range(levels):
            here = (lax.rem(lax.rem(row, rows), GROUP) == q) & (row // rows == l)
            low, high = WINDOWS[q][l]
            first_lane = jnp.where(here, float(low * LANES), first_lane)
            lanes_used = jnp.where(here, float((high - low) * LANES), lanes_used)
    spot = spot - first_lane
    fits = (spot >= 0.0) & (spot < lanes_used) & (order + other < float(SPAN * LANES))
    is_wet = all_wet > 0.0
    all_key = jnp.where(is_wet & fits, spot, -1.0)
    over = jnp.max(jnp.where(is_wet & jnp.logical_not(fits), 1.0, 0.0), axis=0, keepdims=True)
    flags[0] = jnp.broadcast_to(jnp.maximum(over[:, :LANES], over[:, LANES:]), (8, LANES))
    for r in range(cells):
        wet[r] = all_wet[r : r + 1, :]
        key[r] = all_key[r : r + 1, :]

    def series(ref, count, j):
        return ref.reshape(count * CHUNK, LANES)[pl.ds(j, count, stride=CHUNK), :]

    def both(ref, count, j):
        return jnp.concatenate([series(ref.at[h], count, j) for h in range(2)], axis=1)

    def members(c):
        for q in range(GROUP):
            for l in range(levels):
                low, high = WINDOWS[q][l]
                j = c * GROUP + q
                yield l * rows + j, l * per_level + j // CHUNK, j % CHUNK, low, high

    def put(r, size):
        index = lax.broadcasted_iota(jnp.int32, (size, width), 0).astype(jnp.float32)
        place[r, :size] = jnp.where(index == key[r], 1.0, 0.0).astype(jnp.bfloat16)

    def gather(r, b, i, size):
        split = []
        for f in range(2):
            block = [x.at[b, f, h].reshape(snaps * CHUNK, LANES) for h in range(2)]
            at = pl.ds(first_far * CHUNK + i, HALF, stride=CHUNK)
            split.extend(halves(jnp.concatenate([p[at, :] for p in block], axis=1)))
        split = jnp.concatenate(split, axis=0).astype(jnp.bfloat16)
        out = lax.dot_general(
            split, place[r, :size], (((1,), (1,)), ((), ())), preferred_element_type=jnp.float32
        )
        return [out[2 * f * HALF : (2 * f + 1) * HALF] + out[(2 * f + 1) * HALF : (2 * f + 2) * HALF] for f in range(2)]

    def compact(c):
        @pl.when(has_far)
        def _():
            compact_far(c)

    def compact_far(c):
        start, count = tiles(c)
        for r, _, _, low, high in members(c):
            put(r, (high - low) * LANES)
        sums = [[None] * count for f in range(2)]
        for r, b, i, low, high in members(c):
            values = gather(r, b, i, (high - low) * LANES)
            for f in range(2):
                for p in range(low, high):
                    piece = values[f][:, (p - low) * LANES : (p - low + 1) * LANES]
                    sums[f][p] = piece if sums[f][p] is None else sums[f][p] + piece
        for f in range(2):
            for p in range(count):
                packed[f, start + p] = sums[f][p]

    def wait_local(c):
        for f in range(2):
            for h in range(2):
                local(c, f, h).wait()

    for c in range(blocks):
        wait_local(c)
    lane = lax.broadcasted_iota(jnp.int32, (snaps, LANES), 1)

    def pack(r, acc):
        c, j = r // CHUNK, lax.rem(r, CHUNK)
        for f in range(2):
            q = f * cells + r
            first = series(x.at[c, f, 0], snaps, j) * wet[r][:, :LANES]
            acc = jnp.where(lane == q, pltpu.roll(first, q, 1), acc)
            q = (2 + f) * cells + r
            last = series(x.at[c, f, 1], snaps, j) * wet[r][:, width - LANES :]
            acc = jnp.where(lane == q, pltpu.roll(last, lax.rem(q + 1, LANES), 1), acc)
        return acc

    compact(0)
    pl.semaphore_wait(barrier, n_tm - 1 + jnp.where(z > 0, 1, 0) + jnp.where(z < n_tile - 1, 1, 0))
    start_far(0)
    edge[...] = lax.fori_loop(0, cells, pack, jnp.zeros((snaps, LANES), jnp.float32), unroll=4)
    for side in range(2):

        @pl.when(sends[side])
        def _():
            edge_copy(side).start()

    start_flag(0)
    near_copy().start()
    compact(1)
    start_far(1)
    for side in range(2):

        @pl.when(jnp.logical_not(receives[side]))
        def _():
            edge_halo[side] = jnp.zeros(edge_halo.shape[1:], jnp.float32)

        @pl.when(jnp.logical_not(z_receives[side]))
        def _():
            edge_in[side] = jnp.zeros(edge_in.shape[1:], jnp.float32)
            flags_in[side] = jnp.zeros(flags_in.shape[1:], jnp.float32)

    all_x, all_y = 0.5 / sx_ref[...], 0.5 / sy_ref[...]
    for j in range(rows):
        cx[j] = all_x[j : j + 1, :]
        cy[j] = all_y[j : j + 1, :]
    for f in range(2):
        for l in range(levels):
            for j in (0, rows + 1):
                mm[f, l, j] = jnp.zeros((snaps, width), jnp.float32)
    column = lax.broadcasted_iota(jnp.int32, (snaps, 2 * HALF), 1)
    valid = ((column >= HALF) | (t > 0)) & ((column < HALF) | (t < n_tm - 1))
    own_w = own_ref[...]
    halo_w = jnp.where(valid, halo_w_ref[...], 0.0)
    weight_sum = jnp.sum(own_w, axis=1, keepdims=True) + jnp.sum(halo_w, axis=1, keepdims=True)
    own_w = own_w / weight_sum
    halo_w = halo_w / weight_sum
    near_half = jnp.where(even, halo_w[:, HALF:], halo_w[:, :HALF])
    far_half = jnp.where(even, halo_w[:, :HALF], halo_w[:, HALF:])
    near_w[...] = stacked_weights(jnp.concatenate([own_w, near_half], axis=1))
    far_w[...] = stacked_weights(far_half)

    pass_on(0)
    for side in range(2):

        @pl.when(receives[side])
        def _():
            edge_copy(side).wait_recv()

    edge_mean[...] = dot(own_w, edge[...]) + dot(
        halo_w, jnp.concatenate([edge_halo[0], edge_halo[1]], axis=0)
    )
    for side in range(2):

        @pl.when(z_sends[side])
        def _():
            mean_copy(side).start()

    compact(2)
    start_far(2)
    def near_part(r, carry):
        l, j = r // rows, lax.rem(r, rows)
        c, i = r // CHUNK, lax.rem(r, CHUNK)
        for f in range(2):
            pieces = [both(x.at[c, f], snaps, i), both(near.at[c, f], HALF, i)]
            mm[f, l, j + 1] = split_dot(near_w[...], pieces)
        return carry

    if 0 < n_tile - 1:
        finish_flag(0)
    if 0 + 1 < n_tile - 1:
        start_flag(0 + 1)
    near_copy().wait_recv()
    lax.fori_loop(0, cells, near_part, 0, unroll=8)
    compact(3)
    pass_on(1)
    pass_on(2)
    wide = lax.broadcasted_iota(jnp.int32, (snaps, width), 1)

    def spread(r, blocks):
        l, j = r // rows, r % rows
        size = blocks[0].shape[1]
        split = []
        for block in blocks:
            split.extend(halves(block))
        out = jnp.dot(
            jnp.concatenate(split, axis=0).astype(jnp.bfloat16), place[r, :size], preferred_element_type=jnp.float32
        ).astype(jnp.bfloat16)
        mask = wet[r]
        for f in range(2):
            both_halves = jnp.dot(
                far_w[...], out[2 * f * HALF : 2 * (f + 1) * HALF], preferred_element_type=jnp.float32
            )
            mm[f, l, j + 1] = (mm[f, l, j + 1] + both_halves[:snaps] + both_halves[snaps:]) * mask

    def far_part(c):
        start, _ = tiles(c)

        @pl.when(has_far)
        def _():
            for f in range(2):
                far_copy(c, f).wait_recv()
            for r, _, _, low, high in members(c):
                spread(
                    r, [jnp.concatenate([far[f, start + p] for p in range(low, high)], axis=1) for f in range(2)]
                )

        @pl.when(at_end)
        def _():
            for r, _, _, _, _ in members(c):
                for f in range(2):
                    mm[f, r // rows, r % rows + 1] = mm[f, r // rows, r % rows + 1] * wet[r]

    wide = lax.broadcasted_iota(jnp.int32, (8, width), 1)

    def grad_x(f, r, now, masked, scale):
        q = (2 + f) * cells + r
        behind = pltpu.roll(edge_in[0, now, :], lax.rem(2 * LANES - q, LANES), 1)
        q = f * cells + r
        ahead = pltpu.roll(edge_in[1, now, :], lax.rem(2 * LANES - 1 - q, LANES), 1)
        behind = jnp.where(wide == 0, jnp.concatenate([behind, behind], axis=1), pltpu.roll(masked, 1, 1))
        ahead = jnp.where(wide == width - 1, jnp.concatenate([ahead, ahead], axis=1), pltpu.roll(masked, width - 1, 1))
        return (ahead - behind) * scale

    def convert(low, count):
        def body(q, carry):
            l, j = q // count, low + lax.rem(q, count)
            r = l * rows + j
            c, i = r // CHUNK, lax.rem(r, CHUNK)
            mask = -wet[r]
            scale_x = cx[j]
            scale_y = cy[j]
            kept = jnp.zeros((CHUNK, width), jnp.float32)
            for first in range(0, snaps, 8):
                now = pl.ds(first, 8)
                at = pl.ds(first * CHUNK + i, 8, stride=CHUNK)
                eddy, gx, gy = [], [], []
                for f in range(2):
                    masked = mm[f, l, j + 1, now, :]
                    raw = [x.at[c, f, h].reshape(snaps * CHUNK, LANES)[at, :] for h in range(2)]
                    eddy.append(jnp.concatenate(raw, axis=1) - masked)
                    gx.append(grad_x(f, r, now, masked, scale_x))
                    gy.append((mm[f, l, j + 2, now, :] - mm[f, l, j, now, :]) * scale_y)
                eu, ev = eddy
                total = eu * eu * gx[0] + eu * ev * (gy[0] + gx[1]) + ev * ev * gy[1]
                conversion = mask * total
                for h in range(2):
                    cf.at[c, h].reshape(snaps * CHUNK, LANES)[at, :] = conversion[:, h * LANES : (h + 1) * LANES]
                for k in range(0, 8, CHUNK):
                    kept = kept + conversion[k : k + CHUNK]
            part[t, levels * j + l] = jnp.sum(kept, axis=0, keepdims=True)
            return carry

        return body

    def finish(c):
        for k in range(1, n_tm):
            part_copy(c, k, lax.rem(t + n_tm - k, n_tm)).wait_recv()
        low, high = converted(c)
        for j in range(low, high):
            for l in range(levels):
                total = part[0, levels * j + l]
                for s in range(1, n_tm):
                    total = total + part[s, levels * j + l]
                mean_ref[l, j : j + 1, :] = total / (snaps * n_tm)

    if 1 < n_tile - 1:
        finish_flag(1)
    if 1 + 1 < n_tile - 1:
        start_flag(1 + 1)
    for c in range(chunks):
        @pl.when(has_far)
        def _():
            for f in range(2):
                far_copy(c, f).wait_send()

        if c + AHEAD < chunks:
            start_far(c + AHEAD)

        far_part(c)
        if c + AHEAD < chunks:
            pass_on(c + AHEAD)
        if c == 0:
            for side in range(2):

                @pl.when(z_receives[side])
                def _():
                    mean_copy(side).wait_recv()

        low, high = converted(c)
        lax.fori_loop(0, levels * (high - low), convert(low, high - low), 0, unroll=2 * (high - low))
        for k in range(1, n_tm):
            part_copy(c, k, t).start()

    def narrow(s, carry):
        for l in range(levels):
            for h in range(2):
                block = jnp.concatenate([cf[l * per_level + p, h, s] for p in range(per_level)], axis=0)
                conv_ref[s, pl.ds(l * rows, rows), pl.ds(h * LANES, LANES)] = block.astype(jnp.bfloat16)
        return carry

    lax.fori_loop(0, snaps, narrow, 0, unroll=4)
    for s in range(2, n_tile - 1):
        finish_flag(s)
        if s + 1 < n_tile - 1:
            start_flag(s + 1)
    flag_ref[0] = jnp.max(flags[n_tile - 1])
    for c in range(chunks):
        finish(c)

    near_copy().wait_send()
    for side in range(2):

        @pl.when(sends[side])
        def _():
            edge_copy(side).wait_send()

        @pl.when(z_sends[side])
        def _():
            mean_copy(side).wait_send()

    @pl.when(at_end)
    def _():
        for c in range(chunks):
            from_relay(c).wait_send()

    for s in range(n_tile - 1):
        for side in range(2):

            @pl.when(z_sends[side])
            def _():
                flag_copy(s, side).wait_send()

    for c in range(chunks):
        for k in range(1, n_tm):
            part_copy(c, k, t).wait_send()


def full(own, halo, velocity_u, velocity_v, land_sea, bottom_level, spacing_x, spacing_y):
    snaps, cells, width = velocity_u.shape
    rows = land_sea.shape[0]
    levels = cells // rows
    n_tm, n_tile = lax.axis_size("tm"), lax.axis_size("tile")
    chunks = cells // CHUNK
    vmem = pl.BlockSpec(memory_space=pltpu.VMEM)
    hbm = pl.BlockSpec(memory_space=pltpu.HBM)
    f32, bf16 = jnp.float32, jnp.bfloat16
    dma = pltpu.SemaphoreType.DMA
    return pl.pallas_call(
        functools.partial(kernel, n_tm, n_tile, levels),
        out_shape=(
            jax.ShapeDtypeStruct((snaps, cells, width), bf16),
            jax.ShapeDtypeStruct((levels, rows, width), f32),
        ),
        in_specs=[hbm] * 8,
        out_specs=(vmem, vmem),
        scratch_shapes=[
            pltpu.VMEM((rows, width), jnp.int32),
            pltpu.VMEM((rows, width), jnp.int32),
            pltpu.VMEM((rows, width), f32),
            pltpu.VMEM((rows, width), f32),
            pltpu.VMEM(own.shape, f32),
            pltpu.VMEM(halo.shape, f32),
            dma((6,)),
            pltpu.VMEM((chunks, 2, 2, snaps, CHUNK, LANES), f32),
            pltpu.VMEM((2, chunks, 2, 2, HALF, CHUNK, LANES), f32),
            pltpu.VMEM((2, levels, rows + 2, snaps, width), f32),
            pltpu.VMEM((chunks, 2, snaps, CHUNK, LANES), f32),
            pltpu.VMEM((cells, 1, width), f32),
            pltpu.VMEM((rows, 1, width), f32),
            pltpu.VMEM((rows, 1, width), f32),
            pltpu.VMEM((n_tm, cells, 1, width), f32),
            pltpu.VMEM((snaps, LANES), f32),
            pltpu.VMEM((2, HALF, LANES), f32),
            pltpu.VMEM((snaps, LANES), f32),
            pltpu.VMEM((2, snaps, LANES), f32),
            pltpu.VMEM((2 * snaps, 2 * (snaps + HALF)), bf16),
            pltpu.VMEM((2 * snaps, 2 * HALF), bf16),
            pltpu.VMEM((chunks, 2, HALF, CHUNK, LANES), f32),
            dma((chunks, 2)),
            dma((chunks, 2)),
            dma((chunks, 2, 2)),
            dma((2, chunks, 2, 2)),
            dma((2, chunks, 2, 2)),
            dma((2,)),
            dma((2,)),
            dma((2,)),
            dma((2,)),
            dma((chunks, n_tm)),
            dma((chunks, n_tm)),
        ],
        compiler_params=pltpu.CompilerParams(
            collective_id=1, has_side_effects=True, vmem_limit_bytes=60 * 1024 * 1024
        ),
        cost_estimate=pl.CostEstimate(flops=10**9, bytes_accessed=4 * 10**6, transcendentals=0),
    )(
        velocity_u, velocity_v, land_sea, bottom_level, spacing_x, spacing_y, own, halo,
    )


def quick(own, halo, velocity_u, velocity_v, land_sea, bottom_level, spacing_x, spacing_y):
    snaps, cells, width = velocity_u.shape
    rows = land_sea.shape[0]
    levels = cells // rows
    n_tm, n_tile = lax.axis_size("tm"), lax.axis_size("tile")
    blocks = cells // CHUNK
    chunks = rows // GROUP
    packs = chunks * SPAN
    most = max(high - low for pair in WINDOWS for low, high in pair) * LANES
    vmem = pl.BlockSpec(memory_space=pltpu.VMEM)
    hbm = pl.BlockSpec(memory_space=pltpu.HBM)
    f32, bf16 = jnp.float32, jnp.bfloat16
    dma = pltpu.SemaphoreType.DMA
    return pl.pallas_call(
        functools.partial(fast_kernel, n_tm, n_tile, levels),
        out_shape=(
            jax.ShapeDtypeStruct((snaps, cells, width), bf16),
            jax.ShapeDtypeStruct((levels, rows, width), f32),
            jax.ShapeDtypeStruct((1,), f32),
        ),
        in_specs=[hbm] * 8,
        out_specs=(vmem, vmem, pl.BlockSpec(memory_space=pltpu.SMEM)),
        scratch_shapes=[
            pltpu.VMEM((rows, width), jnp.int32),
            pltpu.VMEM((rows, width), jnp.int32),
            pltpu.VMEM((rows, width), f32),
            pltpu.VMEM((rows, width), f32),
            pltpu.VMEM(own.shape, f32),
            pltpu.VMEM(halo.shape, f32),
            dma((6,)),
            pltpu.VMEM((blocks, 2, 2, snaps, CHUNK, LANES), f32),
            pltpu.VMEM((blocks, 2, 2, HALF, CHUNK, LANES), f32),
            pltpu.VMEM((2, levels, rows + 2, snaps, width), f32),
            pltpu.VMEM((blocks, 2, snaps, CHUNK, LANES), f32),
            pltpu.VMEM((cells, 1, width), f32),
            pltpu.VMEM((cells, 1, width), f32),
            pltpu.VMEM((rows, 1, width), f32),
            pltpu.VMEM((rows, 1, width), f32),
            pltpu.VMEM((n_tm, cells, 1, width), f32),
            pltpu.VMEM((snaps, LANES), f32),
            pltpu.VMEM((2, HALF, LANES), f32),
            pltpu.VMEM((snaps, LANES), f32),
            pltpu.VMEM((2, snaps, LANES), f32),
            pltpu.VMEM((2 * snaps, 2 * (snaps + HALF)), bf16),
            pltpu.VMEM((2 * snaps, 2 * HALF), bf16),
            pltpu.VMEM((cells, most, width), bf16),
            pltpu.VMEM((2, packs, HALF, LANES), f32),
            pltpu.VMEM((2, packs, HALF, LANES), f32),
            pltpu.VMEM((packs, HALF, LANES), f32),
            pltpu.VMEM((n_tile, 8, LANES), f32),
            pltpu.VMEM((2, n_tile - 1, 8, LANES), f32),
            dma((chunks,)),
            dma((chunks,)),
            dma((blocks, 2, 2)),
            dma((2,)),
            dma((chunks, 2)),
            dma((chunks, 2)),
            dma((2,)),
            dma((2,)),
            dma((2,)),
            dma((2,)),
            dma((chunks, n_tm)),
            dma((chunks, n_tm)),
            dma((n_tile - 1, 2)),
            dma((n_tile - 1, 2)),
        ],
        compiler_params=pltpu.CompilerParams(
            collective_id=0, has_side_effects=True, vmem_limit_bytes=60 * 1024 * 1024
        ),
        cost_estimate=pl.CostEstimate(flops=10**9, bytes_accessed=4 * 10**6, transcendentals=0),
    )(
        velocity_u, velocity_v, land_sea, bottom_level, spacing_x, spacing_y, own, halo,
    )


def shards(velocity_u, velocity_v, land_sea, bottom_level, spacing_x, spacing_y):
    snaps, levels, rows, width = velocity_u.shape
    cells = levels * rows
    n_tm = lax.axis_size("tm")
    assert width == 2 * LANES and 4 * cells == LANES and snaps == 2 * HALF
    assert rows % (2 * CHUNK) == 0 and levels == 2 and n_tm % 4 == 0 and n_tm >= 8
    own, halo = band_parts(snaps)
    args = (
        jnp.asarray(own), jnp.asarray(halo),
        velocity_u.reshape(snaps, cells, width), velocity_v.reshape(snaps, cells, width),
        land_sea, bottom_level, spacing_x, spacing_y,
    )
    conversion, mean_map, excess = quick(*args)
    conversion, mean_map = lax.cond(
        excess[0] > 0.0, lambda args, done: full(*args), lambda args, done: done, args, (conversion, mean_map)
    )
    conversion, mean_map = store(conversion, mean_map)
    return conversion.reshape(velocity_u.shape), mean_map


def store_kernel(a_ref, b_ref, a_out, b_out, sem):
    copies = [
        pltpu.make_async_copy(a_ref, a_out, sem.at[0]),
        pltpu.make_async_copy(b_ref, b_out, sem.at[1]),
    ]
    for copy in copies:
        copy.start()
    for copy in copies:
        copy.wait()


def store(a, b):
    place = pl.BlockSpec(memory_space=pl.ANY)
    return pl.pallas_call(
        store_kernel,
        out_shape=(jax.ShapeDtypeStruct(a.shape, a.dtype), jax.ShapeDtypeStruct(b.shape, b.dtype)),
        in_specs=[place, place],
        out_specs=(pl.BlockSpec(memory_space=pltpu.HBM), pl.BlockSpec(memory_space=pltpu.HBM)),
        scratch_shapes=[pltpu.SemaphoreType.DMA((2,))],
        name="store",
    )(a, b)


def solution(mesh):
    in_specs = (
        P("tm", None, None, "tile"),
        P("tm", None, None, "tile"),
        P(None, "tile"),
        P(None, "tile"),
        P(None, "tile"),
        P(None, "tile"),
    )
    out_specs = (P("tm", None, None, "tile"), P(None, None, "tile"))
    return jax.shard_map(shards, mesh=mesh, in_specs=in_specs, out_specs=out_specs, check_vma=False)
```

```python
import functools

import jax
import jax.numpy as jnp
import numpy as np
from jax import lax
from jax.experimental import pallas as pl
from jax.experimental.pallas import tpu as pltpu
from jax.sharding import PartitionSpec as P

HALF = 24
CUTOFF = 1.0 / 40.0
LANES = 128
CHUNK = 8
DEPTH = 2
AHEAD = 3
GROUP = 4
WINDOWS = (((0, 3), (0, 1)), ((1, 5), (1, 3)), ((3, 7), (5, 7)), ((5, 8), (7, 8)))
SPAN = 2 * GROUP
MESH = pl.DeviceIdType.MESH


def band_parts(count):
    offset = (np.arange(count + 2 * HALF)[None, :] - np.arange(count)[:, None] - HALF).astype(np.float64)
    weights = 2.0 * CUTOFF * np.sinc(2.0 * CUTOFF * offset) * np.sinc(offset / HALF)
    weights = np.where(np.abs(offset) <= HALF, weights, 0.0).astype(np.float32)
    own = weights[:, HALF : HALF + count]
    halo = np.concatenate([weights[:, :HALF], weights[:, HALF + count :]], axis=1)
    return own, halo


def dot(a, b):
    return jnp.dot(a, b, precision=lax.Precision.HIGHEST, preferred_element_type=jnp.float32)


def halves(a):
    high = a.astype(jnp.bfloat16).astype(jnp.float32)
    return high, a - high


def stacked_weights(w):
    high, low = halves(w)
    return jnp.concatenate(
        [jnp.concatenate([high, high], axis=1), jnp.concatenate([low, low], axis=1)], axis=0
    ).astype(jnp.bfloat16)


def split_dot(weights, pieces):
    split = [halves(p) for p in pieces]
    block = jnp.concatenate([s[0] for s in split] + [s[1] for s in split], axis=0).astype(jnp.bfloat16)
    both = jnp.dot(weights, block, preferred_element_type=jnp.float32)
    half = both.shape[0] // 2
    return both[:half] + both[half:]


def kernel(
    n_tm, n_tile, levels,
    u_ref, v_ref, land_in, bottom_in, sx_in, sy_in, own_in, halo_in,
    conv_ref, mean_ref,
    land_ref, bottom_ref, sx_ref, sy_ref, own_ref, halo_w_ref, small_sem,
    x, halo, mm, cf, wet, cx, cy, part, edge, edge_halo, edge_mean, edge_in,
    near_w, far_w, relayed, relay_send, relay_recv,
    x_sem, bulk_send, bulk_recv, edge_send, edge_recv, em_send, em_recv, part_send, part_recv,
):
    snaps, cells, width = u_ref.shape
    rows = cells // levels
    t = lax.axis_index("tm")
    z = lax.axis_index("tile")
    chunks = cells // CHUNK
    per_level = rows // CHUNK
    fields = (u_ref, v_ref)
    even = lax.rem(t, 2) == 0
    odd = jnp.logical_not(even)

    barrier = pltpu.get_barrier_semaphore()
    for k in range(1, n_tm):
        pl.semaphore_signal(barrier, inc=1, device_id={"tm": lax.rem(t + k, n_tm)}, device_id_type=MESH)

    @pl.when(z > 0)
    def _():
        pl.semaphore_signal(barrier, inc=1, device_id={"tile": z - 1}, device_id_type=MESH)

    @pl.when(z < n_tile - 1)
    def _():
        pl.semaphore_signal(barrier, inc=1, device_id={"tile": z + 1}, device_id_type=MESH)

    def local(c, f, h):
        return pltpu.make_async_copy(
            fields[f].at[:, pl.ds(c * CHUNK, CHUNK), pl.ds(h * LANES, LANES)], x.at[c, f, h], x_sem.at[c, f, h]
        )

    small = (
        (land_in, land_ref), (bottom_in, bottom_ref), (sx_in, sx_ref),
        (sy_in, sy_ref), (own_in, own_ref), (halo_in, halo_w_ref),
    )
    for i, (src, dst) in enumerate(small):
        pltpu.make_async_copy(src, dst, small_sem.at[i]).start()
    for c in range(chunks):
        for f in range(2):
            for h in range(2):
                local(c, f, h).start()

    def bulk(side, c, f, h):
        first = snaps - HALF if side == 0 else 0
        to = t + 1 if side == 0 else t - 1
        return pltpu.make_async_remote_copy(
            src_ref=fields[f].at[pl.ds(first, HALF), pl.ds(c * CHUNK, CHUNK), pl.ds(h * LANES, LANES)],
            dst_ref=halo.at[side, c, f, h],
            send_sem=bulk_send.at[side, c, f, h],
            recv_sem=bulk_recv.at[side, c, f, h],
            device_id={"tm": to},
            device_id_type=MESH,
        )

    middle = (n_tm // 2 - 1, n_tm // 2)
    via = (n_tm - 1, 0)

    def to_relay(side, c, h):
        first = snaps - HALF if side == 0 else 0
        return pltpu.make_async_remote_copy(
            src_ref=fields[1].at[pl.ds(first, HALF), pl.ds(c * CHUNK, CHUNK), pl.ds(h * LANES, LANES)],
            dst_ref=relayed.at[c, h],
            send_sem=bulk_send.at[side, c, 1, h],
            recv_sem=relay_recv.at[c, h],
            device_id={"tm": via[side]},
            device_id_type=MESH,
        )

    def from_relay(side, c, h):
        return pltpu.make_async_remote_copy(
            src_ref=relayed.at[c, h],
            dst_ref=halo.at[side, c, 1, h],
            send_sem=relay_send.at[c, h],
            recv_sem=bulk_recv.at[side, c, 1, h],
            device_id={"tm": middle[1 - side]},
            device_id_type=MESH,
        )

    def pass_on(c):
        if n_tm < 4:
            return
        for side in range(2):

            @pl.when(t == via[side])
            def _():
                for h in range(2):
                    to_relay(side, c, h).wait_recv()
                    from_relay(side, c, h).start()

    def edge_copy(side):
        first = snaps - HALF if side == 0 else 0
        to = t + 1 if side == 0 else t - 1
        return pltpu.make_async_remote_copy(
            src_ref=edge.at[pl.ds(first, HALF), :],
            dst_ref=edge_halo.at[side],
            send_sem=edge_send.at[side],
            recv_sem=edge_recv.at[side],
            device_id={"tm": to},
            device_id_type=MESH,
        )

    def mean_copy(side):
        to = z + 1 if side == 0 else z - 1
        return pltpu.make_async_remote_copy(
            src_ref=edge_mean,
            dst_ref=edge_in.at[side],
            send_sem=em_send.at[side],
            recv_sem=em_recv.at[side],
            device_id={"tile": to},
            device_id_type=MESH,
        )

    def converted(c):
        piece = c % per_level
        low = piece * CHUNK - (1 if piece else 0)
        high = rows if piece == per_level - 1 else (piece + 1) * CHUNK - 1
        return c // per_level, low, high

    def part_copy(c, k, slot):
        l, low, high = converted(c)
        return pltpu.make_async_remote_copy(
            src_ref=part.at[slot, pl.ds(l * rows + low, high - low)],
            dst_ref=part.at[slot, pl.ds(l * rows + low, high - low)],
            send_sem=part_send.at[c, k],
            recv_sem=part_recv.at[c, k],
            device_id={"tm": lax.rem(t + k, n_tm)},
            device_id_type=MESH,
        )

    sends = (t < n_tm - 1, t > 0)
    receives = (t > 0, t < n_tm - 1)
    send_near, send_far = (even, odd), (odd, even)
    near, far = (odd, even), (even, odd)
    z_sends = (z < n_tile - 1, z > 0)
    z_receives = (z > 0, z < n_tile - 1)

    def start_far(c):
        for side in range(2):
            if n_tm >= 4:

                @pl.when(t == middle[side])
                def _():
                    for h in range(2):
                        to_relay(side, c, h).start()
                        bulk(side, c, 0, h).start()

                whole = sends[side] & send_far[side] & (t != middle[side])
            else:
                whole = sends[side] & send_far[side]

            @pl.when(whole)
            def _():
                for f in range(2):
                    for h in range(2):
                        bulk(side, c, f, h).start()

    def finish_send(c, which):
        for side in range(2):

            @pl.when(sends[side] & which[side])
            def _():
                for f in range(2):
                    for h in range(2):
                        bulk(side, c, f, h).wait_send()

    pl.semaphore_wait(barrier, n_tm - 1 + (z > 0).astype(jnp.int32) + (z < n_tile - 1).astype(jnp.int32))

    for c in range(DEPTH):
        start_far(c)
    for side in range(2):

        @pl.when(sends[side] & send_near[side])
        def _():
            for c in range(chunks):
                for f in range(2):
                    for h in range(2):
                        bulk(side, c, f, h).start()

    for side in range(2):

        @pl.when(jnp.logical_not(receives[side]))
        def _():
            halo[side] = jnp.zeros(halo.shape[1:], jnp.float32)
            edge_halo[side] = jnp.zeros(edge_halo.shape[1:], jnp.float32)

        @pl.when(jnp.logical_not(z_receives[side]))
        def _():
            edge_in[side] = jnp.zeros(edge_in.shape[1:], jnp.float32)

    for i, (src, dst) in enumerate(small):
        pltpu.make_async_copy(src, dst, small_sem.at[i]).wait()

    for l in range(levels):
        is_wet = (land_ref[...] == 1) & (l < bottom_ref[...])
        level_wet = jnp.where(is_wet, 1.0, 0.0).astype(jnp.float32)
        for j in range(rows):
            wet[l * rows + j] = level_wet[j : j + 1, :]
    all_x, all_y = 0.5 / sx_ref[...], 0.5 / sy_ref[...]
    for j in range(rows):
        cx[j] = all_x[j : j + 1, :]
        cy[j] = all_y[j : j + 1, :]
    for f in range(2):
        for l in range(levels):
            for j in (0, rows + 1):
                mm[f, l, j] = jnp.zeros((snaps, width), jnp.float32)
    column = lax.broadcasted_iota(jnp.int32, (snaps, 2 * HALF), 1)
    valid = ((column >= HALF) | (t > 0)) & ((column < HALF) | (t < n_tm - 1))
    own_w = own_ref[...]
    halo_w = jnp.where(valid, halo_w_ref[...], 0.0)
    weight_sum = jnp.sum(own_w, axis=1, keepdims=True) + jnp.sum(halo_w, axis=1, keepdims=True)
    own_w = own_w / weight_sum
    halo_w = halo_w / weight_sum
    near_side = 1 - lax.rem(t, 2)
    far_side = lax.rem(t, 2)
    near_half = jnp.where(even, halo_w[:, HALF:], halo_w[:, :HALF])
    far_half = jnp.where(even, halo_w[:, :HALF], halo_w[:, HALF:])
    near_w[...] = stacked_weights(jnp.concatenate([own_w, near_half], axis=1))
    far_w[...] = stacked_weights(far_half)

    for c in range(chunks):
        for f in range(2):
            for h in range(2):
                local(c, f, h).wait()

    def series(ref, count, j):
        return ref.reshape(count * CHUNK, LANES)[pl.ds(j, count, stride=CHUNK), :]

    def both(ref, count, j):
        return jnp.concatenate([series(ref.at[h], count, j) for h in range(2)], axis=1)

    lane = lax.broadcasted_iota(jnp.int32, (snaps, LANES), 1)

    def pack(r, acc):
        c, j = r // CHUNK, lax.rem(r, CHUNK)
        for f in range(2):
            q = f * cells + r
            first = series(x.at[c, f, 0], snaps, j) * wet[r][:, :LANES]
            acc = jnp.where(lane == q, pltpu.roll(first, q, 1), acc)
            q = (2 + f) * cells + r
            last = series(x.at[c, f, 1], snaps, j) * wet[r][:, width - LANES :]
            acc = jnp.where(lane == q, pltpu.roll(last, lax.rem(q + 1, LANES), 1), acc)
        return acc

    edge[...] = lax.fori_loop(0, cells, pack, jnp.zeros((snaps, LANES), jnp.float32), unroll=4)
    for side in range(2):

        @pl.when(sends[side])
        def _():
            edge_copy(side).start()

    pass_on(0)

    for side in range(2):

        @pl.when(receives[side] & near[side])
        def _():
            for c in range(chunks):
                for f in range(2):
                    for h in range(2):
                        bulk(side, c, f, h).wait_recv()

    def near_part(r, carry):
        l, j = r // rows, lax.rem(r, rows)
        c, i = r // CHUNK, lax.rem(r, CHUNK)
        for f in range(2):
            pieces = [both(x.at[c, f], snaps, i), both(halo.at[near_side, c, f], HALF, i)]
            mm[f, l, j + 1] = split_dot(near_w[...], pieces)
        return carry

    lax.fori_loop(0, cells, near_part, 0, unroll=8)
    for c in range(1, DEPTH):
        pass_on(c)

    for side in range(2):

        @pl.when(receives[side])
        def _():
            edge_copy(side).wait_recv()

    edge_mean[...] = dot(own_w, edge[...]) + dot(
        halo_w, jnp.concatenate([edge_halo[0], edge_halo[1]], axis=0)
    )
    for side in range(2):

        @pl.when(z_sends[side])
        def _():
            mean_copy(side).start()

    wide = lax.broadcasted_iota(jnp.int32, (snaps, width), 1)

    def far_part(r, carry):
        l, j = r // rows, lax.rem(r, rows)
        c, i = r // CHUNK, lax.rem(r, CHUNK)
        mask = wet[r]
        for f in range(2):
            pieces = [both(halo.at[far_side, c, f], HALF, i)]
            mm[f, l, j + 1] = (mm[f, l, j + 1] + split_dot(far_w[...], pieces)) * mask
        return carry

    def grad_x(f, r, masked, scale):
        q = (2 + f) * cells + r
        before = pltpu.roll(edge_in[0], lax.rem(2 * LANES - q, LANES), 1)
        q = f * cells + r
        after = pltpu.roll(edge_in[1], lax.rem(2 * LANES - 1 - q, LANES), 1)
        before = jnp.concatenate([before, before], axis=1)
        after = jnp.concatenate([after, after], axis=1)
        behind = jnp.where(wide == 0, before, pltpu.roll(masked, 1, 1))
        ahead = jnp.where(wide == width - 1, after, pltpu.roll(masked, width - 1, 1))
        return (ahead - behind) * scale

    def convert(l):
        def body(j, carry):
            r = l * rows + j
            c, i = r // CHUNK, lax.rem(r, CHUNK)
            mask = wet[r]
            scale_x = cx[j]
            scale_y = cy[j]
            eddy, gx, gy = [], [], []
            for f in range(2):
                masked = mm[f, l, j + 1]
                eddy.append(both(x.at[c, f], snaps, i) - masked)
                gx.append(grad_x(f, r, masked, scale_x))
                gy.append((mm[f, l, j + 2] - mm[f, l, j]) * scale_y)
            eu, ev = eddy
            total = eu * eu * gx[0] + eu * ev * (gy[0] + gx[1]) + ev * ev * gy[1]
            conversion = -mask * total
            for h in range(2):
                cf.at[c, h].reshape(snaps * CHUNK, LANES)[pl.ds(i, snaps, stride=CHUNK), :] = conversion[
                    :, h * LANES : (h + 1) * LANES
                ]
            part[t, r] = jnp.sum(conversion, axis=0, keepdims=True)
            return carry

        return body

    for c in range(chunks):
        finish_send(c, send_far)
        if c + DEPTH < chunks:
            start_far(c + DEPTH)
        for side in range(2):

            @pl.when(receives[side] & far[side])
            def _():
                for f in range(2):
                    for h in range(2):
                        bulk(side, c, f, h).wait_recv()

        lax.fori_loop(c * CHUNK, (c + 1) * CHUNK, far_part, 0, unroll=8)
        if c + DEPTH < chunks:
            pass_on(c + DEPTH)
        if c == 0:
            for side in range(2):

                @pl.when(z_receives[side])
                def _():
                    mean_copy(side).wait_recv()

        l, low, high = converted(c)
        lax.fori_loop(low, high, convert(l), 0, unroll=2)
        for k in range(1, n_tm):
            part_copy(c, k, t).start()
        if c % per_level == per_level - 1:

            def narrow(s, carry):
                for h in range(2):
                    block = jnp.concatenate([cf[l * per_level + p, h, s] for p in range(per_level)], axis=0)
                    conv_ref[s, pl.ds(l * rows, rows), pl.ds(h * LANES, LANES)] = block.astype(jnp.bfloat16)
                return carry

            lax.fori_loop(0, snaps, narrow, 0, unroll=4)

    for c in range(chunks):
        for k in range(1, n_tm):
            part_copy(c, k, lax.rem(t + n_tm - k, n_tm)).wait_recv()
        l, low, high = converted(c)
        for j in range(low, high):
            total = part[0, l * rows + j]
            for s in range(1, n_tm):
                total = total + part[s, l * rows + j]
            mean_ref[l, j : j + 1, :] = total / (snaps * n_tm)

    for c in range(chunks):
        finish_send(c, send_near)
    for side in range(2):

        @pl.when(sends[side])
        def _():
            edge_copy(side).wait_send()

        @pl.when(z_sends[side])
        def _():
            mean_copy(side).wait_send()

        if n_tm >= 4:

            @pl.when(t == via[side])
            def _():
                for c in range(chunks):
                    for h in range(2):
                        from_relay(side, c, h).wait_send()

    for c in range(chunks):
        for k in range(1, n_tm):
            part_copy(c, k, t).wait_send()


def fast_kernel(
    n_tm, n_tile, levels,
    u_ref, v_ref, land_in, bottom_in, sx_in, sy_in, own_in, halo_in,
    conv_ref, mean_ref, flag_ref,
    land_ref, bottom_ref, sx_ref, sy_ref, own_ref, halo_w_ref, small_sem,
    x, near, mm, cf, wet, key, cx, cy, part, edge, edge_halo, edge_mean, edge_in,
    near_w, far_w, place, packed, far, relayed, flags, flags_in,
    relay_send, relay_recv, x_sem, near_sem, far_send, far_recv, edge_send, edge_recv, em_send, em_recv,
    part_send, part_recv, flag_send, flag_recv,
):
    snaps, cells, width = u_ref.shape
    rows = cells // levels
    t = lax.axis_index("tm")
    z = lax.axis_index("tile")
    blocks = cells // CHUNK
    per_level = rows // CHUNK
    chunks = rows // GROUP
    fields = (u_ref, v_ref)
    even = lax.rem(t, 2) == 0
    odd = jnp.logical_not(even)

    barrier = pltpu.get_barrier_semaphore()
    for k in range(1, n_tm):
        pl.semaphore_signal(barrier, inc=1, device_id={"tm": lax.rem(t + k, n_tm)}, device_id_type=MESH)
    @pl.when(z > 0)
    def _():
        pl.semaphore_signal(barrier, inc=1, device_id={"tile": z - 1}, device_id_type=MESH)

    @pl.when(z < n_tile - 1)
    def _():
        pl.semaphore_signal(barrier, inc=1, device_id={"tile": z + 1}, device_id_type=MESH)


    def local(c, f, h):
        return pltpu.make_async_copy(
            fields[f].at[:, pl.ds(c * CHUNK, CHUNK), pl.ds(h * LANES, LANES)], x.at[c, f, h], x_sem.at[c, f, h]
        )

    small = (
        (land_in, land_ref), (bottom_in, bottom_ref), (sx_in, sx_ref),
        (sy_in, sy_ref), (own_in, own_ref), (halo_in, halo_w_ref),
    )
    for i, (src, dst) in enumerate(small):
        pltpu.make_async_copy(src, dst, small_sem.at[i]).start()
    for p in range(per_level):
        for l in range(levels):
            for f in range(2):
                for h in range(2):
                    local(l * per_level + p, f, h).start()

    first_far = jnp.where(even, 0, snaps - HALF)
    first_near = jnp.where(even, snaps - HALF, 0)
    has_far = (t > 0) & (t < n_tm - 1)
    at_end = jnp.logical_not(has_far)
    is_middle = (t == n_tm // 2 - 1) | (t == n_tm // 2)
    far_to = jnp.where(even, t - 1, t + 1)
    via_to = jnp.where(t < n_tm // 2, n_tm - 1, 0)
    forward_to = jnp.where(t == 0, n_tm // 2 - 1, n_tm // 2)

    def tiles(c):
        return c * SPAN, SPAN

    def near_copy():
        return pltpu.make_async_remote_copy(
            src_ref=x.at[:, :, :, pl.ds(first_near, HALF)],
            dst_ref=near,
            send_sem=near_sem.at[0],
            recv_sem=near_sem.at[1],
            device_id={"tm": t + 1 - 2 * lax.rem(t, 2)},
            device_id_type=MESH,
        )

    def far_copy(c, f):
        start, count = tiles(c)
        return pltpu.make_async_remote_copy(
            src_ref=packed.at[f, pl.ds(start, count)],
            dst_ref=far.at[f, pl.ds(start, count)],
            send_sem=far_send.at[c, f],
            recv_sem=far_recv.at[c, f],
            device_id={"tm": far_to},
            device_id_type=MESH,
        )

    def to_relay(c):
        start, count = tiles(c)
        return pltpu.make_async_remote_copy(
            src_ref=packed.at[1, pl.ds(start, count)],
            dst_ref=relayed.at[pl.ds(start, count)],
            send_sem=far_send.at[c, 1],
            recv_sem=relay_recv.at[c],
            device_id={"tm": via_to},
            device_id_type=MESH,
        )

    def from_relay(c):
        start, count = tiles(c)
        return pltpu.make_async_remote_copy(
            src_ref=relayed.at[pl.ds(start, count)],
            dst_ref=far.at[1, pl.ds(start, count)],
            send_sem=relay_send.at[c],
            recv_sem=far_recv.at[c, 1],
            device_id={"tm": forward_to},
            device_id_type=MESH,
        )

    def pass_on(c):
        @pl.when(at_end)
        def _():
            to_relay(c).wait_recv()
            from_relay(c).start()

    def start_far(c):
        @pl.when(has_far)
        def _():
            far_copy(c, 0).start()

        @pl.when(is_middle)
        def _():
            to_relay(c).start()

        @pl.when(has_far & jnp.logical_not(is_middle))
        def _():
            far_copy(c, 1).start()

    def edge_copy(side):
        first = snaps - HALF if side == 0 else 0
        to = t + 1 if side == 0 else t - 1
        return pltpu.make_async_remote_copy(
            src_ref=edge.at[pl.ds(first, HALF), :],
            dst_ref=edge_halo.at[side],
            send_sem=edge_send.at[side],
            recv_sem=edge_recv.at[side],
            device_id={"tm": to},
            device_id_type=MESH,
        )

    def mean_copy(side):
        to = z + 1 if side == 0 else z - 1
        return pltpu.make_async_remote_copy(
            src_ref=edge_mean,
            dst_ref=edge_in.at[side],
            send_sem=em_send.at[side],
            recv_sem=em_recv.at[side],
            device_id={"tile": to},
            device_id_type=MESH,
        )

    def flag_copy(s, side):
        to = z + 1 if side == 0 else z - 1
        return pltpu.make_async_remote_copy(
            src_ref=flags.at[s],
            dst_ref=flags_in.at[side, s],
            send_sem=flag_send.at[s, side],
            recv_sem=flag_recv.at[s, side],
            device_id={"tile": to},
            device_id_type=MESH,
        )

    def start_flag(s):
        for side in range(2):

            @pl.when(z_sends[side])
            def _():
                flag_copy(s, side).start()

    def finish_flag(s):
        for side in range(2):

            @pl.when(z_receives[side])
            def _():
                flag_copy(s, side).wait_recv()

        flags[s + 1] = jnp.maximum(flags[s], jnp.maximum(flags_in[0, s], flags_in[1, s]))

    def converted(c):
        return c * GROUP - (1 if c else 0), rows if c == chunks - 1 else (c + 1) * GROUP - 1

    def part_copy(c, k, slot):
        low, high = converted(c)
        return pltpu.make_async_remote_copy(
            src_ref=part.at[slot, pl.ds(levels * low, levels * (high - low))],
            dst_ref=part.at[slot, pl.ds(levels * low, levels * (high - low))],
            send_sem=part_send.at[c, k],
            recv_sem=part_recv.at[c, k],
            device_id={"tm": lax.rem(t + k, n_tm)},
            device_id_type=MESH,
        )

    sends = (t < n_tm - 1, t > 0)
    receives = (t > 0, t < n_tm - 1)
    z_sends = (z < n_tile - 1, z > 0)
    z_receives = (z > 0, z < n_tile - 1)

    for i, (src, dst) in enumerate(small):
        pltpu.make_async_copy(src, dst, small_sem.at[i]).wait()

    levels_wet = []
    for l in range(levels):
        is_wet = (land_ref[...] == 1) & (l < bottom_ref[...])
        levels_wet.append(jnp.where(is_wet, 1.0, 0.0).astype(jnp.float32))
    all_wet = jnp.concatenate(levels_wet, axis=0)
    lower = lax.broadcasted_iota(jnp.int32, (width, width), 0)
    upper = lax.broadcasted_iota(jnp.int32, (width, width), 1)
    earlier = jnp.where(lower < upper, 1.0, 0.0).astype(jnp.bfloat16)

    def ranked(index):
        j = lax.rem(index, rows)
        side = lax.rem(j, GROUP) // 2
        inner = jnp.where(side == 0, lax.rem(j, 2), 1 - lax.rem(j, 2))
        return 2 * (j // GROUP) + side, 2 * inner + (1 - index // rows)

    set_a, rank_a = ranked(lax.broadcasted_iota(jnp.int32, (cells, cells), 0))
    set_b, rank_b = ranked(lax.broadcasted_iota(jnp.int32, (cells, cells), 1))
    ahead_rows = jnp.where((set_a == set_b) & (rank_b < rank_a), 1.0, 0.0).astype(jnp.bfloat16)
    same_rows = jnp.where((set_a // 2 == set_b // 2) & (set_a != set_b), 1.0, 0.0).astype(jnp.bfloat16)
    wet_bits = all_wet.astype(jnp.bfloat16)
    filled = jnp.dot(
        jnp.concatenate([ahead_rows, same_rows], axis=0), wet_bits, preferred_element_type=jnp.float32
    ).astype(jnp.bfloat16)
    every = jnp.ones((width, width), jnp.bfloat16)
    order = jnp.dot(wet_bits, earlier, preferred_element_type=jnp.float32) + jnp.dot(
        filled[:cells], every, preferred_element_type=jnp.float32
    )
    other = jnp.dot(filled[cells:], every, preferred_element_type=jnp.float32)
    row = lax.broadcasted_iota(jnp.int32, (cells, width), 0)
    right = lax.rem(lax.rem(row, rows), GROUP) >= 2
    spot = jnp.where(right, float(SPAN * LANES - 1) - order, order)
    first_lane = jnp.zeros((cells, width), jnp.float32)
    lanes_used = jnp.zeros((cells, width), jnp.float32)
    for q in range(GROUP):
        for l in range(levels):
            here = (lax.rem(lax.rem(row, rows), GROUP) == q) & (row // rows == l)
            low, high = WINDOWS[q][l]
            first_lane = jnp.where(here, float(low * LANES), first_lane)
            lanes_used = jnp.where(here, float((high - low) * LANES), lanes_used)
    spot = spot - first_lane
    fits = (spot >= 0.0) & (spot < lanes_used) & (order + other < float(SPAN * LANES))
    is_wet = all_wet > 0.0
    all_key = jnp.where(is_wet & fits, spot, -1.0)
    over = jnp.max(jnp.where(is_wet & jnp.logical_not(fits), 1.0, 0.0), axis=0, keepdims=True)
    flags[0] = jnp.broadcast_to(jnp.maximum(over[:, :LANES], over[:, LANES:]), (8, LANES))
    for r in range(cells):
        wet[r] = all_wet[r : r + 1, :]
        key[r] = all_key[r : r + 1, :]

    def series(ref, count, j):
        return ref.reshape(count * CHUNK, LANES)[pl.ds(j, count, stride=CHUNK), :]

    def both(ref, count, j):
        return jnp.concatenate([series(ref.at[h], count, j) for h in range(2)], axis=1)

    def members(c):
        for q in range(GROUP):
            for l in range(levels):
                low, high = WINDOWS[q][l]
                j = c * GROUP + q
                yield l * rows + j, l * per_level + j // CHUNK, j % CHUNK, low, high

    def put(r, size):
        index = lax.broadcasted_iota(jnp.int32, (size, width), 0).astype(jnp.float32)
        place[r, :size] = jnp.where(index == key[r], 1.0, 0.0).astype(jnp.bfloat16)

    def gather(r, b, i, size):
        split = []
        for f in range(2):
            block = [x.at[b, f, h].reshape(snaps * CHUNK, LANES) for h in range(2)]
            at = pl.ds(first_far * CHUNK + i, HALF, stride=CHUNK)
            split.extend(halves(jnp.concatenate([p[at, :] for p in block], axis=1)))
        split = jnp.concatenate(split, axis=0).astype(jnp.bfloat16)
        out = lax.dot_general(
            split, place[r, :size], (((1,), (1,)), ((), ())), preferred_element_type=jnp.float32
        )
        return [out[2 * f * HALF : (2 * f + 1) * HALF] + out[(2 * f + 1) * HALF : (2 * f + 2) * HALF] for f in range(2)]

    def compact(c):
        @pl.when(has_far)
        def _():
            compact_far(c)

    def compact_far(c):
        start, count = tiles(c)
        for r, _, _, low, high in members(c):
            put(r, (high - low) * LANES)
        sums = [[None] * count for f in range(2)]
        for r, b, i, low, high in members(c):
            values = gather(r, b, i, (high - low) * LANES)
            for f in range(2):
                for p in range(low, high):
                    piece = values[f][:, (p - low) * LANES : (p - low + 1) * LANES]
                    sums[f][p] = piece if sums[f][p] is None else sums[f][p] + piece
        for f in range(2):
            for p in range(count):
                packed[f, start + p] = sums[f][p]

    def wait_local(c):
        for f in range(2):
            for h in range(2):
                local(c, f, h).wait()

    for c in range(blocks):
        wait_local(c)
    lane = lax.broadcasted_iota(jnp.int32, (snaps, LANES), 1)

    def pack(r, acc):
        c, j = r // CHUNK, lax.rem(r, CHUNK)
        for f in range(2):
            q = f * cells + r
            first = series(x.at[c, f, 0], snaps, j) * wet[r][:, :LANES]
            acc = jnp.where(lane == q, pltpu.roll(first, q, 1), acc)
            q = (2 + f) * cells + r
            last = series(x.at[c, f, 1], snaps, j) * wet[r][:, width - LANES :]
            acc = jnp.where(lane == q, pltpu.roll(last, lax.rem(q + 1, LANES), 1), acc)
        return acc

    compact(0)
    pl.semaphore_wait(barrier, n_tm - 1 + jnp.where(z > 0, 1, 0) + jnp.where(z < n_tile - 1, 1, 0))
    start_far(0)
    edge[...] = lax.fori_loop(0, cells, pack, jnp.zeros((snaps, LANES), jnp.float32), unroll=4)
    for side in range(2):

        @pl.when(sends[side])
        def _():
            edge_copy(side).start()

    start_flag(0)
    near_copy().start()
    compact(1)
    start_far(1)
    for side in range(2):

        @pl.when(jnp.logical_not(receives[side]))
        def _():
            edge_halo[side] = jnp.zeros(edge_halo.shape[1:], jnp.float32)

        @pl.when(jnp.logical_not(z_receives[side]))
        def _():
            edge_in[side] = jnp.zeros(edge_in.shape[1:], jnp.float32)
            flags_in[side] = jnp.zeros(flags_in.shape[1:], jnp.float32)

    all_x, all_y = 0.5 / sx_ref[...], 0.5 / sy_ref[...]
    for j in range(rows):
        cx[j] = all_x[j : j + 1, :]
        cy[j] = all_y[j : j + 1, :]
    for f in range(2):
        for l in range(levels):
            for j in (0, rows + 1):
                mm[f, l, j] = jnp.zeros((snaps, width), jnp.float32)
    column = lax.broadcasted_iota(jnp.int32, (snaps, 2 * HALF), 1)
    valid = ((column >= HALF) | (t > 0)) & ((column < HALF) | (t < n_tm - 1))
    own_w = own_ref[...]
    halo_w = jnp.where(valid, halo_w_ref[...], 0.0)
    weight_sum = jnp.sum(own_w, axis=1, keepdims=True) + jnp.sum(halo_w, axis=1, keepdims=True)
    own_w = own_w / weight_sum
    halo_w = halo_w / weight_sum
    near_half = jnp.where(even, halo_w[:, HALF:], halo_w[:, :HALF])
    far_half = jnp.where(even, halo_w[:, :HALF], halo_w[:, HALF:])
    near_w[...] = stacked_weights(jnp.concatenate([own_w, near_half], axis=1))
    far_w[...] = stacked_weights(far_half)

    pass_on(0)
    for side in range(2):

        @pl.when(receives[side])
        def _():
            edge_copy(side).wait_recv()

    edge_mean[...] = dot(own_w, edge[...]) + dot(
        halo_w, jnp.concatenate([edge_halo[0], edge_halo[1]], axis=0)
    )
    for side in range(2):

        @pl.when(z_sends[side])
        def _():
            mean_copy(side).start()

    compact(2)
    start_far(2)
    def near_part(r, carry):
        l, j = r // rows, lax.rem(r, rows)
        c, i = r // CHUNK, lax.rem(r, CHUNK)
        for f in range(2):
            pieces = [both(x.at[c, f], snaps, i), both(near.at[c, f], HALF, i)]
            mm[f, l, j + 1] = split_dot(near_w[...], pieces)
        return carry

    if 0 < n_tile - 1:
        finish_flag(0)
    if 0 + 1 < n_tile - 1:
        start_flag(0 + 1)
    near_copy().wait_recv()
    lax.fori_loop(0, cells, near_part, 0, unroll=8)
    compact(3)
    pass_on(1)
    pass_on(2)
    wide = lax.broadcasted_iota(jnp.int32, (snaps, width), 1)

    def spread(r, blocks):
        l, j = r // rows, r % rows
        size = blocks[0].shape[1]
        split = []
        for block in blocks:
            split.extend(halves(block))
        out = jnp.dot(
            jnp.concatenate(split, axis=0).astype(jnp.bfloat16), place[r, :size], preferred_element_type=jnp.float32
        ).astype(jnp.bfloat16)
        mask = wet[r]
        for f in range(2):
            both_halves = jnp.dot(
                far_w[...], out[2 * f * HALF : 2 * (f + 1) * HALF], preferred_element_type=jnp.float32
            )
            mm[f, l, j + 1] = (mm[f, l, j + 1] + both_halves[:snaps] + both_halves[snaps:]) * mask

    def far_part(c):
        start, _ = tiles(c)

        @pl.when(has_far)
        def _():
            for f in range(2):
                far_copy(c, f).wait_recv()
            for r, _, _, low, high in members(c):
                spread(
                    r, [jnp.concatenate([far[f, start + p] for p in range(low, high)], axis=1) for f in range(2)]
                )

        @pl.when(at_end)
        def _():
            for r, _, _, _, _ in members(c):
                for f in range(2):
                    mm[f, r // rows, r % rows + 1] = mm[f, r // rows, r % rows + 1] * wet[r]

    wide = lax.broadcasted_iota(jnp.int32, (8, width), 1)

    def grad_x(f, r, now, masked, scale):
        q = (2 + f) * cells + r
        behind = pltpu.roll(edge_in[0, now, :], lax.rem(2 * LANES - q, LANES), 1)
        q = f * cells + r
        ahead = pltpu.roll(edge_in[1, now, :], lax.rem(2 * LANES - 1 - q, LANES), 1)
        behind = jnp.where(wide == 0, jnp.concatenate([behind, behind], axis=1), pltpu.roll(masked, 1, 1))
        ahead = jnp.where(wide == width - 1, jnp.concatenate([ahead, ahead], axis=1), pltpu.roll(masked, width - 1, 1))
        return (ahead - behind) * scale

    def convert(low, count):
        def body(q, carry):
            l, j = q // count, low + lax.rem(q, count)
            r = l * rows + j
            c, i = r // CHUNK, lax.rem(r, CHUNK)
            mask = -wet[r]
            scale_x = cx[j]
            scale_y = cy[j]
            kept = jnp.zeros((CHUNK, width), jnp.float32)
            for first in range(0, snaps, 8):
                now = pl.ds(first, 8)
                at = pl.ds(first * CHUNK + i, 8, stride=CHUNK)
                eddy, gx, gy = [], [], []
                for f in range(2):
                    masked = mm[f, l, j + 1, now, :]
                    raw = [x.at[c, f, h].reshape(snaps * CHUNK, LANES)[at, :] for h in range(2)]
                    eddy.append(jnp.concatenate(raw, axis=1) - masked)
                    gx.append(grad_x(f, r, now, masked, scale_x))
                    gy.append((mm[f, l, j + 2, now, :] - mm[f, l, j, now, :]) * scale_y)
                eu, ev = eddy
                total = eu * eu * gx[0] + eu * ev * (gy[0] + gx[1]) + ev * ev * gy[1]
                conversion = mask * total
                for h in range(2):
                    cf.at[c, h].reshape(snaps * CHUNK, LANES)[at, :] = conversion[:, h * LANES : (h + 1) * LANES]
                for k in range(0, 8, CHUNK):
                    kept = kept + conversion[k : k + CHUNK]
            part[t, levels * j + l] = jnp.sum(kept, axis=0, keepdims=True)
            return carry

        return body

    def finish(c):
        for k in range(1, n_tm):
            part_copy(c, k, lax.rem(t + n_tm - k, n_tm)).wait_recv()
        low, high = converted(c)
        for j in range(low, high):
            for l in range(levels):
                total = part[0, levels * j + l]
                for s in range(1, n_tm):
                    total = total + part[s, levels * j + l]
                mean_ref[l, j : j + 1, :] = total / (snaps * n_tm)

    if 1 < n_tile - 1:
        finish_flag(1)
    if 1 + 1 < n_tile - 1:
        start_flag(1 + 1)
    for c in range(chunks):
        @pl.when(has_far)
        def _():
            for f in range(2):
                far_copy(c, f).wait_send()

        if c + AHEAD < chunks:
            start_far(c + AHEAD)

        far_part(c)
        if c + AHEAD < chunks:
            pass_on(c + AHEAD)
        if c == 0:
            for side in range(2):

                @pl.when(z_receives[side])
                def _():
                    mean_copy(side).wait_recv()

        low, high = converted(c)
        lax.fori_loop(0, levels * (high - low), convert(low, high - low), 0, unroll=2 * (high - low))
        for k in sorted(range(1, n_tm), key=lambda k: abs(k - n_tm // 2)):
            part_copy(c, k, t).start()

    def narrow(s, carry):
        for l in range(levels):
            for h in range(2):
                block = jnp.concatenate([cf[l * per_level + p, h, s] for p in range(per_level)], axis=0)
                conv_ref[s, pl.ds(l * rows, rows), pl.ds(h * LANES, LANES)] = block.astype(jnp.bfloat16)
        return carry

    lax.fori_loop(0, snaps, narrow, 0, unroll=4)
    for s in range(2, n_tile - 1):
        finish_flag(s)
        if s + 1 < n_tile - 1:
            start_flag(s + 1)
    flag_ref[0] = jnp.max(flags[n_tile - 1])
    for c in range(chunks):
        finish(c)

    near_copy().wait_send()
    for side in range(2):

        @pl.when(sends[side])
        def _():
            edge_copy(side).wait_send()

        @pl.when(z_sends[side])
        def _():
            mean_copy(side).wait_send()

    @pl.when(at_end)
    def _():
        for c in range(chunks):
            from_relay(c).wait_send()

    for s in range(n_tile - 1):
        for side in range(2):

            @pl.when(z_sends[side])
            def _():
                flag_copy(s, side).wait_send()

    for c in range(chunks):
        for k in range(1, n_tm):
            part_copy(c, k, t).wait_send()


def full(own, halo, velocity_u, velocity_v, land_sea, bottom_level, spacing_x, spacing_y):
    snaps, cells, width = velocity_u.shape
    rows = land_sea.shape[0]
    levels = cells // rows
    n_tm, n_tile = lax.axis_size("tm"), lax.axis_size("tile")
    chunks = cells // CHUNK
    vmem = pl.BlockSpec(memory_space=pltpu.VMEM)
    hbm = pl.BlockSpec(memory_space=pltpu.HBM)
    f32, bf16 = jnp.float32, jnp.bfloat16
    dma = pltpu.SemaphoreType.DMA
    return pl.pallas_call(
        functools.partial(kernel, n_tm, n_tile, levels),
        out_shape=(
            jax.ShapeDtypeStruct((snaps, cells, width), bf16),
            jax.ShapeDtypeStruct((levels, rows, width), f32),
        ),
        in_specs=[hbm] * 8,
        out_specs=(vmem, vmem),
        scratch_shapes=[
            pltpu.VMEM((rows, width), jnp.int32),
            pltpu.VMEM((rows, width), jnp.int32),
            pltpu.VMEM((rows, width), f32),
            pltpu.VMEM((rows, width), f32),
            pltpu.VMEM(own.shape, f32),
            pltpu.VMEM(halo.shape, f32),
            dma((6,)),
            pltpu.VMEM((chunks, 2, 2, snaps, CHUNK, LANES), f32),
            pltpu.VMEM((2, chunks, 2, 2, HALF, CHUNK, LANES), f32),
            pltpu.VMEM((2, levels, rows + 2, snaps, width), f32),
            pltpu.VMEM((chunks, 2, snaps, CHUNK, LANES), f32),
            pltpu.VMEM((cells, 1, width), f32),
            pltpu.VMEM((rows, 1, width), f32),
            pltpu.VMEM((rows, 1, width), f32),
            pltpu.VMEM((n_tm, cells, 1, width), f32),
            pltpu.VMEM((snaps, LANES), f32),
            pltpu.VMEM((2, HALF, LANES), f32),
            pltpu.VMEM((snaps, LANES), f32),
            pltpu.VMEM((2, snaps, LANES), f32),
            pltpu.VMEM((2 * snaps, 2 * (snaps + HALF)), bf16),
            pltpu.VMEM((2 * snaps, 2 * HALF), bf16),
            pltpu.VMEM((chunks, 2, HALF, CHUNK, LANES), f32),
            dma((chunks, 2)),
            dma((chunks, 2)),
            dma((chunks, 2, 2)),
            dma((2, chunks, 2, 2)),
            dma((2, chunks, 2, 2)),
            dma((2,)),
            dma((2,)),
            dma((2,)),
            dma((2,)),
            dma((chunks, n_tm)),
            dma((chunks, n_tm)),
        ],
        compiler_params=pltpu.CompilerParams(
            collective_id=1, has_side_effects=True, vmem_limit_bytes=60 * 1024 * 1024
        ),
        cost_estimate=pl.CostEstimate(flops=10**9, bytes_accessed=4 * 10**6, transcendentals=0),
    )(
        velocity_u, velocity_v, land_sea, bottom_level, spacing_x, spacing_y, own, halo,
    )


def quick(own, halo, velocity_u, velocity_v, land_sea, bottom_level, spacing_x, spacing_y):
    snaps, cells, width = velocity_u.shape
    rows = land_sea.shape[0]
    levels = cells // rows
    n_tm, n_tile = lax.axis_size("tm"), lax.axis_size("tile")
    blocks = cells // CHUNK
    chunks = rows // GROUP
    packs = chunks * SPAN
    most = max(high - low for pair in WINDOWS for low, high in pair) * LANES
    vmem = pl.BlockSpec(memory_space=pltpu.VMEM)
    hbm = pl.BlockSpec(memory_space=pltpu.HBM)
    f32, bf16 = jnp.float32, jnp.bfloat16
    dma = pltpu.SemaphoreType.DMA
    return pl.pallas_call(
        functools.partial(fast_kernel, n_tm, n_tile, levels),
        out_shape=(
            jax.ShapeDtypeStruct((snaps, cells, width), bf16),
            jax.ShapeDtypeStruct((levels, rows, width), f32),
            jax.ShapeDtypeStruct((1,), f32),
        ),
        in_specs=[hbm] * 8,
        out_specs=(vmem, vmem, pl.BlockSpec(memory_space=pltpu.SMEM)),
        scratch_shapes=[
            pltpu.VMEM((rows, width), jnp.int32),
            pltpu.VMEM((rows, width), jnp.int32),
            pltpu.VMEM((rows, width), f32),
            pltpu.VMEM((rows, width), f32),
            pltpu.VMEM(own.shape, f32),
            pltpu.VMEM(halo.shape, f32),
            dma((6,)),
            pltpu.VMEM((blocks, 2, 2, snaps, CHUNK, LANES), f32),
            pltpu.VMEM((blocks, 2, 2, HALF, CHUNK, LANES), f32),
            pltpu.VMEM((2, levels, rows + 2, snaps, width), f32),
            pltpu.VMEM((blocks, 2, snaps, CHUNK, LANES), f32),
            pltpu.VMEM((cells, 1, width), f32),
            pltpu.VMEM((cells, 1, width), f32),
            pltpu.VMEM((rows, 1, width), f32),
            pltpu.VMEM((rows, 1, width), f32),
            pltpu.VMEM((n_tm, cells, 1, width), f32),
            pltpu.VMEM((snaps, LANES), f32),
            pltpu.VMEM((2, HALF, LANES), f32),
            pltpu.VMEM((snaps, LANES), f32),
            pltpu.VMEM((2, snaps, LANES), f32),
            pltpu.VMEM((2 * snaps, 2 * (snaps + HALF)), bf16),
            pltpu.VMEM((2 * snaps, 2 * HALF), bf16),
            pltpu.VMEM((cells, most, width), bf16),
            pltpu.VMEM((2, packs, HALF, LANES), f32),
            pltpu.VMEM((2, packs, HALF, LANES), f32),
            pltpu.VMEM((packs, HALF, LANES), f32),
            pltpu.VMEM((n_tile, 8, LANES), f32),
            pltpu.VMEM((2, n_tile - 1, 8, LANES), f32),
            dma((chunks,)),
            dma((chunks,)),
            dma((blocks, 2, 2)),
            dma((2,)),
            dma((chunks, 2)),
            dma((chunks, 2)),
            dma((2,)),
            dma((2,)),
            dma((2,)),
            dma((2,)),
            dma((chunks, n_tm)),
            dma((chunks, n_tm)),
            dma((n_tile - 1, 2)),
            dma((n_tile - 1, 2)),
        ],
        compiler_params=pltpu.CompilerParams(
            collective_id=0, has_side_effects=True, vmem_limit_bytes=60 * 1024 * 1024
        ),
        cost_estimate=pl.CostEstimate(flops=10**9, bytes_accessed=4 * 10**6, transcendentals=0),
    )(
        velocity_u, velocity_v, land_sea, bottom_level, spacing_x, spacing_y, own, halo,
    )


def shards(velocity_u, velocity_v, land_sea, bottom_level, spacing_x, spacing_y):
    snaps, levels, rows, width = velocity_u.shape
    cells = levels * rows
    n_tm = lax.axis_size("tm")
    assert width == 2 * LANES and 4 * cells == LANES and snaps == 2 * HALF
    assert rows % (2 * CHUNK) == 0 and levels == 2 and n_tm % 4 == 0 and n_tm >= 8
    own, halo = band_parts(snaps)
    args = (
        jnp.asarray(own), jnp.asarray(halo),
        velocity_u.reshape(snaps, cells, width), velocity_v.reshape(snaps, cells, width),
        land_sea, bottom_level, spacing_x, spacing_y,
    )
    conversion, mean_map, excess = quick(*args)
    conversion, mean_map = lax.cond(
        excess[0] > 0.0, lambda args, done: full(*args), lambda args, done: done, args, (conversion, mean_map)
    )
    conversion, mean_map = store(conversion, mean_map)
    return conversion.reshape(velocity_u.shape), mean_map


def store_kernel(a_ref, b_ref, a_out, b_out, sem):
    copies = [
        pltpu.make_async_copy(a_ref, a_out, sem.at[0]),
        pltpu.make_async_copy(b_ref, b_out, sem.at[1]),
    ]
    for copy in copies:
        copy.start()
    for copy in copies:
        copy.wait()


def store(a, b):
    place = pl.BlockSpec(memory_space=pl.ANY)
    return pl.pallas_call(
        store_kernel,
        out_shape=(jax.ShapeDtypeStruct(a.shape, a.dtype), jax.ShapeDtypeStruct(b.shape, b.dtype)),
        in_specs=[place, place],
        out_specs=(pl.BlockSpec(memory_space=pltpu.HBM), pl.BlockSpec(memory_space=pltpu.HBM)),
        scratch_shapes=[pltpu.SemaphoreType.DMA((2,))],
        name="store",
    )(a, b)


def solution(mesh):
    in_specs = (
        P("tm", None, None, "tile"),
        P("tm", None, None, "tile"),
        P(None, "tile"),
        P(None, "tile"),
        P(None, "tile"),
        P(None, "tile"),
    )
    out_specs = (P("tm", None, None, "tile"), P(None, None, "tile"))
    return jax.shard_map(shards, mesh=mesh, in_specs=in_specs, out_specs=out_specs, check_vma=False)
```
